256 devices in a mesh: lat: 16 (over y, x_lo, core), lon: 16 (over z, x_hi).
Axes of the slice: x: 4 (x_hi: 2, x_lo: 2; x = x_hi * 2 + x_lo), y: 4, z: 8, core: 2. Of those that a mesh axis runs over, the one named last changes fastest.
Arguments:
- noise: float32 [4, 8, 256, 4096], P(None, None, 'lat', 'lon'), may hold values from -6 to 6
- diff_lat: float32 [8, 256, 4096], P(None, 'lat', 'lon'), may hold values from 0.05 to 0.24
- diff_lon: float32 [8, 256, 4096], P(None, 'lat', 'lon'), may hold values from 0.05 to 0.24
- shear: float32 [8, 256, 4096], P(None, 'lat', 'lon'), may hold values from -0.9 to 0.9
- sea_mask: int32 [8, 256, 4096], P(None, 'lat', 'lon'), may hold values from 0 to 1, as said below
Outputs:
- normalized: float32 [4, 8, 256, 4096], P(None, None, 'lat', 'lon')
- mean_var: float32 [], replicated
The draws below stay inside these ranges and needn't reach their ends.
Inputs may be any that keep to these rules, and one draw needn't show every extreme that they name: `sea_mask`: every block of 16 latitude rows by 256 longitude columns has its own chance for each cell to be wet, from a quarter to one; the block of the first rows and first columns is wet at every level.
All inputs are finite; a program needn't handle non-finite values.
Results may differ from the reference program's by a relative error of at most 0.0003.
Values sent between devices are 32-bit elements; how exact they have to be, the bound alone decides.
A program may use at most 64 MiB of HBM per device.

```python
import jax
import jax.numpy as jnp
from jax import lax

SAMPLES = 4
LEVELS = 8
CX = 16
CY = 256
ITERS = 4
NX = 256
NY = 4096


def draw_sea_mask(key, part):
    tile_key = jax.random.fold_in(key, 11)
    cell_key = jax.random.fold_in(key, 23)
    tile_share = jax.random.randint(tile_key, (NX // CX, NY // CY), 1, 5)
    tile_share = tile_share.at[0, 0].set(4)
    spread_share = jnp.repeat(jnp.repeat(tile_share, CX, axis=0), CY, axis=1)
    cells = jax.random.randint(cell_key, (LEVELS, NX, NY), 0, 4)
    return (cells < spread_share[None, :, :]).astype(jnp.int32)


def shard_levels(rng, shape, split, low, high):
    gain, own = 1.0, jax.random.fold_in(rng, 6)
    for position, shards_of in split:
        heights = jnp.exp(jax.random.uniform(jax.random.fold_in(own, position), (shards_of,), jnp.float32, low / len(split), high / len(split)))
        gain = gain * jnp.repeat(heights, shape[position] // shards_of).reshape([-1 if axis == position else 1 for axis in range(len(shape))])
    return gain


def bell_draw(own_key, dims, scale, bound, cuts=(), kind=jnp.bfloat16):
    drawn = scale * jax.random.normal(own_key, dims, jnp.float32)
    if cuts:
        drawn = drawn * shard_levels(own_key, dims, cuts, -0.22, 0.18)
    return jnp.clip(drawn, -bound, bound).astype(kind)


def setup_inputs(seed: int = 0) -> dict:
    seeds = jax.random.split(jax.random.key(seed), 6)
    return {
        "noise": bell_draw(seeds[0], (SAMPLES, LEVELS, NX, NY), 1.0, 6.0, ((2, 16), (3, 16)), jnp.float32),
        "diff_lat": jnp.clip(0.05 + 0.19 * jax.random.uniform(seeds[1], (LEVELS, NX, NY), jnp.float32) ** shard_levels(seeds[1], (LEVELS, NX, NY), ((1, 16), (2, 16)), -0.2, 0.2), 0.05, 0.24),
        "diff_lon": jnp.clip(0.05 + 0.19 * jax.random.uniform(seeds[2], (LEVELS, NX, NY), jnp.float32) ** shard_levels(seeds[2], (LEVELS, NX, NY), ((1, 16), (2, 16)), -0.2, 0.2), 0.05, 0.24),
        "shear": jnp.clip(jax.random.uniform(seeds[3], (LEVELS, NX, NY), jnp.float32, -0.9, 0.9) * shard_levels(seeds[3], (LEVELS, NX, NY), ((1, 16), (2, 16)), -0.4, 0.0), -0.9, 0.9),
        "sea_mask": draw_sea_mask(jax.random.fold_in(seeds[5], 71), 0),
    }


def offset_weights(diff_lat, diff_lon, shear):
    cross = shear * jnp.sqrt(diff_lat * diff_lon)
    return [((0, 0), 1.0 - 2.0 * (diff_lat + diff_lon)), ((1, 0), diff_lat), ((-1, 0), diff_lat), ((0, 1), diff_lon), ((0, -1), diff_lon), ((1, 1), 0.5 * cross), ((-1, -1), 0.5 * cross), ((1, -1), -0.5 * cross), ((-1, 1), -0.5 * cross)]

def move_rows(field, shift_lat, shift_lon):
    moved = jnp.roll(field, shift_lon, axis=-1)
    zero_row = jnp.zeros_like(moved[:, :1, :])
    if shift_lat == 1:
        moved = jnp.concatenate([zero_row, moved[:, :-1, :]], axis=1)
    elif shift_lat == -1:
        moved = jnp.concatenate([moved[:, 1:, :], zero_row], axis=1)
    return moved

def reference(noise, diff_lat, diff_lon, shear, sea_mask):
    wet = sea_mask.astype(jnp.float32)
    table = offset_weights(diff_lat, diff_lon, shear)

    def diffuse(field):
        for step in range(ITERS):
            masked = wet * field
            total = jnp.zeros_like(field)
            for offset, weight in table:
                total = total + move_rows(weight * masked, offset[0], offset[1])
            field = total
        return field
    diffused = lax.map(diffuse, noise)
    var = lax.optimization_barrier(jnp.sum(diffused * diffused, axis=0)) / SAMPLES
    mean_var = jnp.sum(wet * var) / jnp.sum(wet)
    safe = jnp.where(wet > 0, var, 1.0)
    factor = wet * jnp.sqrt(mean_var / (safe + 1e-06))
    return (diffused * factor, mean_var)
```

```python
import functools

import jax
import jax.numpy as jnp
from jax import lax
from jax.experimental import pallas as pl
from jax.experimental.pallas import tpu as pltpu
from jax.sharding import PartitionSpec as P

SAMPLES = 4
LEVELS = 8
ITERS = 4
LANES = 128
MESH = pl.DeviceIdType.MESH


def kernel(
    n_lat, n_lon, rows, groups,
    noise, k_lat, k_lon, shear, sea,
    out, stat,
    raw, raw_k, raw_m, y, yh, a, ah, var, lon_tx, lon_rx, diag_tx, diag_rx, part, result,
    in_sem, out_sem, lat_tx_sem, lat_rx_sem, lon_tx_sem, lon_rx_sem, diag_tx_sem, diag_rx_sem, sum_tx_sem, sum_rx_sem,
):
    w = ITERS
    tall = rows + 2 * w
    ia, ib = lax.axis_index("lat"), lax.axis_index("lon")
    east, west = lax.rem(ib + 1, n_lon), lax.rem(ib + n_lon - 1, n_lon)
    has_north, has_south = ia > 0, ia < n_lat - 1
    lane = lax.broadcasted_iota(jnp.int32, (LEVELS, LANES), 1)

    def half(h):
        return pl.ds(h * LANES, LANES)

    loads = []
    for f, src in enumerate((k_lat, k_lon, shear)):
        for h in range(2):
            loads.append(pltpu.make_async_copy(src.at[:, half(h)], raw_k.at[f, h], in_sem.at[f, h]))
    for h in range(2):
        loads.append(pltpu.make_async_copy(sea.at[:, half(h)], raw_m.at[h], in_sem.at[3, h]))
    for s in range(SAMPLES):
        for h in range(2):
            loads.append(pltpu.make_async_copy(noise.at[s, :, half(h)], raw.at[s, h], in_sem.at[4 + s, h]))
    for c in loads:
        c.start()

    barrier = pltpu.get_barrier_semaphore()

    def greet(pa, pb):
        pl.semaphore_signal(barrier, inc=1, device_id=(pa, pb), device_id_type=MESH)

    @pl.when(has_north)
    def _():
        for pb in (west, east, ib):
            greet(ia - 1, pb)

    @pl.when(has_south)
    def _():
        for pb in (west, east, ib):
            greet(ia + 1, pb)

    greet(ia, west)
    greet(ia, east)
    for group in groups:
        for ma, mb in group[1:]:
            greet(lax.bitwise_xor(ia, ma), lax.bitwise_xor(ib, mb))

    for c in loads[:8]:
        c.wait()
    for r in range(rows):
        for h in range(2):
            at = pl.ds(r, LEVELS, stride=rows)
            m = raw_m[h, at, :].astype(jnp.float32)
            k11 = raw_k[0, h, at, :]
            k22 = raw_k[1, h, at, :]
            a1 = m * k11
            a2 = m * k22
            a[1, w + r, h] = a1
            a[2, w + r, h] = a2
            a[3, w + r, h] = (0.5 * m) * (raw_k[2, h, at, :] * jnp.sqrt(k11 * k22))
            a[0, w + r, h] = m - 2.0 * (a1 + a2)
    for c in loads[8:]:
        c.wait()
    for s in range(SAMPLES):
        for r in range(rows):
            for h in range(2):
                y[s, w + r, h] = raw[s, h, pl.ds(r, LEVELS, stride=rows), :]

    group_of = lax.shift_right_logical(lane, 2)

    def pack(pieces):
        packed = jnp.zeros((LEVELS, LANES), jnp.float32)
        for k, (value, shift) in enumerate(pieces):
            moved = pltpu.roll(value, (shift + 4 * k) % LANES, 1) if (shift + 4 * k) % LANES else value
            packed = jnp.where(group_of == k, moved, packed)
        return packed

    for side, (h, shift) in enumerate(((1, 4), (0, 0))):
        for v in range(2):
            lon_tx[side, v] = pack([(y[2 * v + k // rows, w + k % rows, h], shift) for k in range(2 * rows)])
        lon_tx[side, 2] = pack([(a[1 + k // rows, w + k % rows, h], shift) for k in range(2 * rows)])
        lon_tx[side, 3] = pack([(a[3, w + k, h], shift) for k in range(rows)])
        for end, first in enumerate((w, rows)):
            pieces = [(y[s, first + i, h], shift) for s in range(SAMPLES) for i in range(w)]
            pieces += [(a[1 + f, first + i, h], shift) for f in range(3) for i in range(w)]
            diag_tx[end, side] = pack(pieces)

    zero = jnp.zeros((LEVELS, LANES), jnp.float32)

    def clear(first, corner):
        for i in range(w):
            for h in range(2):
                for f in range(1, 4):
                    a[f, first + i, h] = zero
                for s in range(SAMPLES):
                    y[s, first + i, h] = zero
        for side in range(2):
            diag_rx[corner, side] = zero

    @pl.when(jnp.logical_not(has_north))
    def _():
        clear(0, 0)

    @pl.when(jnp.logical_not(has_south))
    def _():
        clear(w + rows, 1)

    n_sum = sum(len(group) - 1 for group in groups)
    pl.semaphore_wait(barrier, 2 + n_sum + 3 * has_north.astype(jnp.int32) + 3 * has_south.astype(jnp.int32))

    def remote(src, dst, tx, rx, pa, pb):
        return pltpu.make_async_remote_copy(
            src_ref=src, dst_ref=dst, send_sem=tx, recv_sem=rx, device_id=(pa, pb), device_id_type=MESH
        )

    lon_copies = [
        remote(lon_tx.at[side], lon_rx.at[side], lon_tx_sem.at[side], lon_rx_sem.at[side], ia, (east, west)[side])
        for side in range(2)
    ]
    pa_of = (ia - 1, ia + 1)
    diag_copies = [
        [
            remote(diag_tx.at[end, side], diag_rx.at[1 - end, side], diag_tx_sem.at[end, side], diag_rx_sem.at[1 - end, side], pa_of[end], (east, west)[side])
            for side in range(2)
        ]
        for end in range(2)
    ]

    def lat_copy(end, piece):
        mine = pl.ds((w, rows)[end], w)
        theirs = pl.ds((w + rows, 0)[end], w)
        tx, rx = lat_tx_sem.at[end, piece], lat_rx_sem.at[1 - end, piece]
        if piece == SAMPLES:
            src, dst = a.at[pl.ds(1, 3), mine], a.at[pl.ds(1, 3), theirs]
        else:
            src, dst = y.at[piece, mine], y.at[piece, theirs]
        return remote(src, dst, tx, rx, pa_of[end], ib)

    lat_copies = [[lat_copy(end, piece) for piece in range(SAMPLES + 1)] for end in range(2)]
    present = (has_north, has_south)

    for end in range(2):

        @pl.when(present[end])
        def _(end=end):
            for c in diag_copies[end]:
                c.start()

    for c in lon_copies:
        c.start()
    for end in range(2):

        @pl.when(present[end])
        def _(end=end):
            for piece in (SAMPLES, 0, 1, 2, 3):
                lat_copies[end][piece].start()

    for c in lon_copies:
        c.wait_recv()

    def unpack(from_west, from_east, k):
        e = pltpu.roll(from_east, (LANES - 4 * k) % LANES, 1) if k else from_east
        v = pltpu.roll(from_west, LANES - 4 - 4 * k, 1) if k < 31 else from_west
        return jnp.where(lane < 4, e, jnp.where(lane >= LANES - 4, v, 0.0))

    for v in range(2):
        fw, fe = lon_rx[0, v], lon_rx[1, v]
        for k in range(2 * rows):
            yh[2 * v + k // rows, w + k % rows] = unpack(fw, fe, k)
    fw, fe = lon_rx[0, 2], lon_rx[1, 2]
    for k in range(2 * rows):
        ah[1 + k // rows, w + k % rows] = unpack(fw, fe, k)
    fw, fe = lon_rx[0, 3], lon_rx[1, 3]
    for k in range(rows):
        ah[3, w + k] = unpack(fw, fe, k)
    for end in range(2):

        @pl.when(present[end])
        def _(end=end):
            for side in range(2):
                diag_copies[1 - end][side].wait_recv()

    for end, first in enumerate((0, w + rows)):
        fw, fe = diag_rx[end, 0], diag_rx[end, 1]
        k = 0
        for s in range(SAMPLES):
            for i in range(w):
                yh[s, first + i] = unpack(fw, fe, k)
                k += 1
        for f in range(3):
            for i in range(w):
                ah[1 + f, first + i] = unpack(fw, fe, k)
                k += 1

    for end in range(2):

        @pl.when(present[end])
        def _(end=end):
            lat_copies[1 - end][SAMPLES].wait_recv()

    def centre(a1, a2):
        return jnp.where(a1 > 0.0, 1.0, 0.0) - 2.0 * (a1 + a2)

    for e in range(tall):
        ah[0, e] = centre(ah[1, e], ah[2, e])
        if e < w or e >= w + rows:
            for h in range(2):
                a[0, e, h] = centre(a[1, e, h], a[2, e, h])
    for r in range(rows):
        for h in range(2):
            var[r, h] = zero

    first_lane, last_lane = lane == 0, lane == LANES - 1

    def diffuse(s):
        for t in range(1, ITERS + 1):
            last = t == ITERS

            def field(e, f):
                return [a[f, e, 0], a[f, e, 1], ah[f, e]]

            def products(e):
                z = [y[s, e, 0], y[s, e, 1], yh[s, e]]
                inside = t <= e < tall - t
                p1 = [u * v for u, v in zip(field(e, 1), z)]
                p3 = [u * v for u, v in zip(field(e, 3), z)]
                p0 = [u * v for u, v in zip(field(e, 0), z)] if inside else None
                p2 = [u * v for u, v in zip(field(e, 2), z)] if inside else None
                return p0, p1, p2, p3

            before, here = products(t - 1), products(t)
            for e in range(t, tall - t):
                after = products(e + 1)
                q = [u - v for u, v in zip(before[3], after[3])]
                left = [pltpu.roll(p + d, 1, 1) for p, d in zip(here[2], q)]
                right = [pltpu.roll(p - d, LANES - 1, 1) for p, d in zip(here[2], q)]
                for h in range(2 if last else 3):
                    total = here[0][h] + (before[1][h] + after[1][h])
                    total = total + jnp.where(first_lane, left[h - 1], left[h])
                    total = total + jnp.where(last_lane, right[(h + 1) % 3], right[h])
                    if h < 2:
                        y[s, e, h] = total
                    else:
                        yh[s, e] = total
                    if last:
                        var[e - w, h] += total * total
                before, here = here, after

    def sample(s, carry):
        for end in range(2):

            @pl.when(present[end])
            def _(end=end):
                mine, theirs = pl.ds((w, rows)[1 - end], w), pl.ds((w + rows, 0)[1 - end], w)
                remote(
                    y.at[s, mine], y.at[s, theirs], lat_tx_sem.at[1 - end, s], lat_rx_sem.at[end, s], pa_of[1 - end], ib
                ).wait_recv()
                remote(
                    y.at[s, theirs], y.at[s, theirs], lat_tx_sem.at[end, s], lat_rx_sem.at[end, s], pa_of[end], ib
                ).wait_send()

        diffuse(s)
        return carry

    lax.fori_loop(0, SAMPLES, sample, 0)

    total_v, total_m = zero, zero
    for r in range(rows):
        for h in range(2):
            wet = jnp.where(a[1, w + r, h] > 0.0, 1.0, 0.0)
            v = var[r, h] * (1.0 / SAMPLES)
            total_v = total_v + wet * v
            total_m = total_m + wet
            var[r, h] = wet * lax.rsqrt(jnp.where(wet > 0.0, v, 1.0) + 1e-06)

    row = lax.broadcasted_iota(jnp.int32, (LEVELS, LANES), 0)
    mine = jnp.where(row == 0, jnp.sum(total_v, axis=0, keepdims=True), jnp.sum(total_m, axis=0, keepdims=True))

    def rank(masks):
        out = 0
        for bit, (ma, mb) in enumerate(masks):
            hit = lax.bitwise_and(ia, ma) + lax.bitwise_and(ib, mb)
            out = out + jnp.where(hit > 0, 1 << bit, 0)
        return out

    def sums(phase, mine):
        group = groups[phase]
        size = len(group)
        me = rank([group[1 << i] for i in range(size.bit_length() - 1)])
        part[phase, me] = mine
        copies = []
        for m in range(1, size):
            ma, mb = group[m]
            there = lax.bitwise_xor(me, m)
            pa, pb = lax.bitwise_xor(ia, ma), lax.bitwise_xor(ib, mb)
            slot = part.at[phase, me, pl.ds(0, 2)]
            copies.append(remote(slot, slot, sum_tx_sem.at[phase, m], sum_rx_sem.at[phase, me], pa, pb))
            copies[-1].start()
        return me, copies

    def gather(phase, me, copies):
        size = len(groups[phase])
        for m in range(1, size):
            there = lax.bitwise_xor(me, m)
            slot = part.at[phase, there, pl.ds(0, 2)]
            remote(slot, slot, sum_tx_sem.at[phase, m], sum_rx_sem.at[phase, there], ia, ib).wait_recv()
        total = part[phase, 0, 0:2]
        for j in range(1, size):
            total = total + part[phase, j, 0:2]
        return total

    me0, sent0 = sums(0, mine)

    def scaled(s, carry):
        for r in range(rows):
            for h in range(2):
                raw[s, h, pl.ds(r, LEVELS, stride=rows), :] = y[s, w + r, h] * var[r, h]
        for h in range(2):
            pltpu.make_async_copy(raw.at[s, h], out.at[s, :, half(h)], out_sem.at[s, h]).start()
        return carry

    lax.fori_loop(0, SAMPLES, scaled, 0)
    total = gather(0, me0, sent0)
    me1, sent1 = sums(1, jnp.concatenate([total] * (LEVELS // 2), axis=0))
    for s in range(SAMPLES):
        for h in range(2):
            pltpu.make_async_copy(raw.at[s, h], out.at[s, :, half(h)], out_sem.at[s, h]).wait()
    total = gather(1, me1, sent1)
    both = jnp.sum(total, axis=1, keepdims=True)
    stat[...] = jnp.broadcast_to(both[0:1] / both[1:2], stat.shape)

    for c in lon_copies + sent0 + sent1:
        c.wait_send()
    for end in range(2):

        @pl.when(present[end])
        def _(end=end):
            for c in diag_copies[end] + [lat_copies[end][SAMPLES]]:
                c.wait_send()


def bits_of(n):
    return [1 << i for i in range(n.bit_length() - 1)]


def span(masks):
    out = [(0, 0)]
    for ma, mb in masks:
        out += [(x + ma, z + mb) for x, z in out]
    return out


def shards(n_lat, n_lon, noise, diff_lat, diff_lon, shear, sea_mask):
    samples, levels, rows, cols = noise.shape
    lat_bits, lon_bits = bits_of(n_lat), bits_of(n_lon)
    groups = (
        span([(b, 0) for b in lat_bits[:1]] + [(0, b) for b in lon_bits[1:]]),
        span([(b, 0) for b in lat_bits[1:]] + [(0, b) for b in lon_bits[:1]]),
    )
    size = max(len(g) for g in groups)
    tall = rows + 2 * ITERS
    flat = levels * rows
    f32 = jnp.float32
    anywhere = pl.BlockSpec(memory_space=pl.ANY)
    dma = pltpu.SemaphoreType.DMA
    field, stat = pl.pallas_call(
        functools.partial(kernel, n_lat, n_lon, rows, groups),
        out_shape=(
            jax.ShapeDtypeStruct((samples, flat, cols), f32),
            jax.ShapeDtypeStruct((1, LANES), f32),
        ),
        in_specs=[anywhere] * 5,
        out_specs=(anywhere, pl.BlockSpec(memory_space=pltpu.VMEM)),
        scratch_shapes=[
            pltpu.VMEM((samples, 2, flat, LANES), f32),
            pltpu.VMEM((3, 2, flat, LANES), f32),
            pltpu.VMEM((2, flat, LANES), jnp.int32),
            pltpu.VMEM((samples, tall, 2, levels, LANES), f32),
            pltpu.VMEM((samples, tall, levels, LANES), f32),
            pltpu.VMEM((4, tall, 2, levels, LANES), f32),
            pltpu.VMEM((4, tall, levels, LANES), f32),
            pltpu.VMEM((rows, 2, levels, LANES), f32),
            pltpu.VMEM((2, 4, levels, LANES), f32),
            pltpu.VMEM((2, 4, levels, LANES), f32),
            pltpu.VMEM((2, 2, levels, LANES), f32),
            pltpu.VMEM((2, 2, levels, LANES), f32),
            pltpu.VMEM((2, size, levels, LANES), f32),
            pltpu.VMEM((levels, LANES), f32),
            dma((8, 2)),
            dma((samples, 2)),
            dma((2, samples + 1)),
            dma((2, samples + 1)),
            dma((2,)),
            dma((2,)),
            dma((2, 2)),
            dma((2, 2)),
            dma((2, size)),
            dma((2, size)),
        ],
        compiler_params=pltpu.CompilerParams(
            collective_id=0, has_side_effects=True, vmem_limit_bytes=60 << 20
        ),
    )(
        noise.reshape(samples, flat, cols),
        diff_lat.reshape(flat, cols),
        diff_lon.reshape(flat, cols),
        shear.reshape(flat, cols),
        sea_mask.reshape(flat, cols),
    )
    mean_var = stat[0, 0]
    return ((field * jnp.sqrt(mean_var)).reshape(noise.shape), mean_var)


def solution(mesh):
    return jax.shard_map(
        functools.partial(shards, mesh.shape["lat"], mesh.shape["lon"]),
        mesh=mesh,
        in_specs=(
            P(None, None, "lat", "lon"),
            P(None, "lat", "lon"),
            P(None, "lat", "lon"),
            P(None, "lat", "lon"),
            P(None, "lat", "lon"),
        ),
        out_specs=(P(None, None, "lat", "lon"), P()),
        check_vma=False,
    )
```

```python
import functools

import jax
import jax.numpy as jnp
from jax import lax
from jax.experimental import pallas as pl
from jax.experimental.pallas import tpu as pltpu
from jax.sharding import PartitionSpec as P

SAMPLES = 4
LEVELS = 8
ITERS = 4
LANES = 128
MESH = pl.DeviceIdType.MESH


def kernel(
    n_lat, n_lon, rows, groups,
    noise, k_lat, k_lon, shear, sea,
    out, stat,
    raw, raw_k, raw_m, y, yh, a, ah, var, lon_tx, lon_rx, diag_tx, diag_rx, part, result,
    in_sem, lat_tx_sem, lat_rx_sem, lon_tx_sem, lon_rx_sem, diag_tx_sem, diag_rx_sem, sum_tx_sem, sum_rx_sem,
):
    w = ITERS
    tall = rows + 2 * w
    ia, ib = lax.axis_index("lat"), lax.axis_index("lon")
    east, west = lax.rem(ib + 1, n_lon), lax.rem(ib + n_lon - 1, n_lon)
    has_north, has_south = ia > 0, ia < n_lat - 1
    lane = lax.broadcasted_iota(jnp.int32, (LEVELS, LANES), 1)

    def half(h):
        return pl.ds(h * LANES, LANES)

    loads = []
    for f, src in enumerate((k_lat, k_lon, shear)):
        for h in range(2):
            loads.append(pltpu.make_async_copy(src.at[:, half(h)], raw_k.at[f, h], in_sem.at[f, h]))
    for h in range(2):
        loads.append(pltpu.make_async_copy(sea.at[:, half(h)], raw_m.at[h], in_sem.at[3, h]))
    for s in range(SAMPLES):
        for h in range(2):
            loads.append(pltpu.make_async_copy(noise.at[s, :, half(h)], raw.at[s, h], in_sem.at[4 + s, h]))
    barrier = pltpu.get_barrier_semaphore()

    def greet(pa, pb):
        pl.semaphore_signal(barrier, inc=1, device_id=(pa, pb), device_id_type=MESH)

    @pl.when(has_north)
    def _():
        for pb in (west, east, ib):
            greet(ia - 1, pb)

    @pl.when(has_south)
    def _():
        for pb in (west, east, ib):
            greet(ia + 1, pb)

    greet(ia, west)
    greet(ia, east)
    for c in loads:
        c.start()
    for group in groups:
        for ma, mb in group[1:]:
            greet(lax.bitwise_xor(ia, ma), lax.bitwise_xor(ib, mb))

    for c in loads[:8]:
        c.wait()
    for r in range(rows):
        for h in range(2):
            at = pl.ds(r, LEVELS, stride=rows)
            m = raw_m[h, at, :].astype(jnp.float32)
            k11 = raw_k[0, h, at, :]
            k22 = raw_k[1, h, at, :]
            a1 = m * k11
            a2 = m * k22
            a[1, w + r, h] = a1
            a[2, w + r, h] = a2
            a[3, w + r, h] = (0.5 * m) * (raw_k[2, h, at, :] * jnp.sqrt(k11 * k22))
            a[0, w + r, h] = m - 2.0 * (a1 + a2)
    for c in loads[8:]:
        c.wait()
    for s in range(SAMPLES):
        for r in range(rows):
            for h in range(2):
                y[s, w + r, h] = raw[s, h, pl.ds(r, LEVELS, stride=rows), :]

    group_of = lax.shift_right_logical(lane, 2)

    def pack(pieces):
        packed = jnp.zeros((LEVELS, LANES), jnp.float32)
        for k, (value, shift) in enumerate(pieces):
            moved = pltpu.roll(value, (shift + 4 * k) % LANES, 1) if (shift + 4 * k) % LANES else value
            packed = jnp.where(group_of == k, moved, packed)
        return packed

    for side, (h, shift) in enumerate(((1, 4), (0, 0))):
        for v in range(2):
            lon_tx[side, v] = pack([(y[2 * v + k // rows, w + k % rows, h], shift) for k in range(2 * rows)])
        lon_tx[side, 2] = pack([(a[1 + k // rows, w + k % rows, h], shift) for k in range(2 * rows)])
        lon_tx[side, 3] = pack([(a[3, w + k, h], shift) for k in range(rows)])
        for end, first in enumerate((w, rows)):
            pieces = [(y[s, first + i, h], shift) for s in range(SAMPLES) for i in range(w)]
            pieces += [(a[1 + f, first + i, h], shift) for f in range(3) for i in range(w)]
            diag_tx[end, side] = pack(pieces)

    zero = jnp.zeros((LEVELS, LANES), jnp.float32)

    def clear(first, corner):
        for i in range(w):
            for h in range(2):
                for f in range(1, 4):
                    a[f, first + i, h] = zero
                for s in range(SAMPLES):
                    y[s, first + i, h] = zero
        for side in range(2):
            diag_rx[corner, side] = zero

    @pl.when(jnp.logical_not(has_north))
    def _():
        clear(0, 0)

    @pl.when(jnp.logical_not(has_south))
    def _():
        clear(w + rows, 1)

    n_sum = sum(len(group) - 1 for group in groups)
    pl.semaphore_wait(barrier, 2 + n_sum + 3 * has_north.astype(jnp.int32) + 3 * has_south.astype(jnp.int32))

    def remote(src, dst, tx, rx, pa, pb):
        return pltpu.make_async_remote_copy(
            src_ref=src, dst_ref=dst, send_sem=tx, recv_sem=rx, device_id=(pa, pb), device_id_type=MESH
        )

    lon_copies = [
        remote(lon_tx.at[side], lon_rx.at[side], lon_tx_sem.at[side], lon_rx_sem.at[side], ia, (east, west)[side])
        for side in range(2)
    ]
    pa_of = (ia - 1, ia + 1)
    diag_copies = [
        [
            remote(diag_tx.at[end, side], diag_rx.at[1 - end, side], diag_tx_sem.at[end, side], diag_rx_sem.at[1 - end, side], pa_of[end], (east, west)[side])
            for side in range(2)
        ]
        for end in range(2)
    ]

    def lat_copy(end, piece):
        mine = pl.ds((w, rows)[end], w)
        theirs = pl.ds((w + rows, 0)[end], w)
        tx, rx = lat_tx_sem.at[end, piece], lat_rx_sem.at[1 - end, piece]
        if piece == SAMPLES:
            src, dst = a.at[pl.ds(1, 3), mine], a.at[pl.ds(1, 3), theirs]
        else:
            src, dst = y.at[piece, mine], y.at[piece, theirs]
        return remote(src, dst, tx, rx, pa_of[end], ib)

    lat_copies = [[lat_copy(end, piece) for piece in range(SAMPLES + 1)] for end in range(2)]
    present = (has_north, has_south)

    for end in range(2):

        @pl.when(present[end])
        def _(end=end):
            for c in diag_copies[end]:
                c.start()

    for c in lon_copies:
        c.start()
    for end in range(2):

        @pl.when(present[end])
        def _(end=end):
            for piece in (SAMPLES, 0, 1, 2, 3):
                lat_copies[end][piece].start()

    for c in lon_copies:
        c.wait_recv()

    def unpack(from_west, from_east, k):
        e = pltpu.roll(from_east, (LANES - 4 * k) % LANES, 1) if k else from_east
        v = pltpu.roll(from_west, LANES - 4 - 4 * k, 1) if k < 31 else from_west
        return jnp.where(lane < 4, e, jnp.where(lane >= LANES - 4, v, 0.0))

    for v in range(2):
        fw, fe = lon_rx[0, v], lon_rx[1, v]
        for k in range(2 * rows):
            yh[2 * v + k // rows, w + k % rows] = unpack(fw, fe, k)
    fw, fe = lon_rx[0, 2], lon_rx[1, 2]
    for k in range(2 * rows):
        ah[1 + k // rows, w + k % rows] = unpack(fw, fe, k)
    fw, fe = lon_rx[0, 3], lon_rx[1, 3]
    for k in range(rows):
        ah[3, w + k] = unpack(fw, fe, k)
    for end in range(2):

        @pl.when(present[end])
        def _(end=end):
            for side in range(2):
                diag_copies[1 - end][side].wait_recv()

    for end, first in enumerate((0, w + rows)):
        fw, fe = diag_rx[end, 0], diag_rx[end, 1]
        k = 0
        for s in range(SAMPLES):
            for i in range(w):
                yh[s, first + i] = unpack(fw, fe, k)
                k += 1
        for f in range(3):
            for i in range(w):
                ah[1 + f, first + i] = unpack(fw, fe, k)
                k += 1

    for end in range(2):

        @pl.when(present[end])
        def _(end=end):
            lat_copies[1 - end][SAMPLES].wait_recv()

    def centre(a1, a2):
        return jnp.where(a1 > 0.0, 1.0, 0.0) - 2.0 * (a1 + a2)

    for e in range(tall):
        ah[0, e] = centre(ah[1, e], ah[2, e])
        if e < w or e >= w + rows:
            for h in range(2):
                a[0, e, h] = centre(a[1, e, h], a[2, e, h])
    for r in range(rows):
        for h in range(2):
            var[r, h] = zero

    first_lane, last_lane = lane == 0, lane == LANES - 1

    def diffuse(s):
        for t in range(1, ITERS + 1):
            last = t == ITERS

            def field(e, f):
                return [a[f, e, 0], a[f, e, 1], ah[f, e]]

            def products(e):
                z = [y[s, e, 0], y[s, e, 1], yh[s, e]]
                inside = t <= e < tall - t
                p1 = [u * v for u, v in zip(field(e, 1), z)]
                p3 = [u * v for u, v in zip(field(e, 3), z)]
                p0 = [u * v for u, v in zip(field(e, 0), z)] if inside else None
                p2 = [u * v for u, v in zip(field(e, 2), z)] if inside else None
                return p0, p1, p2, p3

            before, here = products(t - 1), products(t)
            for e in range(t, tall - t):
                after = products(e + 1)
                q = [u - v for u, v in zip(before[3], after[3])]
                left = [pltpu.roll(p + d, 1, 1) for p, d in zip(here[2], q)]
                right = [pltpu.roll(p - d, LANES - 1, 1) for p, d in zip(here[2], q)]
                for h in range(2 if last else 3):
                    total = here[0][h] + (before[1][h] + after[1][h])
                    total = total + jnp.where(first_lane, left[h - 1], left[h])
                    total = total + jnp.where(last_lane, right[(h + 1) % 3], right[h])
                    if h < 2:
                        y[s, e, h] = total
                    else:
                        yh[s, e] = total
                    if last:
                        var[e - w, h] += total * total
                before, here = here, after

    def sample(s, carry):
        for end in range(2):

            @pl.when(present[end])
            def _(end=end):
                mine, theirs = pl.ds((w, rows)[1 - end], w), pl.ds((w + rows, 0)[1 - end], w)
                remote(
                    y.at[s, mine], y.at[s, theirs], lat_tx_sem.at[1 - end, s], lat_rx_sem.at[end, s], pa_of[1 - end], ib
                ).wait_recv()
                remote(
                    y.at[s, theirs], y.at[s, theirs], lat_tx_sem.at[end, s], lat_rx_sem.at[end, s], pa_of[end], ib
                ).wait_send()

        diffuse(s)
        return carry

    lax.fori_loop(0, SAMPLES, sample, 0)

    total_v, total_m = zero, zero
    for r in range(rows):
        for h in range(2):
            wet = jnp.where(a[1, w + r, h] > 0.0, 1.0, 0.0)
            v = var[r, h] * (1.0 / SAMPLES)
            total_v = total_v + wet * v
            total_m = total_m + wet
            var[r, h] = wet * lax.rsqrt(jnp.where(wet > 0.0, v, 1.0) + 1e-06)

    row = lax.broadcasted_iota(jnp.int32, (LEVELS, LANES), 0)
    mine = jnp.where(row == 0, jnp.sum(total_v, axis=0, keepdims=True), jnp.sum(total_m, axis=0, keepdims=True))

    def rank(masks):
        out = 0
        for bit, (ma, mb) in enumerate(masks):
            hit = lax.bitwise_and(ia, ma) + lax.bitwise_and(ib, mb)
            out = out + jnp.where(hit > 0, 1 << bit, 0)
        return out

    def sums(phase, mine):
        group = groups[phase]
        size = len(group)
        me = rank([group[1 << i] for i in range(size.bit_length() - 1)])
        part[phase, me] = mine
        copies = []
        for m in range(1, size):
            ma, mb = group[m]
            there = lax.bitwise_xor(me, m)
            pa, pb = lax.bitwise_xor(ia, ma), lax.bitwise_xor(ib, mb)
            slot = part.at[phase, me, pl.ds(0, 2)]
            copies.append(remote(slot, slot, sum_tx_sem.at[phase, m], sum_rx_sem.at[phase, me], pa, pb))
            copies[-1].start()
        return me, copies

    def gather(phase, me, copies):
        size = len(groups[phase])
        for m in range(1, size):
            there = lax.bitwise_xor(me, m)
            slot = part.at[phase, there, pl.ds(0, 2)]
            remote(slot, slot, sum_tx_sem.at[phase, m], sum_rx_sem.at[phase, there], ia, ib).wait_recv()
        total = part[phase, 0, 0:2]
        for j in range(1, size):
            total = total + part[phase, j, 0:2]
        return total

    me0, sent0 = sums(0, mine)

    def scaled(s, carry):
        for r in range(rows):
            for h in range(2):
                out[s, h, pl.ds(r, LEVELS, stride=rows), :] = y[s, w + r, h] * var[r, h]
        return carry

    lax.fori_loop(0, SAMPLES, scaled, 0)
    total = gather(0, me0, sent0)
    me1, sent1 = sums(1, jnp.concatenate([total] * (LEVELS // 2), axis=0))
    total = gather(1, me1, sent1)
    both = jnp.sum(total, axis=1, keepdims=True)
    stat[...] = jnp.broadcast_to(both[0:1] / both[1:2], stat.shape)

    for c in lon_copies + sent0 + sent1:
        c.wait_send()
    for end in range(2):

        @pl.when(present[end])
        def _(end=end):
            for c in diag_copies[end] + [lat_copies[end][SAMPLES]]:
                c.wait_send()


def scale(field, stat, out, mean, buf, sem):
    mean[...] = stat[...]
    factor = jnp.sqrt(stat[...])
    copies = []
    for s in range(SAMPLES):
        for h in range(2):
            buf[s, h] = field[s, h] * factor
            copies.append(pltpu.make_async_copy(buf.at[s, h], out.at[s, :, pl.ds(h * LANES, LANES)], sem.at[s, h]))
            copies[-1].start()
    for c in copies:
        c.wait()


def bits_of(n):
    return [1 << i for i in range(n.bit_length() - 1)]


def span(masks):
    out = [(0, 0)]
    for ma, mb in masks:
        out += [(x + ma, z + mb) for x, z in out]
    return out


def shards(n_lat, n_lon, noise, diff_lat, diff_lon, shear, sea_mask):
    samples, levels, rows, cols = noise.shape
    lat_bits, lon_bits = bits_of(n_lat), bits_of(n_lon)
    groups = (
        span([(b, 0) for b in lat_bits[:1]] + [(0, b) for b in lon_bits[1:]]),
        span([(b, 0) for b in lat_bits[1:]] + [(0, b) for b in lon_bits[:1]]),
    )
    size = max(len(g) for g in groups)
    tall = rows + 2 * ITERS
    flat = levels * rows
    f32 = jnp.float32
    dma = pltpu.SemaphoreType.DMA
    hbm = pl.BlockSpec(memory_space=pltpu.HBM)
    vmem = pl.BlockSpec(memory_space=pltpu.VMEM)
    field, stat = pl.pallas_call(
        functools.partial(kernel, n_lat, n_lon, rows, groups),
        out_shape=(
            pltpu.VMEM((samples, 2, flat, LANES), f32),
            pltpu.VMEM((1, LANES), f32),
        ),
        in_specs=[hbm] * 5,
        out_specs=(vmem, vmem),
        scratch_shapes=[
            pltpu.VMEM((samples, 2, flat, LANES), f32),
            pltpu.VMEM((3, 2, flat, LANES), f32),
            pltpu.VMEM((2, flat, LANES), jnp.int32),
            pltpu.VMEM((samples, tall, 2, levels, LANES), f32),
            pltpu.VMEM((samples, tall, levels, LANES), f32),
            pltpu.VMEM((4, tall, 2, levels, LANES), f32),
            pltpu.VMEM((4, tall, levels, LANES), f32),
            pltpu.VMEM((rows, 2, levels, LANES), f32),
            pltpu.VMEM((2, 4, levels, LANES), f32),
            pltpu.VMEM((2, 4, levels, LANES), f32),
            pltpu.VMEM((2, 2, levels, LANES), f32),
            pltpu.VMEM((2, 2, levels, LANES), f32),
            pltpu.VMEM((2, size, levels, LANES), f32),
            pltpu.VMEM((levels, LANES), f32),
            dma((8, 2)),
            dma((2, samples + 1)),
            dma((2, samples + 1)),
            dma((2,)),
            dma((2,)),
            dma((2, 2)),
            dma((2, 2)),
            dma((2, size)),
            dma((2, size)),
        ],
        compiler_params=pltpu.CompilerParams(
            collective_id=0, has_side_effects=True, vmem_limit_bytes=60 << 20
        ),
    )(
        noise.reshape(samples, flat, cols),
        diff_lat.reshape(flat, cols),
        diff_lon.reshape(flat, cols),
        shear.reshape(flat, cols),
        sea_mask.reshape(flat, cols),
    )
    out, mean_var = pl.pallas_call(
        scale,
        out_shape=(jax.ShapeDtypeStruct((samples, flat, cols), f32), jax.ShapeDtypeStruct((1, LANES), f32)),
        in_specs=[vmem, vmem],
        out_specs=(hbm, vmem),
        scratch_shapes=[pltpu.VMEM((samples, 2, flat, LANES), f32), dma((samples, 2))],
        compiler_params=pltpu.CompilerParams(vmem_limit_bytes=8 << 20),
    )(pltpu.with_memory_space_constraint(field, pltpu.VMEM), pltpu.with_memory_space_constraint(stat, pltpu.VMEM))
    return out.reshape(noise.shape), mean_var[0, 0]


def solution(mesh):
    return jax.shard_map(
        functools.partial(shards, mesh.shape["lat"], mesh.shape["lon"]),
        mesh=mesh,
        in_specs=(
            P(None, None, "lat", "lon"),
            P(None, "lat", "lon"),
            P(None, "lat", "lon"),
            P(None, "lat", "lon"),
            P(None, "lat", "lon"),
        ),
        out_specs=(P(None, None, "lat", "lon"), P()),
        check_vma=False,
    )
```

```python
import functools

import jax
import jax.numpy as jnp
from jax import lax
from jax.experimental import pallas as pl
from jax.experimental.pallas import tpu as pltpu
from jax.sharding import PartitionSpec as P

SAMPLES = 4
LEVELS = 8
ITERS = 4
LANES = 128
MESH = pl.DeviceIdType.MESH


def kernel(
    n_lat, n_lon, rows, groups,
    noise, k_lat, k_lon, shear, sea,
    out, stat,
    raw, raw_k, raw_m, x, a, edge_tx, edge_rx, k_tx, k_rx, k_mid, corner_tx, corner_rx, hx, ha, lon_tx, lon_rx, diag_tx, diag_rx, xs, var, part,
    in_sem, lat_tx_sem, lat_rx_sem, lon_tx_sem, lon_rx_sem, diag_tx_sem, diag_rx_sem, sum_tx_sem, sum_rx_sem,
):
    w = ITERS
    tall = rows + 2 * w
    ia, ib = lax.axis_index("lat"), lax.axis_index("lon")
    east, west = lax.rem(ib + 1, n_lon), lax.rem(ib + n_lon - 1, n_lon)
    has_north, has_south = ia > 0, ia < n_lat - 1
    present = (has_north, has_south)
    pa_of = (ia - 1, ia + 1)
    lane = lax.broadcasted_iota(jnp.int32, (LEVELS, LANES), 1)
    zero = jnp.zeros((LEVELS, LANES), jnp.float32)

    def half(h):
        return pl.ds(h * LANES, LANES)

    loads = []
    for f, src in enumerate((k_lat, k_lon, shear)):
        for h in range(2):
            loads.append(pltpu.make_async_copy(src.at[:, half(h)], raw_k.at[f, h], in_sem.at[f, h]))
    for h in range(2):
        loads.append(pltpu.make_async_copy(sea.at[:, half(h)], raw_m.at[h], in_sem.at[3, h]))
    for s in range(SAMPLES):
        for h in range(2):
            loads.append(pltpu.make_async_copy(noise.at[s, :, half(h)], raw.at[s, h], in_sem.at[4 + s, h]))

    barrier = pltpu.get_barrier_semaphore()

    def greet(pa, pb):
        pl.semaphore_signal(barrier, inc=1, device_id=(pa, pb), device_id_type=MESH)

    for end in range(2):

        @pl.when(present[end])
        def _(end=end):
            for pb in (west, east, ib):
                greet(pa_of[end], pb)

    greet(ia, west)
    greet(ia, east)
    for c in loads:
        c.start()
    for group in groups:
        for ma, mb in group[1:]:
            greet(lax.bitwise_xor(ia, ma), lax.bitwise_xor(ib, mb))

    for c in loads[:8]:
        c.wait()
    for r in range(rows):
        for h in range(2):
            at = pl.ds(r, LEVELS, stride=rows)
            m = raw_m[h, at, :].astype(jnp.float32)
            k11 = raw_k[0, h, at, :]
            k22 = raw_k[1, h, at, :]
            a1 = m * k11
            a2 = m * k22
            a[1, r, h] = a1
            a[2, r, h] = a2
            a[3, r, h] = (0.5 * m) * (raw_k[2, h, at, :] * jnp.sqrt(k11 * k22))
            a[0, r, h] = m - 2.0 * (a1 + a2)

    place = lax.bitwise_and(lane, 31)
    sample_of = lax.shift_right_logical(lane, 5)
    low_own = jnp.logical_and(place >= 4, place < 16)
    high_own = jnp.logical_and(place >= 16, place < 28)

    def rolled(value, shift):
        shift %= LANES
        return pltpu.roll(value, shift, 1) if shift else value

    def replicate(value):
        value = value + pltpu.roll(value, 32, 1)
        return value + pltpu.roll(value, 64, 1)

    for f in range(1, 4):
        for r in range(rows):
            low = jnp.where(jnp.logical_and(low_own, lane < 32), rolled(a[f, r, 0], 4), 0.0)
            high = jnp.where(jnp.logical_and(high_own, lane < 32), rolled(a[f, r, 1], 28), low)
            ha[f, w + r] = replicate(high)

    for c in loads[8:]:
        c.wait()
    for s in range(SAMPLES):
        for r in range(rows):
            for h in range(2):
                x[0, s, r, h] = raw[s, h, pl.ds(r, LEVELS, stride=rows), :]
    for r in range(rows):
        side = zero
        for s in range(SAMPLES):
            mine = sample_of == s
            side = jnp.where(jnp.logical_and(low_own, mine), rolled(x[0, s, r, 0], 32 * s + 4), side)
            side = jnp.where(jnp.logical_and(high_own, mine), rolled(x[0, s, r, 1], 32 * s + 28), side)
        hx[0, w + r] = side

    offset = (24, 4)
    fours = lax.shift_right_logical(lane, 2)
    in_sample = lax.bitwise_and(fours, 7)
    for side in range(2):
        for v in range(2):
            packed, packed_k = zero, zero
            for j in range(8):
                e = w + 8 * v + j
                packed = jnp.where(in_sample == j, rolled(hx[0, e], 4 * j - offset[side]), packed)
                for f in range(3):
                    packed_k = jnp.where(fours == 8 * f + j, rolled(ha[1 + f, e], 4 * j - offset[side]), packed_k)
            lon_tx[side, v] = packed
            lon_tx[side, 2 + v] = packed_k
        for end, first in enumerate((w, rows)):
            packed = zero
            for i in range(w):
                e = first + i
                packed = jnp.where(in_sample == i, rolled(hx[0, e], 4 * i - offset[side]), packed)
                for f in range(3):
                    packed = jnp.where(fours == 8 * f + 4 + i, rolled(ha[1 + f, e], 16 + 4 * i - offset[side]), packed)
            diag_tx[end, side] = packed

    first_of_two = lax.bitwise_and(lane + 4, 8) != 0
    block_of = lax.bitwise_and(lax.shift_right_logical(lane + LANES - 4, 5), 3)
    for end, first in enumerate((w, rows)):
        for n in range(w // 2):
            e = first + 2 * n
            corner_tx[end, n] = jnp.where(first_of_two, hx[0, e], rolled(hx[0, e + 1], 8))
            packed = zero
            for f in range(3):
                two = jnp.where(first_of_two, ha[1 + f, e], rolled(ha[1 + f, e + 1], 8))
                packed = jnp.where(block_of == f, two, packed)
            corner_tx[end, 2 + n] = packed

    first_lane, last_lane = lane == 0, lane == LANES - 1

    def left(u):
        r0, r1 = pltpu.roll(u[0], 1, 1), pltpu.roll(u[1], 1, 1)
        return [r0, jnp.where(first_lane, r0, r1)]

    def right(u):
        r0, r1 = pltpu.roll(u[0], LANES - 1, 1), pltpu.roll(u[1], LANES - 1, 1)
        return [jnp.where(last_lane, r1, r0), r1]

    def add(*lists):
        lists = [u for u in lists if u is not None]
        total = lists[0]
        for u in lists[1:]:
            total = [p + q for p, q in zip(total, u)]
        return total

    def sub(u, v):
        return [p - q for p, q in zip(u, v)]

    def times(weights, z):
        return [[p * q for p, q in zip(k, z)] if k is not None else None for k in weights]

    def combine(local, above, below, known=None):
        base = add(*[u for u in (known, local and local[0], above and above[1], below and below[1]) if u is not None])
        q3 = sub(above[3], below[3]) if above and below else None
        if local and q3:
            u, v = add(local[2], q3), sub(local[2], q3)
        elif local and above:
            u, v = add(local[2], above[3]), sub(local[2], above[3])
        elif local:
            u, v = sub(local[2], below[3]), add(local[2], below[3])
        elif above:
            return add(base, sub(left(above[3]), right(above[3])))
        else:
            return add(base, sub(right(below[3]), left(below[3])))
        return add(base, add(left(u), right(v)))

    def weights_of(r):
        return [[a[f, r, 0], a[f, r, 1]] for f in range(4)]

    def state(t, s, r):
        return [x[t, s, r, 0], x[t, s, r, 1]]

    def store(t, s, r, value):
        x[t, s, r, 0] = value[0]
        x[t, s, r, 1] = value[1]

    def advance(t, s, first, last):
        def term(r):
            return times(weights_of(r), state(t - 1, s, r))

        above, here = term(first - 1), term(first)
        for r in range(first, last):
            below = term(r + 1)
            store(t, s, r, combine(here, above, below))
            above, here = here, below

    for end in range(2):
        rows_in = (0, 1) if end == 0 else (rows - 1, rows - 2)
        for n, (f, d) in enumerate(((1, 0), (2, 0), (3, 0), (1, 1), (3, 1))):
            for h in range(2):
                k_tx[end, n, h] = a[f, rows_in[d], h]

    def prepare(s, carry):
        advance(1, s, 1, 3)
        advance(1, s, rows - 3, rows - 1)
        for end in range(2):
            row = (lambda d: d) if end == 0 else (lambda d: rows - 1 - d)

            def crossing(term, end=end):
                return combine(None, None, term) if end == 0 else combine(None, term, None)

            def partial(local, inner, end=end):
                return combine(local, None, inner) if end == 0 else combine(local, inner, None)

            t00 = times(weights_of(row(0)), state(0, s, row(0)))
            t01 = times(weights_of(row(1)), state(0, s, row(1)))
            t11 = times(weights_of(row(1)), state(1, s, row(1)))
            t12 = times(weights_of(row(2)), state(1, s, row(2)))
            pieces = (crossing(t00), partial(t00, t01), crossing(t11), partial(t11, t12))
            for n, value in enumerate(pieces):
                for h in range(2):
                    edge_tx[end, s, n, h] = value[h]
        return carry

    lax.fori_loop(0, SAMPLES, prepare, 0)

    for end in range(2):

        @pl.when(jnp.logical_not(present[end]))
        def _(end=end):
            for h in range(2):
                for n in range(5):
                    k_rx[end, n, h] = zero
                for s in range(SAMPLES):
                    for n in range(w):
                        edge_rx[end, s, n, h] = zero
            for side in range(2):
                diag_rx[end, side] = zero
            for n in range(4):
                corner_rx[end, n] = zero

    n_sum = sum(len(group) - 1 for group in groups)
    pl.semaphore_wait(barrier, 2 + n_sum + 3 * has_north.astype(jnp.int32) + 3 * has_south.astype(jnp.int32))

    def remote(src, dst, tx, rx, pa, pb):
        return pltpu.make_async_remote_copy(
            src_ref=src, dst_ref=dst, send_sem=tx, recv_sem=rx, device_id=(pa, pb), device_id_type=MESH
        )

    lon_copies = [
        remote(lon_tx.at[side], lon_rx.at[side], lon_tx_sem.at[side], lon_rx_sem.at[side], ia, (east, west)[side])
        for side in range(2)
    ]
    diag_copies = [
        [
            remote(diag_tx.at[end, side], diag_rx.at[1 - end, side], diag_tx_sem.at[end, side], diag_rx_sem.at[1 - end, side], pa_of[end], (east, west)[side])
            for side in range(2)
        ]
        for end in range(2)
    ]

    def lat_copy(end, piece):
        tx, rx = lat_tx_sem.at[end, piece], lat_rx_sem.at[1 - end, piece]
        if isinstance(piece, int) and piece == SAMPLES:
            return remote(k_tx.at[end], k_rx.at[1 - end], tx, rx, pa_of[end], ib)
        if isinstance(piece, int) and piece == SAMPLES + 1:
            return remote(corner_tx.at[end], corner_rx.at[1 - end], tx, rx, pa_of[end], ib)
        return remote(edge_tx.at[end, piece], edge_rx.at[1 - end, piece], tx, rx, pa_of[end], ib)

    lat_copies = [[lat_copy(end, piece) for piece in range(SAMPLES + 2)] for end in range(2)]

    for end in range(2):

        @pl.when(present[end])
        def _(end=end):
            for c in diag_copies[end]:
                c.start()

    for c in lon_copies:
        c.start()
    for piece in (SAMPLES + 1, SAMPLES, 0, 1, 2, 3):
        for end in range(2):

            @pl.when(present[end])
            def _(end=end, piece=piece):
                lat_copies[end][piece].start()

    def interior(s, carry):
        advance(1, s, 3, rows - 3)
        for t in range(2, ITERS + 1):
            advance(t, s, t, rows - t)
        return carry

    lax.fori_loop(0, SAMPLES, interior, 0)

    for c in lon_copies:
        c.wait_recv()
    from_west, from_east = place < 4, place >= 28
    for v in range(2):
        fw, fe = lon_rx[0, v], lon_rx[1, v]
        for j in range(8):
            e = w + 8 * v + j
            side = jnp.where(from_west, rolled(fw, -4 * j), hx[0, e])
            hx[0, e] = jnp.where(from_east, rolled(fe, 28 - 4 * j), side)
        for f in range(3):
            mine = sample_of == f
            fw = replicate(rolled(jnp.where(mine, lon_rx[0, 2 + v], 0.0), -32 * f))
            fe = replicate(rolled(jnp.where(mine, lon_rx[1, 2 + v], 0.0), -32 * f))
            for j in range(8):
                e = w + 8 * v + j
                side = jnp.where(from_west, rolled(fw, -4 * j), ha[1 + f, e])
                ha[1 + f, e] = jnp.where(from_east, rolled(fe, 28 - 4 * j), side)
    for end, first in enumerate((0, w + rows)):

        @pl.when(present[end])
        def _(end=end):
            for side in range(2):
                diag_copies[1 - end][side].wait_recv()
            lat_copies[1 - end][SAMPLES + 1].wait_recv()

        dw, de = diag_rx[end, 0], diag_rx[end, 1]

        def border(own, fw, fe, i):
            side = jnp.where(from_west, rolled(fw, -4 * i), rolled(own, -8 * (i % 2)))
            return jnp.where(from_east, rolled(fe, 28 - 4 * i), side)

        for i in range(w):
            hx[0, first + i] = border(corner_rx[end, i // 2], dw, de, i)
        for f in range(3):
            mine = jnp.logical_and(sample_of == f, place >= 16)
            fw = replicate(rolled(jnp.where(mine, dw, 0.0), -32 * f - 16))
            fe = replicate(rolled(jnp.where(mine, de, 0.0), -32 * f - 16))
            for n in range(w // 2):
                own = replicate(rolled(jnp.where(block_of == f, corner_rx[end, 2 + n], 0.0), -32 * f))
                for i in (2 * n, 2 * n + 1):
                    ha[1 + f, first + i] = border(own, fw, fe, i)

    def centre(a1, a2):
        return jnp.where(a1 > 0.0, 1.0, 0.0) - 2.0 * (a1 + a2)

    for e in range(tall):
        ha[0, e] = centre(ha[1, e], ha[2, e])
    for t in range(1, ITERS + 1):

        def term(e):
            z = hx[t - 1, e]
            return [ha[f, e] * z for f in range(4)]

        above, here = term(t - 1), term(t)
        for e in range(t, tall - t):
            below = term(e + 1)
            q3 = above[3] - below[3]
            total = here[0] + (above[1] + below[1])
            total = total + pltpu.roll(here[2] + q3, 1, 1)
            hx[t, e] = total + pltpu.roll(here[2] - q3, LANES - 1, 1)
            above, here = here, below

    low_edge, high_edge = lane < 4, lane >= LANES - 4
    for s in range(SAMPLES):
        for r in range(rows):
            side = hx[ITERS, w + r]
            xs[s, r] = jnp.where(low_edge, rolled(side, -32 * s - 4), rolled(side, 100 - 32 * s))
    def finish(s, r, value):
        value = [jnp.where(low_edge, xs[s, r], value[0]), jnp.where(high_edge, xs[s, r], value[1])]
        store(ITERS, s, r, value)
        return [u * u for u in value]

    def wet_sum(total, r, squares):
        for h in range(2):
            v = squares[h] * (1.0 / SAMPLES)
            var[r, h] = v
            total = total + jnp.where(a[1, r, h] > 0.0, v, 0.0)
        return total

    total_v, total_m = zero, zero
    for r in range(rows):
        for h in range(2):
            total_m = total_m + jnp.where(a[1, r, h] > 0.0, 1.0, 0.0)
    for r in range(w, rows - w):
        total_v = wet_sum(total_v, r, add(*[finish(s, r, state(ITERS, s, r)) for s in range(SAMPLES)]))

    for end in range(2):

        @pl.when(present[end])
        def _(end=end):
            lat_copies[1 - end][SAMPLES].wait_recv()

        for h in range(2):
            k_mid[end, h] = centre(k_rx[end, 0, h], k_rx[end, 1, h])

    squares = {}

    def edges(samples):
        for s in samples:
            for end in range(2):

                @pl.when(present[end])
                def _(s=s, end=end):
                    lat_copies[1 - end][s].wait_recv()

        ends = [(end, s) for s in samples for end in range(2)]
        for end, s in ends:
            row = (lambda d: d) if end == 0 else (lambda d: rows - 1 - d)

            def toward(local, outer, inner, known=None, end=end):
                above, below = (outer, inner) if end == 0 else (inner, outer)
                return combine(local, above, below, known)

            def halo(n, end=end):
                return [k_rx[end, n, 0], k_rx[end, n, 1]]

            def known(n, end=end, s=s):
                return [edge_rx[end, s, n, 0], edge_rx[end, s, n, 1]]

            near = [[k_mid[end, 0], k_mid[end, 1]], halo(0), halo(1), halo(2)]
            far = [None, halo(3), None, halo(4)]
            mine = [weights_of(row(d)) for d in range(ITERS + 1)]

            def term(d, value, mine=mine):
                return times(mine[d], value)

            def saved(t, d, row=row, s=s):
                return state(t, s, row(d))

            t0 = [term(d, saved(0, d)) for d in range(2)]
            n1 = toward(None, None, t0[0], known(1))
            y1 = toward(t0[0], None, t0[1], known(0))
            tn = times(near, n1)
            t1 = [term(0, y1), term(1, saved(1, 1)), term(2, saved(1, 2))]
            f2 = toward(None, None, tn, known(3))
            n2 = toward(tn, None, t1[0], known(2))
            y2 = [toward(t1[0], tn, t1[1]), toward(t1[1], t1[0], t1[2])]
            tf, tn = times(far, f2), times(near, n2)
            t2 = [term(0, y2[0]), term(1, y2[1]), term(2, saved(2, 2)), term(3, saved(2, 3))]
            n3 = toward(tn, tf, t2[0])
            y3 = [toward(t2[0], tn, t2[1]), toward(t2[1], t2[0], t2[2]), toward(t2[2], t2[1], t2[3])]
            tn = times(near, n3)
            t3 = [term(d, y3[d]) for d in range(3)] + [term(d, saved(3, d)) for d in (3, 4)]
            for d in range(ITERS):
                value = toward(t3[d], tn if d == 0 else t3[d - 1], t3[d + 1])
                squares.setdefault(row(d), []).append(finish(s, row(d), value))

    edges((0, 1))
    for r in list(squares):
        part_v = add(*squares.pop(r))
        var[r, 0], var[r, 1] = part_v
    edges((2, 3))
    for r in sorted(squares):
        total_v = wet_sum(total_v, r, add([var[r, 0], var[r, 1]], *squares[r]))

    row = lax.broadcasted_iota(jnp.int32, (LEVELS, LANES), 0)
    mine = jnp.where(row == 0, jnp.sum(total_v, axis=0, keepdims=True), jnp.sum(total_m, axis=0, keepdims=True))

    def rank(masks):
        out = 0
        for bit, (ma, mb) in enumerate(masks):
            hit = lax.bitwise_and(ia, ma) + lax.bitwise_and(ib, mb)
            out = out + jnp.where(hit > 0, 1 << bit, 0)
        return out

    def sums(phase, mine):
        group = groups[phase]
        size = len(group)
        me = rank([group[1 << i] for i in range(size.bit_length() - 1)])
        part[phase, me] = mine
        copies = []
        for m in range(1, size):
            ma, mb = group[m]
            pa, pb = lax.bitwise_xor(ia, ma), lax.bitwise_xor(ib, mb)
            slot = part.at[phase, me, pl.ds(0, 2)]
            copies.append(remote(slot, slot, sum_tx_sem.at[phase], sum_rx_sem.at[phase], pa, pb))
            copies[-1].start()

    def all_but_mine(phase):
        slots = part.at[phase, pl.ds(0, len(groups[phase]) - 1), pl.ds(0, 2)]
        return remote(slots, slots, sum_tx_sem.at[phase], sum_rx_sem.at[phase], ia, ib)

    def gather(phase):
        all_but_mine(phase).wait_recv()
        total = part[phase, 0, 0:2]
        for j in range(1, len(groups[phase])):
            total = total + part[phase, j, 0:2]
        return total

    sums(0, mine)
    for r in range(rows):
        for h in range(2):
            wet = jnp.where(a[1, r, h] > 0.0, 1.0, 0.0)
            var[r, h] = wet * lax.rsqrt(jnp.where(wet > 0.0, var[r, h], 1.0) + 1e-06)

    def scaled(s, carry):
        for r in range(rows):
            for h in range(2):
                out[s, h, pl.ds(r, LEVELS, stride=rows), :] = x[ITERS, s, r, h] * var[r, h]
        return carry

    lax.fori_loop(0, SAMPLES, scaled, 0)
    for c in lon_copies:
        c.wait_send()
    for end in range(2):

        @pl.when(present[end])
        def _(end=end):
            for c in diag_copies[end] + lat_copies[end]:
                c.wait_send()

    total = gather(0)
    sums(1, jnp.concatenate([total] * (LEVELS // 2), axis=0))
    for phase in range(2):
        all_but_mine(phase).wait_send()
    total = gather(1)
    both = jnp.sum(total, axis=1, keepdims=True)
    stat[...] = jnp.broadcast_to(both[0:1] / both[1:2], stat.shape)


def scale(field, stat, out, mean, buf, sem):
    copies = [pltpu.make_async_copy(stat, mean, sem.at[SAMPLES, 0])]
    copies[0].start()
    factor = jnp.sqrt(stat[...])
    for s in range(SAMPLES):
        for h in range(2):
            buf[s, h] = field[s, h] * factor
            copies.append(pltpu.make_async_copy(buf.at[s, h], out.at[s, :, pl.ds(h * LANES, LANES)], sem.at[s, h]))
            copies[-1].start()
    for c in copies:
        c.wait()


def bits_of(n):
    return [1 << i for i in range(n.bit_length() - 1)]


def span(masks):
    out = [(0, 0)]
    for ma, mb in masks:
        out += [(x + ma, z + mb) for x, z in out]
    return out


def shards(n_lat, n_lon, noise, diff_lat, diff_lon, shear, sea_mask):
    samples, levels, rows, cols = noise.shape
    lat_bits, lon_bits = bits_of(n_lat), bits_of(n_lon)
    groups = (
        span([(b, 0) for b in lat_bits[:1]] + [(0, b) for b in lon_bits[1:]]),
        span([(b, 0) for b in lat_bits[1:]] + [(0, b) for b in lon_bits[:1]]),
    )
    size = max(len(g) for g in groups)
    tall = rows + 2 * ITERS
    flat = levels * rows
    f32 = jnp.float32
    dma = pltpu.SemaphoreType.DMA
    hbm = pl.BlockSpec(memory_space=pltpu.HBM)
    vmem = pl.BlockSpec(memory_space=pltpu.VMEM)
    field, stat = pl.pallas_call(
        functools.partial(kernel, n_lat, n_lon, rows, groups),
        out_shape=(
            pltpu.VMEM((samples, 2, flat, LANES), f32),
            pltpu.VMEM((1, LANES), f32),
        ),
        in_specs=[hbm] * 5,
        out_specs=(vmem, vmem),
        scratch_shapes=[
            pltpu.VMEM((samples, 2, flat, LANES), f32),
            pltpu.VMEM((3, 2, flat, LANES), f32),
            pltpu.VMEM((2, flat, LANES), jnp.int32),
            pltpu.VMEM((ITERS + 1, samples, rows, 2, levels, LANES), f32),
            pltpu.VMEM((4, rows, 2, levels, LANES), f32),
            pltpu.VMEM((2, samples, ITERS, 2, levels, LANES), f32),
            pltpu.VMEM((2, samples, ITERS, 2, levels, LANES), f32),
            pltpu.VMEM((2, 5, 2, levels, LANES), f32),
            pltpu.VMEM((2, 5, 2, levels, LANES), f32),
            pltpu.VMEM((2, 2, levels, LANES), f32),
            pltpu.VMEM((2, 4, levels, LANES), f32),
            pltpu.VMEM((2, 4, levels, LANES), f32),
            pltpu.VMEM((ITERS + 1, tall, levels, LANES), f32),
            pltpu.VMEM((4, tall, levels, LANES), f32),
            pltpu.VMEM((2, 4, levels, LANES), f32),
            pltpu.VMEM((2, 4, levels, LANES), f32),
            pltpu.VMEM((2, 2, levels, LANES), f32),
            pltpu.VMEM((2, 2, levels, LANES), f32),
            pltpu.VMEM((samples, rows, levels, LANES), f32),
            pltpu.VMEM((rows, 2, levels, LANES), f32),
            pltpu.VMEM((2, size, levels, LANES), f32),
            dma((8, 2)),
            dma((2, samples + 2)),
            dma((2, samples + 2)),
            dma((2,)),
            dma((2,)),
            dma((2, 2)),
            dma((2, 2)),
            dma((2,)),
            dma((2,)),
        ],
        compiler_params=pltpu.CompilerParams(
            collective_id=0, has_side_effects=True, vmem_limit_bytes=60 << 20
        ),
    )(
        noise.reshape(samples, flat, cols),
        diff_lat.reshape(flat, cols),
        diff_lon.reshape(flat, cols),
        shear.reshape(flat, cols),
        sea_mask.reshape(flat, cols),
    )
    out, mean_var = pl.pallas_call(
        scale,
        out_shape=(jax.ShapeDtypeStruct((samples, flat, cols), f32), jax.ShapeDtypeStruct((1, LANES), f32)),
        in_specs=[vmem, vmem],
        out_specs=(hbm, hbm),
        scratch_shapes=[pltpu.VMEM((samples, 2, flat, LANES), f32), dma((samples + 1, 2))],
        compiler_params=pltpu.CompilerParams(vmem_limit_bytes=8 << 20),
    )(pltpu.with_memory_space_constraint(field, pltpu.VMEM), pltpu.with_memory_space_constraint(stat, pltpu.VMEM))
    return out.reshape(noise.shape), mean_var[0, 0]


def solution(mesh):
    return jax.shard_map(
        functools.partial(shards, mesh.shape["lat"], mesh.shape["lon"]),
        mesh=mesh,
        in_specs=(
            P(None, None, "lat", "lon"),
            P(None, "lat", "lon"),
            P(None, "lat", "lon"),
            P(None, "lat", "lon"),
            P(None, "lat", "lon"),
        ),
        out_specs=(P(None, None, "lat", "lon"), P()),
        check_vma=False,
    )
```

```python
import functools

import jax
import jax.numpy as jnp
from jax import lax
from jax.experimental import pallas as pl
from jax.experimental.pallas import tpu as pltpu
from jax.sharding import PartitionSpec as P

SAMPLES = 4
LEVELS = 8
ITERS = 4
LANES = 128
MESH = pl.DeviceIdType.MESH


def kernel(
    n_lat, n_lon, rows, groups,
    noise, k_lat, k_lon, shear, sea,
    out, stat,
    raw, raw_k, raw_m, x, a, edge_tx, edge_rx, k_tx, k_rx, k_mid, echo, corner_tx, corner_rx, hx, ha, lon_tx, lon_rx, diag_tx, diag_rx, xs, var, part,
    in_sem, lat_tx_sem, lat_rx_sem, lon_tx_sem, lon_rx_sem, diag_tx_sem, diag_rx_sem, sum_tx_sem, sum_rx_sem,
):
    w = ITERS
    tall = rows + 2 * w
    ia, ib = lax.axis_index("lat"), lax.axis_index("lon")
    east, west = lax.rem(ib + 1, n_lon), lax.rem(ib + n_lon - 1, n_lon)
    has_north, has_south = ia > 0, ia < n_lat - 1
    present = (has_north, has_south)
    pa_of = (ia - 1, ia + 1)
    lane = lax.broadcasted_iota(jnp.int32, (LEVELS, LANES), 1)
    zero = jnp.zeros((LEVELS, LANES), jnp.float32)

    def half(h):
        return pl.ds(h * LANES, LANES)

    loads = []
    for f, src in enumerate((k_lat, k_lon, shear)):
        for h in range(2):
            loads.append(pltpu.make_async_copy(src.at[:, half(h)], raw_k.at[f, h], in_sem.at[f, h]))
    for h in range(2):
        loads.append(pltpu.make_async_copy(sea.at[:, half(h)], raw_m.at[h], in_sem.at[3, h]))
    for s in range(SAMPLES):
        for h in range(2):
            loads.append(pltpu.make_async_copy(noise.at[s, :, half(h)], raw.at[s, h], in_sem.at[4 + s, h]))

    barrier = pltpu.get_barrier_semaphore()

    def greet(pa, pb):
        pl.semaphore_signal(barrier, inc=1, device_id=(pa, pb), device_id_type=MESH)

    for end in range(2):

        @pl.when(present[end])
        def _(end=end):
            for pb in (west, east, ib):
                greet(pa_of[end], pb)

    greet(ia, west)
    greet(ia, east)
    for c in loads:
        c.start()
    for group in groups:
        for ma, mb in group[1:]:
            greet(lax.bitwise_xor(ia, ma), lax.bitwise_xor(ib, mb))

    for c in loads[:8]:
        c.wait()
    for r in range(rows):
        for h in range(2):
            at = pl.ds(r, LEVELS, stride=rows)
            m = raw_m[h, at, :].astype(jnp.float32)
            k11 = raw_k[0, h, at, :]
            k22 = raw_k[1, h, at, :]
            a1 = m * k11
            a2 = m * k22
            a[1, r, h] = a1
            a[2, r, h] = a2
            a[3, r, h] = (0.5 * m) * (raw_k[2, h, at, :] * jnp.sqrt(k11 * k22))
            a[0, r, h] = m - 2.0 * (a1 + a2)

    place = lax.bitwise_and(lane, 31)
    sample_of = lax.shift_right_logical(lane, 5)
    low_own = jnp.logical_and(place >= 4, place < 16)
    high_own = jnp.logical_and(place >= 16, place < 28)

    def rolled(value, shift):
        shift %= LANES
        return pltpu.roll(value, shift, 1) if shift else value

    def replicate(value):
        value = value + pltpu.roll(value, 32, 1)
        return value + pltpu.roll(value, 64, 1)

    for f in range(1, 4):
        for r in range(rows):
            low = jnp.where(jnp.logical_and(low_own, lane < 32), rolled(a[f, r, 0], 4), 0.0)
            high = jnp.where(jnp.logical_and(high_own, lane < 32), rolled(a[f, r, 1], 28), low)
            ha[f, w + r] = replicate(high)

    for c in loads[8:]:
        c.wait()
    for s in range(SAMPLES):
        for r in range(rows):
            for h in range(2):
                x[0, s, r, h] = raw[s, h, pl.ds(r, LEVELS, stride=rows), :]
    for r in range(rows):
        side = zero
        for s in range(SAMPLES):
            mine = sample_of == s
            side = jnp.where(jnp.logical_and(low_own, mine), rolled(x[0, s, r, 0], 32 * s + 4), side)
            side = jnp.where(jnp.logical_and(high_own, mine), rolled(x[0, s, r, 1], 32 * s + 28), side)
        hx[0, w + r] = side

    offset = (24, 4)
    fours = lax.shift_right_logical(lane, 2)
    in_sample = lax.bitwise_and(fours, 7)
    for side in range(2):
        for v in range(2):
            packed, packed_k = zero, zero
            for j in range(8):
                e = w + 8 * v + j
                packed = jnp.where(in_sample == j, rolled(hx[0, e], 4 * j - offset[side]), packed)
                for f in range(3):
                    packed_k = jnp.where(fours == 8 * f + j, rolled(ha[1 + f, e], 4 * j - offset[side]), packed_k)
            lon_tx[side, v] = packed
            lon_tx[side, 2 + v] = packed_k
        for end, first in enumerate((w, rows)):
            packed = zero
            for i in range(w):
                e = first + i
                packed = jnp.where(in_sample == i, rolled(hx[0, e], 4 * i - offset[side]), packed)
                for f in range(3):
                    packed = jnp.where(fours == 8 * f + 4 + i, rolled(ha[1 + f, e], 16 + 4 * i - offset[side]), packed)
            diag_tx[end, side] = packed

    first_of_two = lax.bitwise_and(lane + 4, 8) != 0
    block_of = lax.bitwise_and(lax.shift_right_logical(lane + LANES - 4, 5), 3)
    for end, first in enumerate((w, rows)):
        for n in range(w // 2):
            e = first + 2 * n
            corner_tx[end, n] = jnp.where(first_of_two, hx[0, e], rolled(hx[0, e + 1], 8))
            packed = zero
            for f in range(3):
                two = jnp.where(first_of_two, ha[1 + f, e], rolled(ha[1 + f, e + 1], 8))
                packed = jnp.where(block_of == f, two, packed)
            corner_tx[end, 2 + n] = packed

    first_lane, last_lane = lane == 0, lane == LANES - 1

    def left(u):
        r0, r1 = pltpu.roll(u[0], 1, 1), pltpu.roll(u[1], 1, 1)
        return [r0, jnp.where(first_lane, r0, r1)]

    def right(u):
        r0, r1 = pltpu.roll(u[0], LANES - 1, 1), pltpu.roll(u[1], LANES - 1, 1)
        return [jnp.where(last_lane, r1, r0), r1]

    def add(*lists):
        lists = [u for u in lists if u is not None]
        total = lists[0]
        for u in lists[1:]:
            total = [p + q for p, q in zip(total, u)]
        return total

    def sub(u, v):
        return [p - q for p, q in zip(u, v)]

    def times(weights, z):
        return [[p * q for p, q in zip(k, z)] if k is not None else None for k in weights]

    def combine(local, above, below, known=None):
        base = add(*[u for u in (known, local and local[0], above and above[1], below and below[1]) if u is not None])
        q3 = sub(above[3], below[3]) if above and below else None
        if local and q3:
            u, v = add(local[2], q3), sub(local[2], q3)
        elif local and above:
            u, v = add(local[2], above[3]), sub(local[2], above[3])
        elif local:
            u, v = sub(local[2], below[3]), add(local[2], below[3])
        elif above:
            return add(base, sub(left(above[3]), right(above[3])))
        else:
            return add(base, sub(right(below[3]), left(below[3])))
        return add(base, add(left(u), right(v)))

    def weights_of(r):
        return [[a[f, r, 0], a[f, r, 1]] for f in range(4)]

    def state(t, s, r):
        return [x[t, s, r, 0], x[t, s, r, 1]]

    def store(t, s, r, value):
        x[t, s, r, 0] = value[0]
        x[t, s, r, 1] = value[1]

    def advance(t, s, first, last):
        def term(r):
            return times(weights_of(r), state(t - 1, s, r))

        above, here = term(first - 1), term(first)
        for r in range(first, last):
            below = term(r + 1)
            store(t, s, r, combine(here, above, below))
            above, here = here, below

    for end in range(2):
        rows_in = (0, 1) if end == 0 else (rows - 1, rows - 2)
        for n, (f, d) in enumerate(((1, 0), (2, 0), (3, 0), (1, 1), (3, 1))):
            for h in range(2):
                k_tx[end, n, h] = a[f, rows_in[d], h]

    pairs = [(end, s) for s in range(SAMPLES) for end in range(2)]

    def row_of(end, d):
        return d if end == 0 else rows - 1 - d

    def term(t, end, s, d):
        return times(weights_of(row_of(end, d)), state(t, s, row_of(end, d)))

    def cross(n, end, s, local):
        value = combine(None, None, local) if end == 0 else combine(None, local, None)
        for h in range(2):
            edge_tx[end, n, s, h] = value[h]

    def partial(end, local, inner, outer=None):
        return combine(local, outer, inner) if end == 0 else combine(local, inner, outer)

    for end, s in pairs:
        cross(0, end, s, term(0, end, s, 0))

    for end in range(2):

        @pl.when(jnp.logical_not(present[end]))
        def _(end=end):
            for h in range(2):
                for n in range(5):
                    k_rx[end, n, h] = zero
                for s in range(SAMPLES):
                    for n in range(w):
                        edge_rx[end, n, s, h] = zero
            for side in range(2):
                diag_rx[end, side] = zero
            for n in range(4):
                corner_rx[end, n] = zero

    n_sum = sum(len(group) - 1 for group in groups)
    pl.semaphore_wait(barrier, 2 + n_sum + 3 * has_north.astype(jnp.int32) + 3 * has_south.astype(jnp.int32))

    def remote(src, dst, tx, rx, pa, pb):
        return pltpu.make_async_remote_copy(
            src_ref=src, dst_ref=dst, send_sem=tx, recv_sem=rx, device_id=(pa, pb), device_id_type=MESH
        )

    lon_copies = [
        remote(lon_tx.at[side], lon_rx.at[side], lon_tx_sem.at[side], lon_rx_sem.at[side], ia, (east, west)[side])
        for side in range(2)
    ]
    diag_copies = [
        [
            remote(diag_tx.at[end, side], diag_rx.at[1 - end, side], diag_tx_sem.at[end, side], diag_rx_sem.at[1 - end, side], pa_of[end], (east, west)[side])
            for side in range(2)
        ]
        for end in range(2)
    ]

    def lat_copy(end, piece):
        tx, rx = lat_tx_sem.at[end, piece], lat_rx_sem.at[1 - end, piece]
        if piece == ITERS:
            return remote(k_tx.at[end], k_rx.at[1 - end], tx, rx, pa_of[end], ib)
        if piece == ITERS + 1:
            return remote(corner_tx.at[end], corner_rx.at[1 - end], tx, rx, pa_of[end], ib)
        return remote(edge_tx.at[end, piece], edge_rx.at[1 - end, piece], tx, rx, pa_of[end], ib)

    lat_copies = [[lat_copy(end, piece) for piece in range(ITERS + 2)] for end in range(2)]

    for end in range(2):

        @pl.when(present[end])
        def _(end=end):
            for c in diag_copies[end]:
                c.start()

    for c in lon_copies:
        c.start()
    def send(piece):
        for end in range(2):

            @pl.when(present[end])
            def _(end=end):
                lat_copies[end][piece].start()

    send(ITERS + 1)
    send(0)
    send(ITERS)
    alone = {}
    for end, s in pairs:
        alone[end, s] = times(weights_of(row_of(end, 0)), partial(end, term(0, end, s, 0), term(0, end, s, 1)))
        cross(1, end, s, alone[end, s])
    send(1)
    for s in range(SAMPLES):
        advance(1, s, 1, 3)
        advance(1, s, rows - 3, rows - 1)
    for end, s in pairs:
        t10, t11 = alone[end, s], term(1, end, s, 1)
        t20 = times(weights_of(row_of(end, 0)), partial(end, t10, t11))
        t21 = times(weights_of(row_of(end, 1)), partial(end, t11, term(1, end, s, 2), t10))
        alone[end, s] = t20, t21
        cross(2, end, s, t20)
    send(2)
    for end, s in pairs:
        cross(3, end, s, times(weights_of(row_of(end, 0)), partial(end, *alone[end, s])))
    send(3)

    def interior(s, carry):
        advance(1, s, 3, rows - 3)
        for t in range(2, ITERS + 1):
            advance(t, s, t, rows - t)
        return carry

    lax.fori_loop(0, SAMPLES, interior, 0)

    for c in lon_copies:
        c.wait_recv()
    beyond_edge = jnp.logical_or(place < 4, place >= 28)
    even_four = lax.bitwise_and(fours, 1) == 0
    block_before = lax.bitwise_and(lax.shift_right_logical(lane + 4, 5), 3)

    def woven(fw, fe, shift):
        fe = rolled(fe, shift)
        return jnp.where(even_four, fw, fe), jnp.where(even_four, fe, fw)

    for v in range(2):
        both = woven(lon_rx[0, v], lon_rx[1, v], 28)
        for j in range(8):
            e = w + 8 * v + j
            hx[0, e] = jnp.where(beyond_edge, rolled(both[j % 2], -4 * j), hx[0, e])
        both = woven(lon_rx[0, 2 + v], lon_rx[1, 2 + v], -4)
        for f in range(3):
            even = replicate(jnp.where(block_before == f, both[0], 0.0))
            odd = replicate(jnp.where(sample_of == f, both[1], 0.0))
            for j in range(8):
                e = w + 8 * v + j
                ha[1 + f, e] = jnp.where(beyond_edge, rolled((even, odd)[j % 2], -4 * j), ha[1 + f, e])
    for end, first in enumerate((0, w + rows)):

        @pl.when(present[end])
        def _(end=end):
            for side in range(2):
                diag_copies[1 - end][side].wait_recv()
            lat_copies[1 - end][ITERS + 1].wait_recv()

        dw, de = diag_rx[end, 0], diag_rx[end, 1]
        both = woven(dw, de, 28)
        for i in range(w):
            own = rolled(corner_rx[end, i // 2], -8 * (i % 2))
            hx[0, first + i] = jnp.where(beyond_edge, rolled(both[i % 2], -4 * i), own)
        both = woven(dw, de, -4)
        for f in range(3):
            mine = jnp.logical_and(sample_of == f, place >= 12)
            halves = [replicate(jnp.where(mine, u, 0.0)) for u in both]
            for n in range(w // 2):
                own = replicate(jnp.where(block_of == f, corner_rx[end, 2 + n], 0.0))
                for i in (2 * n, 2 * n + 1):
                    moved = rolled(halves[i % 2], -16 - 4 * i)
                    ha[1 + f, first + i] = jnp.where(beyond_edge, moved, rolled(own, -8 * (i % 2)))

    def centre(a1, a2):
        return jnp.where(a1 > 0.0, 1.0, 0.0) - 2.0 * (a1 + a2)

    for e in range(tall):
        ha[0, e] = centre(ha[1, e], ha[2, e])
    for t in range(1, ITERS + 1):

        def term(e):
            z = hx[t - 1, e]
            return [ha[f, e] * z for f in range(4)]

        above, here = term(t - 1), term(t)
        for e in range(t, tall - t):
            below = term(e + 1)
            q3 = above[3] - below[3]
            total = here[0] + (above[1] + below[1])
            total = total + pltpu.roll(here[2] + q3, 1, 1)
            hx[t, e] = total + pltpu.roll(here[2] - q3, LANES - 1, 1)
            above, here = here, below

    low_edge, high_edge = lane < 4, lane >= LANES - 4
    for r in range(rows):
        side = hx[ITERS, w + r]
        side = jnp.where(place < 4, rolled(side, -24), side)
        for s in range(SAMPLES):
            xs[s, r] = rolled(side, -32 * s - 4)

    def finish(s, r, value):
        value = [jnp.where(low_edge, xs[s, r], value[0]), jnp.where(high_edge, xs[s, r], value[1])]
        store(ITERS, s, r, value)
        return [u * u for u in value]

    def wet_sum(total, r, squares):
        for h in range(2):
            v = squares[h] * (1.0 / SAMPLES)
            var[r, h] = v
            total = total + jnp.where(a[1, r, h] > 0.0, v, 0.0)
        return total

    total_v, total_m = zero, zero
    for r in range(rows):
        for h in range(2):
            total_m = total_m + jnp.where(a[1, r, h] > 0.0, 1.0, 0.0)
    for r in range(w, rows - w):
        total_v = wet_sum(total_v, r, add(*[finish(s, r, state(ITERS, s, r)) for s in range(SAMPLES)]))

    def arrived(piece):
        for end in range(2):

            @pl.when(present[end])
            def _(end=end):
                lat_copies[1 - end][piece].wait_recv()

    def toward(end, local, outer, inner, known=None):
        above, below = (outer, inner) if end == 0 else (inner, outer)
        return combine(local, above, below, known)

    def known(n, end, s):
        return [edge_rx[end, n, s, 0], edge_rx[end, n, s, 1]]

    def near(end):
        return [[k_mid[end, 0], k_mid[end, 1]]] + [[k_rx[end, n, 0], k_rx[end, n, 1]] for n in range(3)]

    def far(end):
        return [None, [k_rx[end, 3, 0], k_rx[end, 3, 1]], None, [k_rx[end, 4, 0], k_rx[end, 4, 1]]]

    def keep(end, s, n, value):
        echo[end, s, n, 0], echo[end, s, n, 1] = value

    def kept(end, s, n):
        return [echo[end, s, n, 0], echo[end, s, n, 1]]

    def terms(t, end, s, count):
        return [times(weights_of(row_of(end, d)), state(t, s, row_of(end, d))) for d in range(count)]

    arrived(0)
    for end, s in pairs:
        t0 = terms(0, end, s, 2)
        keep(end, s, 0, toward(end, None, None, t0[0]))
        store(1, s, row_of(end, 0), toward(end, t0[0], None, t0[1], known(0, end, s)))
    arrived(ITERS)
    for end in range(2):
        for h in range(2):
            k_mid[end, h] = centre(k_rx[end, 0, h], k_rx[end, 1, h])
    arrived(1)
    for end, s in pairs:
        t1 = terms(1, end, s, 3)
        beyond = times(near(end), kept(end, s, 0))
        keep(end, s, 1, toward(end, None, None, beyond))
        keep(end, s, 0, toward(end, beyond, None, t1[0]))
        store(2, s, row_of(end, 0), toward(end, t1[0], beyond, t1[1], known(1, end, s)))
        store(2, s, row_of(end, 1), toward(end, t1[1], t1[0], t1[2]))
    arrived(2)
    for end, s in pairs:
        t2 = terms(2, end, s, 4)
        beyond = times(near(end), kept(end, s, 0))
        keep(end, s, 0, toward(end, beyond, times(far(end), kept(end, s, 1)), t2[0]))
        store(3, s, row_of(end, 0), toward(end, t2[0], beyond, t2[1], known(2, end, s)))
        for d in (1, 2):
            store(3, s, row_of(end, d), toward(end, t2[d], t2[d - 1], t2[d + 1]))
    squares = {}
    for end, s in pairs:
        t3 = terms(3, end, s, 5)
        beyond = times(near(end), kept(end, s, 0))
        store(ITERS, s, row_of(end, 0), toward(end, t3[0], beyond, t3[1]))
        for d in range(1, ITERS):
            r = row_of(end, d)
            squares.setdefault(r, []).append(finish(s, r, toward(end, t3[d], t3[d - 1], t3[d + 1])))
    for r in sorted(squares):
        total_v = wet_sum(total_v, r, add(*squares[r]))
    arrived(3)
    for end in range(2):
        r = row_of(end, 0)
        ends = [finish(s, r, add(state(ITERS, s, r), known(3, end, s))) for s in range(SAMPLES)]
        total_v = wet_sum(total_v, r, add(*ends))

    row = lax.broadcasted_iota(jnp.int32, (LEVELS, LANES), 0)
    mine = jnp.where(row == 0, jnp.sum(total_v, axis=0, keepdims=True), jnp.sum(total_m, axis=0, keepdims=True))

    def rank(masks):
        out = 0
        for bit, (ma, mb) in enumerate(masks):
            hit = lax.bitwise_and(ia, ma) + lax.bitwise_and(ib, mb)
            out = out + jnp.where(hit > 0, 1 << bit, 0)
        return out

    def sums(phase, mine):
        group = groups[phase]
        size = len(group)
        me = rank([group[1 << i] for i in range(size.bit_length() - 1)])
        part[phase, me] = mine
        copies = []
        for m in range(1, size):
            ma, mb = group[m]
            pa, pb = lax.bitwise_xor(ia, ma), lax.bitwise_xor(ib, mb)
            slot = part.at[phase, me, pl.ds(0, 2)]
            copies.append(remote(slot, slot, sum_tx_sem.at[phase], sum_rx_sem.at[phase], pa, pb))
            copies[-1].start()

    def all_but_mine(phase):
        slots = part.at[phase, pl.ds(0, len(groups[phase]) - 1), pl.ds(0, 2)]
        return remote(slots, slots, sum_tx_sem.at[phase], sum_rx_sem.at[phase], ia, ib)

    def gather(phase):
        all_but_mine(phase).wait_recv()
        total = part[phase, 0, 0:2]
        for j in range(1, len(groups[phase])):
            total = total + part[phase, j, 0:2]
        return total

    sums(0, mine)
    for r in range(rows):
        for h in range(2):
            wet = jnp.where(a[1, r, h] > 0.0, 1.0, 0.0)
            var[r, h] = wet * lax.rsqrt(jnp.where(wet > 0.0, var[r, h], 1.0) + 1e-06)

    def scaled(s, carry):
        for r in range(rows):
            for h in range(2):
                out[s, h, pl.ds(r, LEVELS, stride=rows), :] = x[ITERS, s, r, h] * var[r, h]
        return carry

    lax.fori_loop(0, SAMPLES, scaled, 0)
    for c in lon_copies:
        c.wait_send()
    for end in range(2):

        @pl.when(present[end])
        def _(end=end):
            for c in diag_copies[end] + lat_copies[end]:
                c.wait_send()

    total = gather(0)
    sums(1, jnp.concatenate([total] * (LEVELS // 2), axis=0))
    for phase in range(2):
        all_but_mine(phase).wait_send()
    total = gather(1)
    both = jnp.sum(total, axis=1, keepdims=True)
    stat[...] = jnp.broadcast_to(both[0:1] / both[1:2], stat.shape)


def scale(field, stat, out, mean, buf, sem):
    copies = [pltpu.make_async_copy(stat, mean, sem.at[SAMPLES, 0])]
    copies[0].start()
    factor = jnp.sqrt(stat[...])
    for s in range(SAMPLES):
        for h in range(2):
            buf[s, h] = field[s, h] * factor
            copies.append(pltpu.make_async_copy(buf.at[s, h], out.at[s, :, pl.ds(h * LANES, LANES)], sem.at[s, h]))
            copies[-1].start()
    for c in copies:
        c.wait()


def bits_of(n):
    return [1 << i for i in range(n.bit_length() - 1)]


def span(masks):
    out = [(0, 0)]
    for ma, mb in masks:
        out += [(x + ma, z + mb) for x, z in out]
    return out


def shards(n_lat, n_lon, noise, diff_lat, diff_lon, shear, sea_mask):
    samples, levels, rows, cols = noise.shape
    lat_bits, lon_bits = bits_of(n_lat), bits_of(n_lon)
    groups = (
        span([(b, 0) for b in lat_bits[:1]] + [(0, b) for b in lon_bits[1:]]),
        span([(b, 0) for b in lat_bits[1:]] + [(0, b) for b in lon_bits[:1]]),
    )
    size = max(len(g) for g in groups)
    tall = rows + 2 * ITERS
    flat = levels * rows
    f32 = jnp.float32
    dma = pltpu.SemaphoreType.DMA
    hbm = pl.BlockSpec(memory_space=pltpu.HBM)
    vmem = pl.BlockSpec(memory_space=pltpu.VMEM)
    field, stat = pl.pallas_call(
        functools.partial(kernel, n_lat, n_lon, rows, groups),
        out_shape=(
            pltpu.VMEM((samples, 2, flat, LANES), f32),
            pltpu.VMEM((1, LANES), f32),
        ),
        in_specs=[hbm] * 5,
        out_specs=(vmem, vmem),
        scratch_shapes=[
            pltpu.VMEM((samples, 2, flat, LANES), f32),
            pltpu.VMEM((3, 2, flat, LANES), f32),
            pltpu.VMEM((2, flat, LANES), jnp.int32),
            pltpu.VMEM((ITERS + 1, samples, rows, 2, levels, LANES), f32),
            pltpu.VMEM((4, rows, 2, levels, LANES), f32),
            pltpu.VMEM((2, ITERS, samples, 2, levels, LANES), f32),
            pltpu.VMEM((2, ITERS, samples, 2, levels, LANES), f32),
            pltpu.VMEM((2, 5, 2, levels, LANES), f32),
            pltpu.VMEM((2, 5, 2, levels, LANES), f32),
            pltpu.VMEM((2, 2, levels, LANES), f32),
            pltpu.VMEM((2, samples, 2, 2, levels, LANES), f32),
            pltpu.VMEM((2, 4, levels, LANES), f32),
            pltpu.VMEM((2, 4, levels, LANES), f32),
            pltpu.VMEM((ITERS + 1, tall, levels, LANES), f32),
            pltpu.VMEM((4, tall, levels, LANES), f32),
            pltpu.VMEM((2, 4, levels, LANES), f32),
            pltpu.VMEM((2, 4, levels, LANES), f32),
            pltpu.VMEM((2, 2, levels, LANES), f32),
            pltpu.VMEM((2, 2, levels, LANES), f32),
            pltpu.VMEM((samples, rows, levels, LANES), f32),
            pltpu.VMEM((rows, 2, levels, LANES), f32),
            pltpu.VMEM((2, size, levels, LANES), f32),
            dma((8, 2)),
            dma((2, ITERS + 2)),
            dma((2, ITERS + 2)),
            dma((2,)),
            dma((2,)),
            dma((2, 2)),
            dma((2, 2)),
            dma((2,)),
            dma((2,)),
        ],
        compiler_params=pltpu.CompilerParams(
            collective_id=0, has_side_effects=True, vmem_limit_bytes=60 << 20
        ),
    )(
        noise.reshape(samples, flat, cols),
        diff_lat.reshape(flat, cols),
        diff_lon.reshape(flat, cols),
        shear.reshape(flat, cols),
        sea_mask.reshape(flat, cols),
    )
    out, mean_var = pl.pallas_call(
        scale,
        out_shape=(jax.ShapeDtypeStruct((samples, flat, cols), f32), jax.ShapeDtypeStruct((1, LANES), f32)),
        in_specs=[vmem, vmem],
        out_specs=(hbm, hbm),
        scratch_shapes=[pltpu.VMEM((samples, 2, flat, LANES), f32), dma((samples + 1, 2))],
        compiler_params=pltpu.CompilerParams(vmem_limit_bytes=8 << 20),
    )(pltpu.with_memory_space_constraint(field, pltpu.VMEM), pltpu.with_memory_space_constraint(stat, pltpu.VMEM))
    return out.reshape(noise.shape), mean_var[0, 0]


def solution(mesh):
    return jax.shard_map(
        functools.partial(shards, mesh.shape["lat"], mesh.shape["lon"]),
        mesh=mesh,
        in_specs=(
            P(None, None, "lat", "lon"),
            P(None, "lat", "lon"),
            P(None, "lat", "lon"),
            P(None, "lat", "lon"),
            P(None, "lat", "lon"),
        ),
        out_specs=(P(None, None, "lat", "lon"), P()),
        check_vma=False,
    )
```

```python
import functools

import jax
import jax.numpy as jnp
from jax import lax
from jax.experimental import pallas as pl
from jax.experimental.pallas import tpu as pltpu
from jax.sharding import PartitionSpec as P

SAMPLES = 4
LEVELS = 8
ITERS = 4
LANES = 128
MESH = pl.DeviceIdType.MESH


def kernel(
    n_lat, n_lon, rows, groups,
    noise, k_lat, k_lon, shear, sea,
    out, stat,
    raw, raw_k, raw_m, x, a, edge_tx, edge_rx, k_tx, k_rx, k_mid, echo, corner_tx, corner_rx, hx, ha, lon_tx, lon_rx, diag_tx, diag_rx, xs, var, part,
    in_sem, lat_tx_sem, lat_rx_sem, lon_tx_sem, lon_rx_sem, diag_tx_sem, diag_rx_sem, sum_tx_sem, sum_rx_sem,
):
    w = ITERS
    tall = rows + 2 * w
    ia, ib = lax.axis_index("lat"), lax.axis_index("lon")
    east, west = lax.rem(ib + 1, n_lon), lax.rem(ib + n_lon - 1, n_lon)
    has_north, has_south = ia > 0, ia < n_lat - 1
    present = (has_north, has_south)
    pa_of = (ia - 1, ia + 1)
    lane = lax.broadcasted_iota(jnp.int32, (LEVELS, LANES), 1)
    zero = jnp.zeros((LEVELS, LANES), jnp.float32)

    def half(h):
        return pl.ds(h * LANES, LANES)

    loads = []
    for f, src in enumerate((k_lat, k_lon, shear)):
        for h in range(2):
            loads.append(pltpu.make_async_copy(src.at[:, half(h)], raw_k.at[f, h], in_sem.at[f, h]))
    for h in range(2):
        loads.append(pltpu.make_async_copy(sea.at[:, half(h)], raw_m.at[h], in_sem.at[3, h]))
    for s in range(SAMPLES):
        for h in range(2):
            loads.append(pltpu.make_async_copy(noise.at[s, :, half(h)], raw.at[s, h], in_sem.at[4 + s, h]))

    barrier = pltpu.get_barrier_semaphore()

    def greet(pa, pb):
        pl.semaphore_signal(barrier, inc=1, device_id=(pa, pb), device_id_type=MESH)

    for end in range(2):

        @pl.when(present[end])
        def _(end=end):
            for pb in (west, east, ib):
                greet(pa_of[end], pb)

    greet(ia, west)
    greet(ia, east)
    for c in loads:
        c.start()
    for group in groups:
        for ma, mb in group[1:]:
            greet(lax.bitwise_xor(ia, ma), lax.bitwise_xor(ib, mb))

    for c in loads[:8]:
        c.wait()
    for r in range(rows):
        for h in range(2):
            at = pl.ds(r, LEVELS, stride=rows)
            m = raw_m[h, at, :].astype(jnp.float32)
            k11 = raw_k[0, h, at, :]
            k22 = raw_k[1, h, at, :]
            a1 = m * k11
            a2 = m * k22
            a[1, r, h] = a1
            a[2, r, h] = a2
            a[3, r, h] = (0.5 * m) * (raw_k[2, h, at, :] * jnp.sqrt(k11 * k22))
            a[0, r, h] = m - 2.0 * (a1 + a2)

    place = lax.bitwise_and(lane, 31)
    sample_of = lax.shift_right_logical(lane, 5)
    low_own = jnp.logical_and(place >= 4, place < 16)
    high_own = jnp.logical_and(place >= 16, place < 28)

    def rolled(value, shift):
        shift %= LANES
        return pltpu.roll(value, shift, 1) if shift else value

    def replicate(value):
        value = value + pltpu.roll(value, 32, 1)
        return value + pltpu.roll(value, 64, 1)

    for f in range(1, 4):
        for r in range(rows):
            low = jnp.where(jnp.logical_and(low_own, lane < 32), rolled(a[f, r, 0], 4), 0.0)
            high = jnp.where(jnp.logical_and(high_own, lane < 32), rolled(a[f, r, 1], 28), low)
            ha[f, w + r] = replicate(high)

    for c in loads[8:]:
        c.wait()
    for s in range(SAMPLES):
        for r in range(rows):
            for h in range(2):
                x[0, s, r, h] = raw[s, h, pl.ds(r, LEVELS, stride=rows), :]
    for r in range(rows):
        side = zero
        for s in range(SAMPLES):
            mine = sample_of == s
            side = jnp.where(jnp.logical_and(low_own, mine), rolled(x[0, s, r, 0], 32 * s + 4), side)
            side = jnp.where(jnp.logical_and(high_own, mine), rolled(x[0, s, r, 1], 32 * s + 28), side)
        hx[0, w + r] = side

    offset = (24, 4)
    fours = lax.shift_right_logical(lane, 2)
    in_sample = lax.bitwise_and(fours, 7)
    for side in range(2):
        for v in range(2):
            packed, packed_k = zero, zero
            for j in range(8):
                e = w + 8 * v + j
                packed = jnp.where(in_sample == j, rolled(hx[0, e], 4 * j - offset[side]), packed)
                for f in range(3):
                    packed_k = jnp.where(fours == 8 * f + j, rolled(ha[1 + f, e], 4 * j - offset[side]), packed_k)
            lon_tx[side, v] = packed
            lon_tx[side, 2 + v] = packed_k
        for end, first in enumerate((w, rows)):
            packed = zero
            for i in range(w):
                e = first + i
                packed = jnp.where(in_sample == i, rolled(hx[0, e], 4 * i - offset[side]), packed)
                for f in range(3):
                    packed = jnp.where(fours == 8 * f + 4 + i, rolled(ha[1 + f, e], 16 + 4 * i - offset[side]), packed)
            diag_tx[end, side] = packed

    first_of_two = lax.bitwise_and(lane + 4, 8) != 0
    block_of = lax.bitwise_and(lax.shift_right_logical(lane + LANES - 4, 5), 3)
    for end, first in enumerate((w, rows)):
        for n in range(w // 2):
            e = first + 2 * n
            corner_tx[end, n] = jnp.where(first_of_two, hx[0, e], rolled(hx[0, e + 1], 8))
            packed = zero
            for f in range(3):
                two = jnp.where(first_of_two, ha[1 + f, e], rolled(ha[1 + f, e + 1], 8))
                packed = jnp.where(block_of == f, two, packed)
            corner_tx[end, 2 + n] = packed

    first_lane, last_lane = lane == 0, lane == LANES - 1

    def left(u):
        r0, r1 = pltpu.roll(u[0], 1, 1), pltpu.roll(u[1], 1, 1)
        return [r0, jnp.where(first_lane, r0, r1)]

    def right(u):
        r0, r1 = pltpu.roll(u[0], LANES - 1, 1), pltpu.roll(u[1], LANES - 1, 1)
        return [jnp.where(last_lane, r1, r0), r1]

    def add(*lists):
        lists = [u for u in lists if u is not None]
        total = lists[0]
        for u in lists[1:]:
            total = [p + q for p, q in zip(total, u)]
        return total

    def sub(u, v):
        return [p - q for p, q in zip(u, v)]

    def times(weights, z):
        return [[p * q for p, q in zip(k, z)] if k is not None else None for k in weights]

    def combine(local, above, below, known=None):
        base = add(*[u for u in (known, local and local[0], above and above[1], below and below[1]) if u is not None])
        q3 = sub(above[3], below[3]) if above and below else None
        if local and q3:
            u, v = add(local[2], q3), sub(local[2], q3)
        elif local and above:
            u, v = add(local[2], above[3]), sub(local[2], above[3])
        elif local:
            u, v = sub(local[2], below[3]), add(local[2], below[3])
        elif above:
            return add(base, sub(left(above[3]), right(above[3])))
        else:
            return add(base, sub(right(below[3]), left(below[3])))
        return add(base, add(left(u), right(v)))

    def weights_of(r):
        return [[a[f, r, 0], a[f, r, 1]] for f in range(4)]

    def state(t, s, r):
        return [x[t, s, r, 0], x[t, s, r, 1]]

    def store(t, s, r, value):
        x[t, s, r, 0] = value[0]
        x[t, s, r, 1] = value[1]

    def advance(t, s, first, last):
        def term(r):
            return times(weights_of(r), state(t - 1, s, r))

        above, here = term(first - 1), term(first)
        for r in range(first, last):
            below = term(r + 1)
            store(t, s, r, combine(here, above, below))
            above, here = here, below

    for end in range(2):
        rows_in = (0, 1) if end == 0 else (rows - 1, rows - 2)
        for n, (f, d) in enumerate(((1, 0), (2, 0), (3, 0), (1, 1), (3, 1))):
            for h in range(2):
                k_tx[end, n, h] = a[f, rows_in[d], h]

    pairs = [(end, s) for s in range(SAMPLES) for end in range(2)]

    def row_of(end, d):
        return d if end == 0 else rows - 1 - d

    def term(t, end, s, d):
        return times(weights_of(row_of(end, d)), state(t, s, row_of(end, d)))

    def cross(n, end, s, local):
        value = combine(None, None, local) if end == 0 else combine(None, local, None)
        for h in range(2):
            edge_tx[end, n, s, h] = value[h]

    def partial(end, local, inner, outer=None):
        return combine(local, outer, inner) if end == 0 else combine(local, inner, outer)

    for end, s in pairs:
        cross(0, end, s, term(0, end, s, 0))

    for end in range(2):

        @pl.when(jnp.logical_not(present[end]))
        def _(end=end):
            for h in range(2):
                for n in range(5):
                    k_rx[end, n, h] = zero
                for s in range(SAMPLES):
                    for n in range(w):
                        edge_rx[end, n, s, h] = zero
            for side in range(2):
                diag_rx[end, side] = zero
            for n in range(4):
                corner_rx[end, n] = zero

    n_sum = sum(len(group) - 1 for group in groups)
    pl.semaphore_wait(barrier, 2 + n_sum + 3 * has_north.astype(jnp.int32) + 3 * has_south.astype(jnp.int32))

    def remote(src, dst, tx, rx, pa, pb):
        return pltpu.make_async_remote_copy(
            src_ref=src, dst_ref=dst, send_sem=tx, recv_sem=rx, device_id=(pa, pb), device_id_type=MESH
        )

    lon_copies = [
        remote(lon_tx.at[side], lon_rx.at[side], lon_tx_sem.at[side], lon_rx_sem.at[side], ia, (east, west)[side])
        for side in range(2)
    ]
    diag_copies = [
        [
            remote(diag_tx.at[end, side], diag_rx.at[1 - end, side], diag_tx_sem.at[end, side], diag_rx_sem.at[1 - end, side], pa_of[end], (east, west)[side])
            for side in range(2)
        ]
        for end in range(2)
    ]

    def lat_copy(end, piece):
        tx, rx = lat_tx_sem.at[end, piece], lat_rx_sem.at[1 - end, piece]
        if piece == ITERS:
            return remote(k_tx.at[end], k_rx.at[1 - end], tx, rx, pa_of[end], ib)
        if piece == ITERS + 1:
            return remote(corner_tx.at[end], corner_rx.at[1 - end], tx, rx, pa_of[end], ib)
        return remote(edge_tx.at[end, piece], edge_rx.at[1 - end, piece], tx, rx, pa_of[end], ib)

    lat_copies = [[lat_copy(end, piece) for piece in range(ITERS + 2)] for end in range(2)]

    for end in range(2):

        @pl.when(present[end])
        def _(end=end):
            for c in diag_copies[end]:
                c.start()

    for c in lon_copies:
        c.start()
    def send(piece):
        for end in range(2):

            @pl.when(present[end])
            def _(end=end):
                lat_copies[end][piece].start()

    send(ITERS + 1)
    send(0)
    send(ITERS)
    alone = {}
    for end, s in pairs:
        alone[end, s] = times(weights_of(row_of(end, 0)), partial(end, term(0, end, s, 0), term(0, end, s, 1)))
        cross(1, end, s, alone[end, s])
    send(1)
    for s in range(SAMPLES):
        advance(1, s, 1, 3)
        advance(1, s, rows - 3, rows - 1)
    for end, s in pairs:
        t10, t11 = alone[end, s], term(1, end, s, 1)
        t20 = times(weights_of(row_of(end, 0)), partial(end, t10, t11))
        t21 = times(weights_of(row_of(end, 1)), partial(end, t11, term(1, end, s, 2), t10))
        alone[end, s] = t20, t21
        cross(2, end, s, t20)
    send(2)
    for end, s in pairs:
        cross(3, end, s, times(weights_of(row_of(end, 0)), partial(end, *alone[end, s])))
    send(3)

    def interior(s, carry):
        advance(1, s, 3, rows - 3)
        for t in range(2, ITERS + 1):
            advance(t, s, t, rows - t)
        return carry

    lax.fori_loop(0, SAMPLES, interior, 0)

    for c in lon_copies:
        c.wait_recv()
    beyond_edge = jnp.logical_or(place < 4, place >= 28)
    even_four = lax.bitwise_and(fours, 1) == 0
    block_before = lax.bitwise_and(lax.shift_right_logical(lane + 4, 5), 3)

    def woven(fw, fe, shift):
        fe = rolled(fe, shift)
        return jnp.where(even_four, fw, fe), jnp.where(even_four, fe, fw)

    for v in range(2):
        both = woven(lon_rx[0, v], lon_rx[1, v], 28)
        for j in range(8):
            e = w + 8 * v + j
            hx[0, e] = jnp.where(beyond_edge, rolled(both[j % 2], -4 * j), hx[0, e])
        both = woven(lon_rx[0, 2 + v], lon_rx[1, 2 + v], -4)
        for f in range(3):
            even = replicate(jnp.where(block_before == f, both[0], 0.0))
            odd = replicate(jnp.where(sample_of == f, both[1], 0.0))
            for j in range(8):
                e = w + 8 * v + j
                ha[1 + f, e] = jnp.where(beyond_edge, rolled((even, odd)[j % 2], -4 * j), ha[1 + f, e])
    for end, first in enumerate((0, w + rows)):

        @pl.when(present[end])
        def _(end=end):
            for side in range(2):
                diag_copies[1 - end][side].wait_recv()
            lat_copies[1 - end][ITERS + 1].wait_recv()

        dw, de = diag_rx[end, 0], diag_rx[end, 1]
        both = woven(dw, de, 28)
        for i in range(w):
            own = rolled(corner_rx[end, i // 2], -8 * (i % 2))
            hx[0, first + i] = jnp.where(beyond_edge, rolled(both[i % 2], -4 * i), own)
        both = woven(dw, de, -4)
        for f in range(3):
            mine = jnp.logical_and(sample_of == f, place >= 12)
            halves = [replicate(jnp.where(mine, u, 0.0)) for u in both]
            for n in range(w // 2):
                own = replicate(jnp.where(block_of == f, corner_rx[end, 2 + n], 0.0))
                for i in (2 * n, 2 * n + 1):
                    moved = rolled(halves[i % 2], -16 - 4 * i)
                    ha[1 + f, first + i] = jnp.where(beyond_edge, moved, rolled(own, -8 * (i % 2)))

    def centre(a1, a2):
        return jnp.where(a1 > 0.0, 1.0, 0.0) - 2.0 * (a1 + a2)

    for e in range(tall):
        ha[0, e] = centre(ha[1, e], ha[2, e])
    for t in range(1, ITERS + 1):

        def term(e):
            z = hx[t - 1, e]
            return [ha[f, e] * z for f in range(4)]

        above, here = term(t - 1), term(t)
        for e in range(t, tall - t):
            below = term(e + 1)
            q3 = above[3] - below[3]
            total = here[0] + (above[1] + below[1])
            total = total + pltpu.roll(here[2] + q3, 1, 1)
            hx[t, e] = total + pltpu.roll(here[2] - q3, LANES - 1, 1)
            above, here = here, below

    low_edge, high_edge = lane < 4, lane >= LANES - 4
    for r in range(rows):
        side = hx[ITERS, w + r]
        side = jnp.where(place < 4, rolled(side, -24), side)
        for s in range(SAMPLES):
            xs[s, r] = rolled(side, -32 * s - 4)

    def finish(s, r, value):
        value = [jnp.where(low_edge, xs[s, r], value[0]), jnp.where(high_edge, xs[s, r], value[1])]
        store(ITERS, s, r, value)
        return [u * u for u in value]

    def wet_sum(total, r, squares):
        for h in range(2):
            v = squares[h] * (1.0 / SAMPLES)
            var[r, h] = v
            total = total + jnp.where(a[1, r, h] > 0.0, v, 0.0)
        return total

    total_v, total_m = zero, zero
    for r in range(rows):
        for h in range(2):
            total_m = total_m + jnp.where(a[1, r, h] > 0.0, 1.0, 0.0)
    for r in range(w, rows - w):
        total_v = wet_sum(total_v, r, add(*[finish(s, r, state(ITERS, s, r)) for s in range(SAMPLES)]))

    def arrived(piece):
        for end in range(2):

            @pl.when(present[end])
            def _(end=end):
                lat_copies[1 - end][piece].wait_recv()

    def toward(end, local, outer, inner, known=None):
        above, below = (outer, inner) if end == 0 else (inner, outer)
        return combine(local, above, below, known)

    def known(n, end, s):
        return [edge_rx[end, n, s, 0], edge_rx[end, n, s, 1]]

    def near(end):
        return [[k_mid[end, 0], k_mid[end, 1]]] + [[k_rx[end, n, 0], k_rx[end, n, 1]] for n in range(3)]

    def far(end):
        return [None, [k_rx[end, 3, 0], k_rx[end, 3, 1]], None, [k_rx[end, 4, 0], k_rx[end, 4, 1]]]

    def keep(end, s, n, value):
        echo[end, s, n, 0], echo[end, s, n, 1] = value

    def kept(end, s, n):
        return [echo[end, s, n, 0], echo[end, s, n, 1]]

    def terms(t, end, s, count):
        return [times(weights_of(row_of(end, d)), state(t, s, row_of(end, d))) for d in range(count)]

    arrived(0)
    for end, s in pairs:
        t0 = terms(0, end, s, 2)
        keep(end, s, 0, toward(end, None, None, t0[0]))
        store(1, s, row_of(end, 0), toward(end, t0[0], None, t0[1], known(0, end, s)))
    arrived(ITERS)
    for end in range(2):
        for h in range(2):
            k_mid[end, h] = centre(k_rx[end, 0, h], k_rx[end, 1, h])
    arrived(1)
    for end, s in pairs:
        t1 = terms(1, end, s, 3)
        beyond = times(near(end), kept(end, s, 0))
        keep(end, s, 1, toward(end, None, None, beyond))
        keep(end, s, 0, toward(end, beyond, None, t1[0]))
        store(2, s, row_of(end, 0), toward(end, t1[0], beyond, t1[1], known(1, end, s)))
        store(2, s, row_of(end, 1), toward(end, t1[1], t1[0], t1[2]))
    arrived(2)
    for end, s in pairs:
        t2 = terms(2, end, s, 4)
        beyond = times(near(end), kept(end, s, 0))
        keep(end, s, 0, toward(end, beyond, times(far(end), kept(end, s, 1)), t2[0]))
        store(3, s, row_of(end, 0), toward(end, t2[0], beyond, t2[1], known(2, end, s)))
        for d in (1, 2):
            store(3, s, row_of(end, d), toward(end, t2[d], t2[d - 1], t2[d + 1]))
    squares = {}
    for end, s in pairs:
        t3 = terms(3, end, s, 5)
        beyond = times(near(end), kept(end, s, 0))
        store(ITERS, s, row_of(end, 0), toward(end, t3[0], beyond, t3[1]))
        for d in range(1, ITERS):
            r = row_of(end, d)
            squares.setdefault(r, []).append(finish(s, r, toward(end, t3[d], t3[d - 1], t3[d + 1])))
    for r in sorted(squares):
        total_v = wet_sum(total_v, r, add(*squares[r]))
    arrived(3)
    for end in range(2):
        r = row_of(end, 0)
        ends = [finish(s, r, add(state(ITERS, s, r), known(3, end, s))) for s in range(SAMPLES)]
        total_v = wet_sum(total_v, r, add(*ends))

    row = lax.broadcasted_iota(jnp.int32, (LEVELS, LANES), 0)
    mine = jnp.where(row == 0, jnp.sum(total_v, axis=0, keepdims=True), jnp.sum(total_m, axis=0, keepdims=True))

    def rank(masks):
        out = 0
        for bit, (ma, mb) in enumerate(masks):
            hit = lax.bitwise_and(ia, ma) + lax.bitwise_and(ib, mb)
            out = out + jnp.where(hit > 0, 1 << bit, 0)
        return out

    def sums(phase, mine):
        group = groups[phase]
        size = len(group)
        me = rank([group[1 << i] for i in range(size.bit_length() - 1)])
        part[phase, me] = mine
        copies = []
        for m in reversed(range(1, size)):
            ma, mb = group[m]
            pa, pb = lax.bitwise_xor(ia, ma), lax.bitwise_xor(ib, mb)
            slot = part.at[phase, me, pl.ds(0, 2)]
            copies.append(remote(slot, slot, sum_tx_sem.at[phase], sum_rx_sem.at[phase], pa, pb))
            copies[-1].start()

    def all_but_mine(phase):
        slots = part.at[phase, pl.ds(0, len(groups[phase]) - 1), pl.ds(0, 2)]
        return remote(slots, slots, sum_tx_sem.at[phase], sum_rx_sem.at[phase], ia, ib)

    def gather(phase):
        all_but_mine(phase).wait_recv()
        total = part[phase, 0, 0:2]
        for j in range(1, len(groups[phase])):
            total = total + part[phase, j, 0:2]
        return total

    sums(0, mine)
    for r in range(rows):
        for h in range(2):
            wet = jnp.where(a[1, r, h] > 0.0, 1.0, 0.0)
            var[r, h] = wet * lax.rsqrt(jnp.where(wet > 0.0, var[r, h], 1.0) + 1e-06)

    def scaled(s, carry):
        for r in range(rows):
            for h in range(2):
                out[s, h, pl.ds(r, LEVELS, stride=rows), :] = x[ITERS, s, r, h] * var[r, h]
        return carry

    lax.fori_loop(0, SAMPLES, scaled, 0)
    for c in lon_copies:
        c.wait_send()
    for end in range(2):

        @pl.when(present[end])
        def _(end=end):
            for c in diag_copies[end] + lat_copies[end]:
                c.wait_send()

    total = gather(0)
    sums(1, jnp.concatenate([total] * (LEVELS // 2), axis=0))
    for phase in range(2):
        all_but_mine(phase).wait_send()
    total = gather(1)
    both = jnp.sum(total, axis=1, keepdims=True)
    stat[...] = jnp.broadcast_to(both[0:1] / both[1:2], stat.shape)


def scale(field, stat, out, mean, buf, sem):
    copies = [pltpu.make_async_copy(stat, mean, sem.at[SAMPLES, 0])]
    copies[0].start()
    factor = jnp.sqrt(stat[...])
    for s in range(SAMPLES):
        for h in range(2):
            buf[s, h] = field[s, h] * factor
            copies.append(pltpu.make_async_copy(buf.at[s, h], out.at[s, :, pl.ds(h * LANES, LANES)], sem.at[s, h]))
            copies[-1].start()
    for c in copies:
        c.wait()


def bits_of(n):
    return [1 << i for i in range(n.bit_length() - 1)]


def span(masks):
    out = [(0, 0)]
    for ma, mb in masks:
        out += [(x + ma, z + mb) for x, z in out]
    return out


def shards(n_lat, n_lon, noise, diff_lat, diff_lon, shear, sea_mask):
    samples, levels, rows, cols = noise.shape
    lat_bits, lon_bits = bits_of(n_lat), bits_of(n_lon)
    groups = (
        span([(b, 0) for b in lat_bits[:1]] + [(0, b) for b in lon_bits[1:]]),
        span([(b, 0) for b in lat_bits[1:]] + [(0, b) for b in lon_bits[:1]]),
    )
    size = max(len(g) for g in groups)
    tall = rows + 2 * ITERS
    flat = levels * rows
    f32 = jnp.float32
    dma = pltpu.SemaphoreType.DMA
    hbm = pl.BlockSpec(memory_space=pltpu.HBM)
    vmem = pl.BlockSpec(memory_space=pltpu.VMEM)
    field, stat = pl.pallas_call(
        functools.partial(kernel, n_lat, n_lon, rows, groups),
        out_shape=(
            pltpu.VMEM((samples, 2, flat, LANES), f32),
            pltpu.VMEM((1, LANES), f32),
        ),
        in_specs=[hbm] * 5,
        out_specs=(vmem, vmem),
        scratch_shapes=[
            pltpu.VMEM((samples, 2, flat, LANES), f32),
            pltpu.VMEM((3, 2, flat, LANES), f32),
            pltpu.VMEM((2, flat, LANES), jnp.int32),
            pltpu.VMEM((ITERS + 1, samples, rows, 2, levels, LANES), f32),
            pltpu.VMEM((4, rows, 2, levels, LANES), f32),
            pltpu.VMEM((2, ITERS, samples, 2, levels, LANES), f32),
            pltpu.VMEM((2, ITERS, samples, 2, levels, LANES), f32),
            pltpu.VMEM((2, 5, 2, levels, LANES), f32),
            pltpu.VMEM((2, 5, 2, levels, LANES), f32),
            pltpu.VMEM((2, 2, levels, LANES), f32),
            pltpu.VMEM((2, samples, 2, 2, levels, LANES), f32),
            pltpu.VMEM((2, 4, levels, LANES), f32),
            pltpu.VMEM((2, 4, levels, LANES), f32),
            pltpu.VMEM((ITERS + 1, tall, levels, LANES), f32),
            pltpu.VMEM((4, tall, levels, LANES), f32),
            pltpu.VMEM((2, 4, levels, LANES), f32),
            pltpu.VMEM((2, 4, levels, LANES), f32),
            pltpu.VMEM((2, 2, levels, LANES), f32),
            pltpu.VMEM((2, 2, levels, LANES), f32),
            pltpu.VMEM((samples, rows, levels, LANES), f32),
            pltpu.VMEM((rows, 2, levels, LANES), f32),
            pltpu.VMEM((2, size, levels, LANES), f32),
            dma((8, 2)),
            dma((2, ITERS + 2)),
            dma((2, ITERS + 2)),
            dma((2,)),
            dma((2,)),
            dma((2, 2)),
            dma((2, 2)),
            dma((2,)),
            dma((2,)),
        ],
        compiler_params=pltpu.CompilerParams(
            collective_id=0, has_side_effects=True, vmem_limit_bytes=60 << 20
        ),
    )(
        noise.reshape(samples, flat, cols),
        diff_lat.reshape(flat, cols),
        diff_lon.reshape(flat, cols),
        shear.reshape(flat, cols),
        sea_mask.reshape(flat, cols),
    )
    out, mean_var = pl.pallas_call(
        scale,
        out_shape=(jax.ShapeDtypeStruct((samples, flat, cols), f32), jax.ShapeDtypeStruct((1, LANES), f32)),
        in_specs=[vmem, vmem],
        out_specs=(hbm, hbm),
        scratch_shapes=[pltpu.VMEM((samples, 2, flat, LANES), f32), dma((samples + 1, 2))],
        compiler_params=pltpu.CompilerParams(vmem_limit_bytes=8 << 20),
    )(pltpu.with_memory_space_constraint(field, pltpu.VMEM), pltpu.with_memory_space_constraint(stat, pltpu.VMEM))
    return out.reshape(noise.shape), mean_var[0, 0]


def solution(mesh):
    return jax.shard_map(
        functools.partial(shards, mesh.shape["lat"], mesh.shape["lon"]),
        mesh=mesh,
        in_specs=(
            P(None, None, "lat", "lon"),
            P(None, "lat", "lon"),
            P(None, "lat", "lon"),
            P(None, "lat", "lon"),
            P(None, "lat", "lon"),
        ),
        out_specs=(P(None, None, "lat", "lon"), P()),
        check_vma=False,
    )
```

```python
import functools

import jax
import jax.numpy as jnp
from jax import lax
from jax.experimental import pallas as pl
from jax.experimental.pallas import tpu as pltpu
from jax.sharding import PartitionSpec as P

SAMPLES = 4
LEVELS = 8
ITERS = 4
LANES = 128
MESH = pl.DeviceIdType.MESH


def kernel(
    n_lat, n_lon, rows, groups,
    noise, k_lat, k_lon, shear, sea,
    out, stat,
    raw, raw_k, raw_m, x, a, edge_tx, edge_rx, k_tx, k_rx, k_mid, echo, corner_tx, corner_rx, hx, ha, lon_tx, lon_rx, diag_tx, diag_rx, xs, var, part,
    in_sem, lat_tx_sem, lat_rx_sem, lon_tx_sem, lon_rx_sem, diag_tx_sem, diag_rx_sem, sum_tx_sem, sum_rx_sem,
):
    w = ITERS
    tall = rows + 2 * w
    ia, ib = lax.axis_index("lat"), lax.axis_index("lon")
    east, west = lax.rem(ib + 1, n_lon), lax.rem(ib + n_lon - 1, n_lon)
    has_north, has_south = ia > 0, ia < n_lat - 1
    present = (has_north, has_south)
    pa_of = (ia - 1, ia + 1)
    lane = lax.broadcasted_iota(jnp.int32, (LEVELS, LANES), 1)
    zero = jnp.zeros((LEVELS, LANES), jnp.float32)

    def half(h):
        return pl.ds(h * LANES, LANES)

    loads = []
    for f, src in enumerate((k_lat, k_lon, shear)):
        for h in range(2):
            loads.append(pltpu.make_async_copy(src.at[:, half(h)], raw_k.at[f, h], in_sem.at[f, h]))
    for h in range(2):
        loads.append(pltpu.make_async_copy(sea.at[:, half(h)], raw_m.at[h], in_sem.at[3, h]))
    for s in range(SAMPLES):
        for h in range(2):
            loads.append(pltpu.make_async_copy(noise.at[s, :, half(h)], raw.at[s, h], in_sem.at[4 + s, h]))

    barrier = pltpu.get_barrier_semaphore()

    def greet(pa, pb):
        pl.semaphore_signal(barrier, inc=1, device_id=(pa, pb), device_id_type=MESH)

    for end in range(2):

        @pl.when(present[end])
        def _(end=end):
            for pb in (west, east, ib):
                greet(pa_of[end], pb)

    greet(ia, west)
    greet(ia, east)
    for c in loads:
        c.start()
    for group in groups:
        for ma, mb in reversed(group[1:]):
            greet(lax.bitwise_xor(ia, ma), lax.bitwise_xor(ib, mb))

    for c in loads[:8]:
        c.wait()
    for r in range(rows):
        for h in range(2):
            at = pl.ds(r, LEVELS, stride=rows)
            m = raw_m[h, at, :].astype(jnp.float32)
            k11 = raw_k[0, h, at, :]
            k22 = raw_k[1, h, at, :]
            a1 = m * k11
            a2 = m * k22
            a[1, r, h] = a1
            a[2, r, h] = a2
            a[3, r, h] = (0.5 * m) * (raw_k[2, h, at, :] * jnp.sqrt(k11 * k22))
            a[0, r, h] = m - 2.0 * (a1 + a2)

    place = lax.bitwise_and(lane, 31)
    sample_of = lax.shift_right_logical(lane, 5)
    low_own = jnp.logical_and(place >= 4, place < 16)
    high_own = jnp.logical_and(place >= 16, place < 28)

    def rolled(value, shift):
        shift %= LANES
        return pltpu.roll(value, shift, 1) if shift else value

    def replicate(value):
        value = value + pltpu.roll(value, 32, 1)
        return value + pltpu.roll(value, 64, 1)

    for f in range(1, 4):
        for r in range(rows):
            low = jnp.where(jnp.logical_and(low_own, lane < 32), rolled(a[f, r, 0], 4), 0.0)
            high = jnp.where(jnp.logical_and(high_own, lane < 32), rolled(a[f, r, 1], 28), low)
            ha[f, w + r] = replicate(high)

    for c in loads[8:]:
        c.wait()
    for s in range(SAMPLES):
        for r in range(rows):
            for h in range(2):
                x[0, s, r, h] = raw[s, h, pl.ds(r, LEVELS, stride=rows), :]
    for r in range(rows):
        side = zero
        for s in range(SAMPLES):
            mine = sample_of == s
            side = jnp.where(jnp.logical_and(low_own, mine), rolled(x[0, s, r, 0], 32 * s + 4), side)
            side = jnp.where(jnp.logical_and(high_own, mine), rolled(x[0, s, r, 1], 32 * s + 28), side)
        hx[0, w + r] = side

    offset = (24, 4)
    fours = lax.shift_right_logical(lane, 2)
    in_sample = lax.bitwise_and(fours, 7)
    for side in range(2):
        for v in range(2):
            packed, packed_k = zero, zero
            for j in range(8):
                e = w + 8 * v + j
                packed = jnp.where(in_sample == j, rolled(hx[0, e], 4 * j - offset[side]), packed)
                for f in range(3):
                    packed_k = jnp.where(fours == 8 * f + j, rolled(ha[1 + f, e], 4 * j - offset[side]), packed_k)
            lon_tx[side, v] = packed
            lon_tx[side, 2 + v] = packed_k
        for end, first in enumerate((w, rows)):
            packed = zero
            for i in range(w):
                e = first + i
                packed = jnp.where(in_sample == i, rolled(hx[0, e], 4 * i - offset[side]), packed)
                for f in range(3):
                    packed = jnp.where(fours == 8 * f + 4 + i, rolled(ha[1 + f, e], 16 + 4 * i - offset[side]), packed)
            diag_tx[end, side] = packed

    first_of_two = lax.bitwise_and(lane + 4, 8) != 0
    block_of = lax.bitwise_and(lax.shift_right_logical(lane + LANES - 4, 5), 3)
    for end, first in enumerate((w, rows)):
        for n in range(w // 2):
            e = first + 2 * n
            corner_tx[end, n] = jnp.where(first_of_two, hx[0, e], rolled(hx[0, e + 1], 8))
            packed = zero
            for f in range(3):
                two = jnp.where(first_of_two, ha[1 + f, e], rolled(ha[1 + f, e + 1], 8))
                packed = jnp.where(block_of == f, two, packed)
            corner_tx[end, 2 + n] = packed

    first_lane, last_lane = lane == 0, lane == LANES - 1

    def left(u):
        r0, r1 = pltpu.roll(u[0], 1, 1), pltpu.roll(u[1], 1, 1)
        return [r0, jnp.where(first_lane, r0, r1)]

    def right(u):
        r0, r1 = pltpu.roll(u[0], LANES - 1, 1), pltpu.roll(u[1], LANES - 1, 1)
        return [jnp.where(last_lane, r1, r0), r1]

    def add(*lists):
        lists = [u for u in lists if u is not None]
        total = lists[0]
        for u in lists[1:]:
            total = [p + q for p, q in zip(total, u)]
        return total

    def sub(u, v):
        return [p - q for p, q in zip(u, v)]

    def times(weights, z):
        return [[p * q for p, q in zip(k, z)] if k is not None else None for k in weights]

    def combine(local, above, below, known=None):
        base = add(*[u for u in (known, local and local[0], above and above[1], below and below[1]) if u is not None])
        q3 = sub(above[3], below[3]) if above and below else None
        if local and q3:
            u, v = add(local[2], q3), sub(local[2], q3)
        elif local and above:
            u, v = add(local[2], above[3]), sub(local[2], above[3])
        elif local:
            u, v = sub(local[2], below[3]), add(local[2], below[3])
        elif above:
            return add(base, sub(left(above[3]), right(above[3])))
        else:
            return add(base, sub(right(below[3]), left(below[3])))
        return add(base, add(left(u), right(v)))

    def weights_of(r):
        return [[a[f, r, 0], a[f, r, 1]] for f in range(4)]

    def state(t, s, r):
        return [x[t, s, r, 0], x[t, s, r, 1]]

    def store(t, s, r, value):
        x[t, s, r, 0] = value[0]
        x[t, s, r, 1] = value[1]

    def advance(t, s, first, last):
        def term(r):
            return times(weights_of(r), state(t - 1, s, r))

        above, here = term(first - 1), term(first)
        for r in range(first, last):
            below = term(r + 1)
            store(t, s, r, combine(here, above, below))
            above, here = here, below

    for end in range(2):
        rows_in = (0, 1) if end == 0 else (rows - 1, rows - 2)
        for n, (f, d) in enumerate(((1, 0), (2, 0), (3, 0), (1, 1), (3, 1))):
            for h in range(2):
                k_tx[end, n, h] = a[f, rows_in[d], h]

    pairs = [(end, s) for s in range(SAMPLES) for end in range(2)]

    def row_of(end, d):
        return d if end == 0 else rows - 1 - d

    def term(t, end, s, d):
        return times(weights_of(row_of(end, d)), state(t, s, row_of(end, d)))

    def cross(n, end, s, local):
        value = combine(None, None, local) if end == 0 else combine(None, local, None)
        for h in range(2):
            edge_tx[end, n, s, h] = value[h]

    def partial(end, local, inner, outer=None):
        return combine(local, outer, inner) if end == 0 else combine(local, inner, outer)

    for end, s in pairs:
        cross(0, end, s, term(0, end, s, 0))

    for end in range(2):

        @pl.when(jnp.logical_not(present[end]))
        def _(end=end):
            for h in range(2):
                for n in range(5):
                    k_rx[end, n, h] = zero
                for s in range(SAMPLES):
                    for n in range(w):
                        edge_rx[end, n, s, h] = zero
            for side in range(2):
                diag_rx[end, side] = zero
            for n in range(4):
                corner_rx[end, n] = zero

    n_sum = sum(len(group) - 1 for group in groups)
    pl.semaphore_wait(barrier, 2 + n_sum + 3 * has_north.astype(jnp.int32) + 3 * has_south.astype(jnp.int32))

    def remote(src, dst, tx, rx, pa, pb):
        return pltpu.make_async_remote_copy(
            src_ref=src, dst_ref=dst, send_sem=tx, recv_sem=rx, device_id=(pa, pb), device_id_type=MESH
        )

    lon_copies = [
        remote(lon_tx.at[side], lon_rx.at[side], lon_tx_sem.at[side], lon_rx_sem.at[side], ia, (east, west)[side])
        for side in range(2)
    ]
    diag_copies = [
        [
            remote(diag_tx.at[end, side], diag_rx.at[1 - end, side], diag_tx_sem.at[end, side], diag_rx_sem.at[1 - end, side], pa_of[end], (east, west)[side])
            for side in range(2)
        ]
        for end in range(2)
    ]

    def lat_copy(end, piece):
        tx, rx = lat_tx_sem.at[end, piece], lat_rx_sem.at[1 - end, piece]
        if piece == ITERS:
            return remote(k_tx.at[end], k_rx.at[1 - end], tx, rx, pa_of[end], ib)
        if piece == ITERS + 1:
            return remote(corner_tx.at[end], corner_rx.at[1 - end], tx, rx, pa_of[end], ib)
        return remote(edge_tx.at[end, piece], edge_rx.at[1 - end, piece], tx, rx, pa_of[end], ib)

    lat_copies = [[lat_copy(end, piece) for piece in range(ITERS + 2)] for end in range(2)]

    for end in range(2):

        @pl.when(present[end])
        def _(end=end):
            for c in diag_copies[end]:
                c.start()

    for c in lon_copies:
        c.start()
    def send(piece):
        for end in range(2):

            @pl.when(present[end])
            def _(end=end):
                lat_copies[end][piece].start()

    send(ITERS + 1)
    send(0)
    send(ITERS)
    alone = {}
    for end, s in pairs:
        alone[end, s] = times(weights_of(row_of(end, 0)), partial(end, term(0, end, s, 0), term(0, end, s, 1)))
        cross(1, end, s, alone[end, s])
    send(1)
    for s in range(SAMPLES):
        advance(1, s, 1, 3)
        advance(1, s, rows - 3, rows - 1)
    for end, s in pairs:
        t10, t11 = alone[end, s], term(1, end, s, 1)
        t20 = times(weights_of(row_of(end, 0)), partial(end, t10, t11))
        t21 = times(weights_of(row_of(end, 1)), partial(end, t11, term(1, end, s, 2), t10))
        alone[end, s] = t20, t21
        cross(2, end, s, t20)
    send(2)
    for end, s in pairs:
        cross(3, end, s, times(weights_of(row_of(end, 0)), partial(end, *alone[end, s])))
    send(3)

    def interior(s, carry):
        advance(1, s, 3, rows - 3)
        for t in range(2, ITERS + 1):
            advance(t, s, t, rows - t)
        return carry

    lax.fori_loop(0, SAMPLES, interior, 0)

    for c in lon_copies:
        c.wait_recv()
    beyond_edge = jnp.logical_or(place < 4, place >= 28)
    even_four = lax.bitwise_and(fours, 1) == 0
    block_before = lax.bitwise_and(lax.shift_right_logical(lane + 4, 5), 3)

    def woven(fw, fe, shift):
        fe = rolled(fe, shift)
        return jnp.where(even_four, fw, fe), jnp.where(even_four, fe, fw)

    for v in range(2):
        both = woven(lon_rx[0, v], lon_rx[1, v], 28)
        for j in range(8):
            e = w + 8 * v + j
            hx[0, e] = jnp.where(beyond_edge, rolled(both[j % 2], -4 * j), hx[0, e])
        both = woven(lon_rx[0, 2 + v], lon_rx[1, 2 + v], -4)
        for f in range(3):
            even = replicate(jnp.where(block_before == f, both[0], 0.0))
            odd = replicate(jnp.where(sample_of == f, both[1], 0.0))
            for j in range(8):
                e = w + 8 * v + j
                ha[1 + f, e] = jnp.where(beyond_edge, rolled((even, odd)[j % 2], -4 * j), ha[1 + f, e])
    for end, first in enumerate((0, w + rows)):

        @pl.when(present[end])
        def _(end=end):
            for side in range(2):
                diag_copies[1 - end][side].wait_recv()
            lat_copies[1 - end][ITERS + 1].wait_recv()

        dw, de = diag_rx[end, 0], diag_rx[end, 1]
        both = woven(dw, de, 28)
        for i in range(w):
            own = rolled(corner_rx[end, i // 2], -8 * (i % 2))
            hx[0, first + i] = jnp.where(beyond_edge, rolled(both[i % 2], -4 * i), own)
        both = woven(dw, de, -4)
        for f in range(3):
            mine = jnp.logical_and(sample_of == f, place >= 12)
            halves = [replicate(jnp.where(mine, u, 0.0)) for u in both]
            for n in range(w // 2):
                own = replicate(jnp.where(block_of == f, corner_rx[end, 2 + n], 0.0))
                for i in (2 * n, 2 * n + 1):
                    moved = rolled(halves[i % 2], -16 - 4 * i)
                    ha[1 + f, first + i] = jnp.where(beyond_edge, moved, rolled(own, -8 * (i % 2)))

    def centre(a1, a2):
        return jnp.where(a1 > 0.0, 1.0, 0.0) - 2.0 * (a1 + a2)

    for e in range(tall):
        ha[0, e] = centre(ha[1, e], ha[2, e])
    for t in range(1, ITERS + 1):

        def term(e):
            z = hx[t - 1, e]
            return [ha[f, e] * z for f in range(4)]

        above, here = term(t - 1), term(t)
        for e in range(t, tall - t):
            below = term(e + 1)
            q3 = above[3] - below[3]
            total = here[0] + (above[1] + below[1])
            total = total + pltpu.roll(here[2] + q3, 1, 1)
            hx[t, e] = total + pltpu.roll(here[2] - q3, LANES - 1, 1)
            above, here = here, below

    low_edge, high_edge = lane < 4, lane >= LANES - 4
    for r in range(rows):
        side = hx[ITERS, w + r]
        side = jnp.where(place < 4, rolled(side, -24), side)
        for s in range(SAMPLES):
            xs[s, r] = rolled(side, -32 * s - 4)

    def finish(s, r, value):
        value = [jnp.where(low_edge, xs[s, r], value[0]), jnp.where(high_edge, xs[s, r], value[1])]
        store(ITERS, s, r, value)
        return [u * u for u in value]

    def wet_sum(total, r, squares):
        for h in range(2):
            v = squares[h] * (1.0 / SAMPLES)
            var[r, h] = v
            total = total + jnp.where(a[1, r, h] > 0.0, v, 0.0)
        return total

    total_v, total_m = zero, zero
    for r in range(rows):
        for h in range(2):
            total_m = total_m + jnp.where(a[1, r, h] > 0.0, 1.0, 0.0)
    for r in range(w, rows - w):
        total_v = wet_sum(total_v, r, add(*[finish(s, r, state(ITERS, s, r)) for s in range(SAMPLES)]))

    def arrived(piece):
        for end in range(2):

            @pl.when(present[end])
            def _(end=end):
                lat_copies[1 - end][piece].wait_recv()

    def toward(end, local, outer, inner, known=None):
        above, below = (outer, inner) if end == 0 else (inner, outer)
        return combine(local, above, below, known)

    def known(n, end, s):
        return [edge_rx[end, n, s, 0], edge_rx[end, n, s, 1]]

    def near(end):
        return [[k_mid[end, 0], k_mid[end, 1]]] + [[k_rx[end, n, 0], k_rx[end, n, 1]] for n in range(3)]

    def far(end):
        return [None, [k_rx[end, 3, 0], k_rx[end, 3, 1]], None, [k_rx[end, 4, 0], k_rx[end, 4, 1]]]

    def keep(end, s, n, value):
        echo[end, s, n, 0], echo[end, s, n, 1] = value

    def kept(end, s, n):
        return [echo[end, s, n, 0], echo[end, s, n, 1]]

    def terms(t, end, s, count):
        return [times(weights_of(row_of(end, d)), state(t, s, row_of(end, d))) for d in range(count)]

    arrived(0)
    for end, s in pairs:
        t0 = terms(0, end, s, 2)
        keep(end, s, 0, toward(end, None, None, t0[0]))
        store(1, s, row_of(end, 0), toward(end, t0[0], None, t0[1], known(0, end, s)))
    arrived(ITERS)
    for end in range(2):
        for h in range(2):
            k_mid[end, h] = centre(k_rx[end, 0, h], k_rx[end, 1, h])
    arrived(1)
    for end, s in pairs:
        t1 = terms(1, end, s, 3)
        beyond = times(near(end), kept(end, s, 0))
        keep(end, s, 1, toward(end, None, None, beyond))
        keep(end, s, 0, toward(end, beyond, None, t1[0]))
        store(2, s, row_of(end, 0), toward(end, t1[0], beyond, t1[1], known(1, end, s)))
        store(2, s, row_of(end, 1), toward(end, t1[1], t1[0], t1[2]))
    arrived(2)
    for end, s in pairs:
        t2 = terms(2, end, s, 4)
        beyond = times(near(end), kept(end, s, 0))
        keep(end, s, 0, toward(end, beyond, times(far(end), kept(end, s, 1)), t2[0]))
        store(3, s, row_of(end, 0), toward(end, t2[0], beyond, t2[1], known(2, end, s)))
        for d in (1, 2):
            store(3, s, row_of(end, d), toward(end, t2[d], t2[d - 1], t2[d + 1]))
    squares = {}
    for end, s in pairs:
        t3 = terms(3, end, s, 5)
        beyond = times(near(end), kept(end, s, 0))
        store(ITERS, s, row_of(end, 0), toward(end, t3[0], beyond, t3[1]))
        for d in range(1, ITERS):
            r = row_of(end, d)
            squares.setdefault(r, []).append(finish(s, r, toward(end, t3[d], t3[d - 1], t3[d + 1])))
    for r in sorted(squares):
        total_v = wet_sum(total_v, r, add(*squares[r]))
    arrived(3)
    for end in range(2):
        r = row_of(end, 0)
        ends = [finish(s, r, add(state(ITERS, s, r), known(3, end, s))) for s in range(SAMPLES)]
        total_v = wet_sum(total_v, r, add(*ends))

    row = lax.broadcasted_iota(jnp.int32, (LEVELS, LANES), 0)
    mine = jnp.where(row == 0, jnp.sum(total_v, axis=0, keepdims=True), jnp.sum(total_m, axis=0, keepdims=True))

    def rank(masks):
        out = 0
        for bit, (ma, mb) in enumerate(masks):
            hit = lax.bitwise_and(ia, ma) + lax.bitwise_and(ib, mb)
            out = out + jnp.where(hit > 0, 1 << bit, 0)
        return out

    def sums(phase, mine):
        group = groups[phase]
        size = len(group)
        me = rank([group[1 << i] for i in range(size.bit_length() - 1)])
        part[phase, me] = mine
        copies = []
        for m in reversed(range(1, size)):
            ma, mb = group[m]
            pa, pb = lax.bitwise_xor(ia, ma), lax.bitwise_xor(ib, mb)
            slot = part.at[phase, me, pl.ds(0, 2)]
            copies.append(remote(slot, slot, sum_tx_sem.at[phase], sum_rx_sem.at[phase], pa, pb))
            copies[-1].start()

    def all_but_mine(phase):
        slots = part.at[phase, pl.ds(0, len(groups[phase]) - 1), pl.ds(0, 2)]
        return remote(slots, slots, sum_tx_sem.at[phase], sum_rx_sem.at[phase], ia, ib)

    def gather(phase):
        all_but_mine(phase).wait_recv()
        total = part[phase, 0, 0:2]
        for j in range(1, len(groups[phase])):
            total = total + part[phase, j, 0:2]
        return total

    sums(0, mine)
    for r in range(rows):
        for h in range(2):
            wet = jnp.where(a[1, r, h] > 0.0, 1.0, 0.0)
            var[r, h] = wet * lax.rsqrt(jnp.where(wet > 0.0, var[r, h], 1.0) + 1e-06)

    def scaled(s, carry):
        for r in range(rows):
            for h in range(2):
                out[s, h, pl.ds(r, LEVELS, stride=rows), :] = x[ITERS, s, r, h] * var[r, h]
        return carry

    lax.fori_loop(0, SAMPLES, scaled, 0)
    for c in lon_copies:
        c.wait_send()
    for end in range(2):

        @pl.when(present[end])
        def _(end=end):
            for c in diag_copies[end] + lat_copies[end]:
                c.wait_send()

    total = gather(0)
    sums(1, jnp.concatenate([total] * (LEVELS // 2), axis=0))
    for phase in range(2):
        all_but_mine(phase).wait_send()
    total = gather(1)
    both = jnp.sum(total, axis=1, keepdims=True)
    stat[...] = jnp.broadcast_to(both[0:1] / both[1:2], stat.shape)


def scale(field, stat, out, mean, buf, sem):
    copies = [pltpu.make_async_copy(stat, mean, sem.at[SAMPLES, 0])]
    copies[0].start()
    factor = jnp.sqrt(stat[...])
    for s in range(SAMPLES):
        for h in range(2):
            buf[s, h] = field[s, h] * factor
            copies.append(pltpu.make_async_copy(buf.at[s, h], out.at[s, :, pl.ds(h * LANES, LANES)], sem.at[s, h]))
            copies[-1].start()
    for c in copies:
        c.wait()


def bits_of(n):
    return [1 << i for i in range(n.bit_length() - 1)]


def span(masks):
    out = [(0, 0)]
    for ma, mb in masks:
        out += [(x + ma, z + mb) for x, z in out]
    return out


def shards(n_lat, n_lon, noise, diff_lat, diff_lon, shear, sea_mask):
    samples, levels, rows, cols = noise.shape
    lat_bits, lon_bits = bits_of(n_lat), bits_of(n_lon)
    groups = (
        span([(b, 0) for b in lat_bits[:1]] + [(0, b) for b in lon_bits[1:]]),
        span([(b, 0) for b in lat_bits[1:]] + [(0, b) for b in lon_bits[:1]]),
    )
    size = max(len(g) for g in groups)
    tall = rows + 2 * ITERS
    flat = levels * rows
    f32 = jnp.float32
    dma = pltpu.SemaphoreType.DMA
    hbm = pl.BlockSpec(memory_space=pltpu.HBM)
    vmem = pl.BlockSpec(memory_space=pltpu.VMEM)
    field, stat = pl.pallas_call(
        functools.partial(kernel, n_lat, n_lon, rows, groups),
        out_shape=(
            pltpu.VMEM((samples, 2, flat, LANES), f32),
            pltpu.VMEM((1, LANES), f32),
        ),
        in_specs=[hbm] * 5,
        out_specs=(vmem, vmem),
        scratch_shapes=[
            pltpu.VMEM((samples, 2, flat, LANES), f32),
            pltpu.VMEM((3, 2, flat, LANES), f32),
            pltpu.VMEM((2, flat, LANES), jnp.int32),
            pltpu.VMEM((ITERS + 1, samples, rows, 2, levels, LANES), f32),
            pltpu.VMEM((4, rows, 2, levels, LANES), f32),
            pltpu.VMEM((2, ITERS, samples, 2, levels, LANES), f32),
            pltpu.VMEM((2, ITERS, samples, 2, levels, LANES), f32),
            pltpu.VMEM((2, 5, 2, levels, LANES), f32),
            pltpu.VMEM((2, 5, 2, levels, LANES), f32),
            pltpu.VMEM((2, 2, levels, LANES), f32),
            pltpu.VMEM((2, samples, 2, 2, levels, LANES), f32),
            pltpu.VMEM((2, 4, levels, LANES), f32),
            pltpu.VMEM((2, 4, levels, LANES), f32),
            pltpu.VMEM((ITERS + 1, tall, levels, LANES), f32),
            pltpu.VMEM((4, tall, levels, LANES), f32),
            pltpu.VMEM((2, 4, levels, LANES), f32),
            pltpu.VMEM((2, 4, levels, LANES), f32),
            pltpu.VMEM((2, 2, levels, LANES), f32),
            pltpu.VMEM((2, 2, levels, LANES), f32),
            pltpu.VMEM((samples, rows, levels, LANES), f32),
            pltpu.VMEM((rows, 2, levels, LANES), f32),
            pltpu.VMEM((2, size, levels, LANES), f32),
            dma((8, 2)),
            dma((2, ITERS + 2)),
            dma((2, ITERS + 2)),
            dma((2,)),
            dma((2,)),
            dma((2, 2)),
            dma((2, 2)),
            dma((2,)),
            dma((2,)),
        ],
        compiler_params=pltpu.CompilerParams(
            collective_id=0, has_side_effects=True, vmem_limit_bytes=60 << 20
        ),
    )(
        noise.reshape(samples, flat, cols),
        diff_lat.reshape(flat, cols),
        diff_lon.reshape(flat, cols),
        shear.reshape(flat, cols),
        sea_mask.reshape(flat, cols),
    )
    out, mean_var = pl.pallas_call(
        scale,
        out_shape=(jax.ShapeDtypeStruct((samples, flat, cols), f32), jax.ShapeDtypeStruct((1, LANES), f32)),
        in_specs=[vmem, vmem],
        out_specs=(hbm, hbm),
        scratch_shapes=[pltpu.VMEM((samples, 2, flat, LANES), f32), dma((samples + 1, 2))],
        compiler_params=pltpu.CompilerParams(vmem_limit_bytes=8 << 20),
    )(pltpu.with_memory_space_constraint(field, pltpu.VMEM), pltpu.with_memory_space_constraint(stat, pltpu.VMEM))
    return out.reshape(noise.shape), mean_var[0, 0]


def solution(mesh):
    return jax.shard_map(
        functools.partial(shards, mesh.shape["lat"], mesh.shape["lon"]),
        mesh=mesh,
        in_specs=(
            P(None, None, "lat", "lon"),
            P(None, "lat", "lon"),
            P(None, "lat", "lon"),
            P(None, "lat", "lon"),
            P(None, "lat", "lon"),
        ),
        out_specs=(P(None, None, "lat", "lon"), P()),
        check_vma=False,
    )
```

```python
import functools

import jax
import jax.numpy as jnp
from jax import lax
from jax.experimental import pallas as pl
from jax.experimental.pallas import tpu as pltpu
from jax.sharding import PartitionSpec as P

SAMPLES = 4
LEVELS = 8
ITERS = 4
LANES = 128
MESH = pl.DeviceIdType.MESH


def kernel(
    n_lat, n_lon, rows, groups,
    noise, k_lat, k_lon, shear, sea,
    out, stat,
    raw, raw_k, raw_m, x, a, edge_tx, edge_rx, k_tx, k_rx, k_mid, echo, corner_tx, corner_rx, hx, ha, lon_tx, lon_rx, diag_tx, diag_rx, xs, var, part,
    in_sem, lat_tx_sem, lat_rx_sem, lon_tx_sem, lon_rx_sem, diag_tx_sem, diag_rx_sem, sum_tx_sem, sum_rx_sem,
):
    w = ITERS
    tall = rows + 2 * w
    ia, ib = lax.axis_index("lat"), lax.axis_index("lon")
    east, west = lax.rem(ib + 1, n_lon), lax.rem(ib + n_lon - 1, n_lon)
    has_north, has_south = ia > 0, ia < n_lat - 1
    present = (has_north, has_south)
    pa_of = (ia - 1, ia + 1)
    lane = lax.broadcasted_iota(jnp.int32, (LEVELS, LANES), 1)
    zero = jnp.zeros((LEVELS, LANES), jnp.float32)

    def half(h):
        return pl.ds(h * LANES, LANES)

    loads = []
    for f, src in enumerate((k_lat, k_lon, shear)):
        for h in range(2):
            loads.append(pltpu.make_async_copy(src.at[:, half(h)], raw_k.at[f, h], in_sem.at[f, h]))
    for h in range(2):
        loads.append(pltpu.make_async_copy(sea.at[:, half(h)], raw_m.at[h], in_sem.at[3, h]))
    for s in range(SAMPLES):
        for h in range(2):
            loads.append(pltpu.make_async_copy(noise.at[s, :, half(h)], raw.at[s, h], in_sem.at[4 + s, h]))

    barrier = pltpu.get_barrier_semaphore()

    def greet(pa, pb):
        pl.semaphore_signal(barrier, inc=1, device_id=(pa, pb), device_id_type=MESH)

    for end in range(2):

        @pl.when(present[end])
        def _(end=end):
            for pb in (west, east, ib):
                greet(pa_of[end], pb)

    greet(ia, west)
    greet(ia, east)
    for c in loads:
        c.start()
    for group in groups:
        for _, (ma, mb) in far_first(group):
            greet(lax.bitwise_xor(ia, ma), lax.bitwise_xor(ib, mb))

    for c in loads[:8]:
        c.wait()
    for r in range(rows):
        for h in range(2):
            at = pl.ds(r, LEVELS, stride=rows)
            m = raw_m[h, at, :].astype(jnp.float32)
            k11 = raw_k[0, h, at, :]
            k22 = raw_k[1, h, at, :]
            a1 = m * k11
            a2 = m * k22
            a[1, r, h] = a1
            a[2, r, h] = a2
            a[3, r, h] = (0.5 * m) * (raw_k[2, h, at, :] * jnp.sqrt(k11 * k22))
            a[0, r, h] = m - 2.0 * (a1 + a2)

    place = lax.bitwise_and(lane, 31)
    sample_of = lax.shift_right_logical(lane, 5)
    low_own = jnp.logical_and(place >= 4, place < 16)
    high_own = jnp.logical_and(place >= 16, place < 28)

    def rolled(value, shift):
        shift %= LANES
        return pltpu.roll(value, shift, 1) if shift else value

    def replicate(value):
        value = value + pltpu.roll(value, 32, 1)
        return value + pltpu.roll(value, 64, 1)

    for f in range(1, 4):
        for r in range(rows):
            low = jnp.where(jnp.logical_and(low_own, lane < 32), rolled(a[f, r, 0], 4), 0.0)
            high = jnp.where(jnp.logical_and(high_own, lane < 32), rolled(a[f, r, 1], 28), low)
            ha[f, w + r] = replicate(high)

    for c in loads[8:]:
        c.wait()
    for s in range(SAMPLES):
        for r in range(rows):
            for h in range(2):
                x[0, s, r, h] = raw[s, h, pl.ds(r, LEVELS, stride=rows), :]
    for r in range(rows):
        side = zero
        for s in range(SAMPLES):
            mine = sample_of == s
            side = jnp.where(jnp.logical_and(low_own, mine), rolled(x[0, s, r, 0], 32 * s + 4), side)
            side = jnp.where(jnp.logical_and(high_own, mine), rolled(x[0, s, r, 1], 32 * s + 28), side)
        hx[0, w + r] = side

    offset = (24, 4)
    fours = lax.shift_right_logical(lane, 2)
    in_sample = lax.bitwise_and(fours, 7)
    for side in range(2):
        for v in range(2):
            packed, packed_k = zero, zero
            for j in range(8):
                e = w + 8 * v + j
                packed = jnp.where(in_sample == j, rolled(hx[0, e], 4 * j - offset[side]), packed)
                for f in range(3):
                    packed_k = jnp.where(fours == 8 * f + j, rolled(ha[1 + f, e], 4 * j - offset[side]), packed_k)
            lon_tx[side, v] = packed
            lon_tx[side, 2 + v] = packed_k
        for end, first in enumerate((w, rows)):
            packed = zero
            for i in range(w):
                e = first + i
                packed = jnp.where(in_sample == i, rolled(hx[0, e], 4 * i - offset[side]), packed)
                for f in range(3):
                    packed = jnp.where(fours == 8 * f + 4 + i, rolled(ha[1 + f, e], 16 + 4 * i - offset[side]), packed)
            diag_tx[end, side] = packed

    first_of_two = lax.bitwise_and(lane + 4, 8) != 0
    block_of = lax.bitwise_and(lax.shift_right_logical(lane + LANES - 4, 5), 3)
    for end, first in enumerate((w, rows)):
        for n in range(w // 2):
            e = first + 2 * n
            corner_tx[end, n] = jnp.where(first_of_two, hx[0, e], rolled(hx[0, e + 1], 8))
            packed = zero
            for f in range(3):
                two = jnp.where(first_of_two, ha[1 + f, e], rolled(ha[1 + f, e + 1], 8))
                packed = jnp.where(block_of == f, two, packed)
            corner_tx[end, 2 + n] = packed

    first_lane, last_lane = lane == 0, lane == LANES - 1

    def left(u):
        r0, r1 = pltpu.roll(u[0], 1, 1), pltpu.roll(u[1], 1, 1)
        return [r0, jnp.where(first_lane, r0, r1)]

    def right(u):
        r0, r1 = pltpu.roll(u[0], LANES - 1, 1), pltpu.roll(u[1], LANES - 1, 1)
        return [jnp.where(last_lane, r1, r0), r1]

    def add(*lists):
        lists = [u for u in lists if u is not None]
        total = lists[0]
        for u in lists[1:]:
            total = [p + q for p, q in zip(total, u)]
        return total

    def sub(u, v):
        return [p - q for p, q in zip(u, v)]

    def times(weights, z):
        return [[p * q for p, q in zip(k, z)] if k is not None else None for k in weights]

    def combine(local, above, below, known=None):
        base = add(*[u for u in (known, local and local[0], above and above[1], below and below[1]) if u is not None])
        q3 = sub(above[3], below[3]) if above and below else None
        if local and q3:
            u, v = add(local[2], q3), sub(local[2], q3)
        elif local and above:
            u, v = add(local[2], above[3]), sub(local[2], above[3])
        elif local:
            u, v = sub(local[2], below[3]), add(local[2], below[3])
        elif above:
            return add(base, sub(left(above[3]), right(above[3])))
        else:
            return add(base, sub(right(below[3]), left(below[3])))
        return add(base, add(left(u), right(v)))

    def weights_of(r):
        return [[a[f, r, 0], a[f, r, 1]] for f in range(4)]

    def state(t, s, r):
        return [x[t, s, r, 0], x[t, s, r, 1]]

    def store(t, s, r, value):
        x[t, s, r, 0] = value[0]
        x[t, s, r, 1] = value[1]

    def advance(t, s, first, last):
        def term(r):
            return times(weights_of(r), state(t - 1, s, r))

        above, here = term(first - 1), term(first)
        for r in range(first, last):
            below = term(r + 1)
            store(t, s, r, combine(here, above, below))
            above, here = here, below

    for end in range(2):
        rows_in = (0, 1) if end == 0 else (rows - 1, rows - 2)
        for n, (f, d) in enumerate(((1, 0), (2, 0), (3, 0), (1, 1), (3, 1))):
            for h in range(2):
                k_tx[end, n, h] = a[f, rows_in[d], h]

    pairs = [(end, s) for s in range(SAMPLES) for end in range(2)]

    def row_of(end, d):
        return d if end == 0 else rows - 1 - d

    def term(t, end, s, d):
        return times(weights_of(row_of(end, d)), state(t, s, row_of(end, d)))

    def cross(n, end, s, local):
        value = combine(None, None, local) if end == 0 else combine(None, local, None)
        for h in range(2):
            edge_tx[end, n, s, h] = value[h]

    def partial(end, local, inner, outer=None):
        return combine(local, outer, inner) if end == 0 else combine(local, inner, outer)

    for end, s in pairs:
        cross(0, end, s, term(0, end, s, 0))

    for end in range(2):

        @pl.when(jnp.logical_not(present[end]))
        def _(end=end):
            for h in range(2):
                for n in range(5):
                    k_rx[end, n, h] = zero
                for s in range(SAMPLES):
                    for n in range(w):
                        edge_rx[end, n, s, h] = zero
            for side in range(2):
                diag_rx[end, side] = zero
            for n in range(4):
                corner_rx[end, n] = zero

    n_sum = sum(len(group) - 1 for group in groups)
    pl.semaphore_wait(barrier, 2 + n_sum + 3 * has_north.astype(jnp.int32) + 3 * has_south.astype(jnp.int32))

    def remote(src, dst, tx, rx, pa, pb):
        return pltpu.make_async_remote_copy(
            src_ref=src, dst_ref=dst, send_sem=tx, recv_sem=rx, device_id=(pa, pb), device_id_type=MESH
        )

    lon_copies = [
        remote(lon_tx.at[side], lon_rx.at[side], lon_tx_sem.at[side], lon_rx_sem.at[side], ia, (east, west)[side])
        for side in range(2)
    ]
    diag_copies = [
        [
            remote(diag_tx.at[end, side], diag_rx.at[1 - end, side], diag_tx_sem.at[end, side], diag_rx_sem.at[1 - end, side], pa_of[end], (east, west)[side])
            for side in range(2)
        ]
        for end in range(2)
    ]

    def lat_copy(end, piece):
        tx, rx = lat_tx_sem.at[end, piece], lat_rx_sem.at[1 - end, piece]
        if piece == ITERS:
            return remote(k_tx.at[end], k_rx.at[1 - end], tx, rx, pa_of[end], ib)
        if piece == ITERS + 1:
            return remote(corner_tx.at[end], corner_rx.at[1 - end], tx, rx, pa_of[end], ib)
        return remote(edge_tx.at[end, piece], edge_rx.at[1 - end, piece], tx, rx, pa_of[end], ib)

    lat_copies = [[lat_copy(end, piece) for piece in range(ITERS + 2)] for end in range(2)]

    for end in range(2):

        @pl.when(present[end])
        def _(end=end):
            for c in diag_copies[end]:
                c.start()

    for c in lon_copies:
        c.start()
    def send(piece):
        for end in range(2):

            @pl.when(present[end])
            def _(end=end):
                lat_copies[end][piece].start()

    send(ITERS + 1)
    send(0)
    send(ITERS)
    alone = {}
    for end, s in pairs:
        alone[end, s] = times(weights_of(row_of(end, 0)), partial(end, term(0, end, s, 0), term(0, end, s, 1)))
        cross(1, end, s, alone[end, s])
    send(1)
    for s in range(SAMPLES):
        advance(1, s, 1, 3)
        advance(1, s, rows - 3, rows - 1)
    for end, s in pairs:
        t10, t11 = alone[end, s], term(1, end, s, 1)
        t20 = times(weights_of(row_of(end, 0)), partial(end, t10, t11))
        t21 = times(weights_of(row_of(end, 1)), partial(end, t11, term(1, end, s, 2), t10))
        alone[end, s] = t20, t21
        cross(2, end, s, t20)
    send(2)
    for end, s in pairs:
        cross(3, end, s, times(weights_of(row_of(end, 0)), partial(end, *alone[end, s])))
    send(3)

    def interior(s, carry):
        advance(1, s, 3, rows - 3)
        for t in range(2, ITERS + 1):
            advance(t, s, t, rows - t)
        return carry

    lax.fori_loop(0, SAMPLES, interior, 0)

    for c in lon_copies:
        c.wait_recv()
    beyond_edge = jnp.logical_or(place < 4, place >= 28)
    even_four = lax.bitwise_and(fours, 1) == 0
    block_before = lax.bitwise_and(lax.shift_right_logical(lane + 4, 5), 3)

    def woven(fw, fe, shift):
        fe = rolled(fe, shift)
        return jnp.where(even_four, fw, fe), jnp.where(even_four, fe, fw)

    for v in range(2):
        both = woven(lon_rx[0, v], lon_rx[1, v], 28)
        for j in range(8):
            e = w + 8 * v + j
            hx[0, e] = jnp.where(beyond_edge, rolled(both[j % 2], -4 * j), hx[0, e])
        both = woven(lon_rx[0, 2 + v], lon_rx[1, 2 + v], -4)
        for f in range(3):
            even = replicate(jnp.where(block_before == f, both[0], 0.0))
            odd = replicate(jnp.where(sample_of == f, both[1], 0.0))
            for j in range(8):
                e = w + 8 * v + j
                ha[1 + f, e] = jnp.where(beyond_edge, rolled((even, odd)[j % 2], -4 * j), ha[1 + f, e])
    for end, first in enumerate((0, w + rows)):

        @pl.when(present[end])
        def _(end=end):
            for side in range(2):
                diag_copies[1 - end][side].wait_recv()
            lat_copies[1 - end][ITERS + 1].wait_recv()

        dw, de = diag_rx[end, 0], diag_rx[end, 1]
        both = woven(dw, de, 28)
        for i in range(w):
            own = rolled(corner_rx[end, i // 2], -8 * (i % 2))
            hx[0, first + i] = jnp.where(beyond_edge, rolled(both[i % 2], -4 * i), own)
        both = woven(dw, de, -4)
        for f in range(3):
            mine = jnp.logical_and(sample_of == f, place >= 12)
            halves = [replicate(jnp.where(mine, u, 0.0)) for u in both]
            for n in range(w // 2):
                own = replicate(jnp.where(block_of == f, corner_rx[end, 2 + n], 0.0))
                for i in (2 * n, 2 * n + 1):
                    moved = rolled(halves[i % 2], -16 - 4 * i)
                    ha[1 + f, first + i] = jnp.where(beyond_edge, moved, rolled(own, -8 * (i % 2)))

    def centre(a1, a2):
        return jnp.where(a1 > 0.0, 1.0, 0.0) - 2.0 * (a1 + a2)

    for e in range(tall):
        ha[0, e] = centre(ha[1, e], ha[2, e])
    for t in range(1, ITERS + 1):

        def term(e):
            z = hx[t - 1, e]
            return [ha[f, e] * z for f in range(4)]

        above, here = term(t - 1), term(t)
        for e in range(t, tall - t):
            below = term(e + 1)
            q3 = above[3] - below[3]
            total = here[0] + (above[1] + below[1])
            total = total + pltpu.roll(here[2] + q3, 1, 1)
            hx[t, e] = total + pltpu.roll(here[2] - q3, LANES - 1, 1)
            above, here = here, below

    low_edge, high_edge = lane < 4, lane >= LANES - 4
    for r in range(rows):
        side = hx[ITERS, w + r]
        side = jnp.where(place < 4, rolled(side, -24), side)
        for s in range(SAMPLES):
            xs[s, r] = rolled(side, -32 * s - 4)

    def finish(s, r, value):
        value = [jnp.where(low_edge, xs[s, r], value[0]), jnp.where(high_edge, xs[s, r], value[1])]
        store(ITERS, s, r, value)
        return [u * u for u in value]

    def wet_sum(total, r, squares):
        for h in range(2):
            v = squares[h] * (1.0 / SAMPLES)
            var[r, h] = v
            total = total + jnp.where(a[1, r, h] > 0.0, v, 0.0)
        return total

    total_v, total_m = zero, zero
    for r in range(rows):
        for h in range(2):
            total_m = total_m + jnp.where(a[1, r, h] > 0.0, 1.0, 0.0)
    for r in range(w, rows - w):
        total_v = wet_sum(total_v, r, add(*[finish(s, r, state(ITERS, s, r)) for s in range(SAMPLES)]))

    def arrived(piece):
        for end in range(2):

            @pl.when(present[end])
            def _(end=end):
                lat_copies[1 - end][piece].wait_recv()

    def toward(end, local, outer, inner, known=None):
        above, below = (outer, inner) if end == 0 else (inner, outer)
        return combine(local, above, below, known)

    def known(n, end, s):
        return [edge_rx[end, n, s, 0], edge_rx[end, n, s, 1]]

    def near(end):
        return [[k_mid[end, 0], k_mid[end, 1]]] + [[k_rx[end, n, 0], k_rx[end, n, 1]] for n in range(3)]

    def far(end):
        return [None, [k_rx[end, 3, 0], k_rx[end, 3, 1]], None, [k_rx[end, 4, 0], k_rx[end, 4, 1]]]

    def keep(end, s, n, value):
        echo[end, s, n, 0], echo[end, s, n, 1] = value

    def kept(end, s, n):
        return [echo[end, s, n, 0], echo[end, s, n, 1]]

    def terms(t, end, s, count):
        return [times(weights_of(row_of(end, d)), state(t, s, row_of(end, d))) for d in range(count)]

    arrived(0)
    for end, s in pairs:
        t0 = terms(0, end, s, 2)
        keep(end, s, 0, toward(end, None, None, t0[0]))
        store(1, s, row_of(end, 0), toward(end, t0[0], None, t0[1], known(0, end, s)))
    arrived(ITERS)
    for end in range(2):
        for h in range(2):
            k_mid[end, h] = centre(k_rx[end, 0, h], k_rx[end, 1, h])
    arrived(1)
    for end, s in pairs:
        t1 = terms(1, end, s, 3)
        beyond = times(near(end), kept(end, s, 0))
        keep(end, s, 1, toward(end, None, None, beyond))
        keep(end, s, 0, toward(end, beyond, None, t1[0]))
        store(2, s, row_of(end, 0), toward(end, t1[0], beyond, t1[1], known(1, end, s)))
        store(2, s, row_of(end, 1), toward(end, t1[1], t1[0], t1[2]))
    arrived(2)
    for end, s in pairs:
        t2 = terms(2, end, s, 4)
        beyond = times(near(end), kept(end, s, 0))
        keep(end, s, 0, toward(end, beyond, times(far(end), kept(end, s, 1)), t2[0]))
        store(3, s, row_of(end, 0), toward(end, t2[0], beyond, t2[1], known(2, end, s)))
        for d in (1, 2):
            store(3, s, row_of(end, d), toward(end, t2[d], t2[d - 1], t2[d + 1]))
    squares = {}
    for end, s in pairs:
        t3 = terms(3, end, s, 5)
        beyond = times(near(end), kept(end, s, 0))
        store(ITERS, s, row_of(end, 0), toward(end, t3[0], beyond, t3[1]))
        for d in range(1, ITERS):
            r = row_of(end, d)
            squares.setdefault(r, []).append(finish(s, r, toward(end, t3[d], t3[d - 1], t3[d + 1])))
    for r in sorted(squares):
        total_v = wet_sum(total_v, r, add(*squares[r]))
    arrived(3)
    for end in range(2):
        r = row_of(end, 0)
        ends = [finish(s, r, add(state(ITERS, s, r), known(3, end, s))) for s in range(SAMPLES)]
        total_v = wet_sum(total_v, r, add(*ends))

    row = lax.broadcasted_iota(jnp.int32, (LEVELS, LANES), 0)
    mine = jnp.where(row == 0, jnp.sum(total_v, axis=0, keepdims=True), jnp.sum(total_m, axis=0, keepdims=True))

    def rank(masks):
        out = 0
        for bit, (ma, mb) in enumerate(masks):
            hit = lax.bitwise_and(ia, ma) + lax.bitwise_and(ib, mb)
            out = out + jnp.where(hit > 0, 1 << bit, 0)
        return out

    def sums(phase, mine):
        group = groups[phase]
        size = len(group)
        me = rank([group[1 << i] for i in range(size.bit_length() - 1)])
        part[phase, me] = mine
        copies = []
        for _, (ma, mb) in far_first(group):
            pa, pb = lax.bitwise_xor(ia, ma), lax.bitwise_xor(ib, mb)
            slot = part.at[phase, me, pl.ds(0, 2)]
            copies.append(remote(slot, slot, sum_tx_sem.at[phase], sum_rx_sem.at[phase], pa, pb))
            copies[-1].start()

    def all_but_mine(phase):
        slots = part.at[phase, pl.ds(0, len(groups[phase]) - 1), pl.ds(0, 2)]
        return remote(slots, slots, sum_tx_sem.at[phase], sum_rx_sem.at[phase], ia, ib)

    def gather(phase):
        all_but_mine(phase).wait_recv()
        total = part[phase, 0, 0:2]
        for j in range(1, len(groups[phase])):
            total = total + part[phase, j, 0:2]
        return total

    sums(0, mine)
    for r in range(rows):
        for h in range(2):
            wet = jnp.where(a[1, r, h] > 0.0, 1.0, 0.0)
            var[r, h] = wet * lax.rsqrt(jnp.where(wet > 0.0, var[r, h], 1.0) + 1e-06)

    def scaled(s, carry):
        for r in range(rows):
            for h in range(2):
                out[s, h, pl.ds(r, LEVELS, stride=rows), :] = x[ITERS, s, r, h] * var[r, h]
        return carry

    lax.fori_loop(0, SAMPLES, scaled, 0)
    for c in lon_copies:
        c.wait_send()
    for end in range(2):

        @pl.when(present[end])
        def _(end=end):
            for c in diag_copies[end] + lat_copies[end]:
                c.wait_send()

    total = gather(0)
    sums(1, jnp.concatenate([total] * (LEVELS // 2), axis=0))
    for phase in range(2):
        all_but_mine(phase).wait_send()
    total = gather(1)
    both = jnp.sum(total, axis=1, keepdims=True)
    stat[...] = jnp.broadcast_to(both[0:1] / both[1:2], stat.shape)


def scale(field, stat, out, mean, buf, sem):
    copies = [pltpu.make_async_copy(stat, mean, sem.at[SAMPLES, 0])]
    copies[0].start()
    factor = jnp.sqrt(stat[...])
    for s in range(SAMPLES):
        for h in range(2):
            buf[s, h] = field[s, h] * factor
            copies.append(pltpu.make_async_copy(buf.at[s, h], out.at[s, :, pl.ds(h * LANES, LANES)], sem.at[s, h]))
            copies[-1].start()
    for c in copies:
        c.wait()


def hops(ma, mb):
    def apart(p, q, n):
        return min((p - q) % n, (q - p) % n)

    most = 0
    for i in range(16):
        for j in range(16):
            k, n = i ^ ma, j ^ mb
            x, other_x = j % 2 * 2 + i // 2 % 2, n % 2 * 2 + k // 2 % 2
            most = max(most, apart(i // 4, k // 4, 4) + apart(j // 2, n // 2, 8) + apart(x, other_x, 4))
    return most


def far_first(group):
    return sorted(((hops(*masks), masks) for masks in group[1:]), reverse=True)


def bits_of(n):
    return [1 << i for i in range(n.bit_length() - 1)]


def span(masks):
    out = [(0, 0)]
    for ma, mb in masks:
        out += [(x + ma, z + mb) for x, z in out]
    return out


def shards(n_lat, n_lon, noise, diff_lat, diff_lon, shear, sea_mask):
    samples, levels, rows, cols = noise.shape
    lat_bits, lon_bits = bits_of(n_lat), bits_of(n_lon)
    groups = (
        span([(b, 0) for b in lat_bits[:1]] + [(0, b) for b in lon_bits[1:]]),
        span([(b, 0) for b in lat_bits[1:]] + [(0, b) for b in lon_bits[:1]]),
    )
    size = max(len(g) for g in groups)
    tall = rows + 2 * ITERS
    flat = levels * rows
    f32 = jnp.float32
    dma = pltpu.SemaphoreType.DMA
    hbm = pl.BlockSpec(memory_space=pltpu.HBM)
    vmem = pl.BlockSpec(memory_space=pltpu.VMEM)
    field, stat = pl.pallas_call(
        functools.partial(kernel, n_lat, n_lon, rows, groups),
        out_shape=(
            pltpu.VMEM((samples, 2, flat, LANES), f32),
            pltpu.VMEM((1, LANES), f32),
        ),
        in_specs=[hbm] * 5,
        out_specs=(vmem, vmem),
        scratch_shapes=[
            pltpu.VMEM((samples, 2, flat, LANES), f32),
            pltpu.VMEM((3, 2, flat, LANES), f32),
            pltpu.VMEM((2, flat, LANES), jnp.int32),
            pltpu.VMEM((ITERS + 1, samples, rows, 2, levels, LANES), f32),
            pltpu.VMEM((4, rows, 2, levels, LANES), f32),
            pltpu.VMEM((2, ITERS, samples, 2, levels, LANES), f32),
            pltpu.VMEM((2, ITERS, samples, 2, levels, LANES), f32),
            pltpu.VMEM((2, 5, 2, levels, LANES), f32),
            pltpu.VMEM((2, 5, 2, levels, LANES), f32),
            pltpu.VMEM((2, 2, levels, LANES), f32),
            pltpu.VMEM((2, samples, 2, 2, levels, LANES), f32),
            pltpu.VMEM((2, 4, levels, LANES), f32),
            pltpu.VMEM((2, 4, levels, LANES), f32),
            pltpu.VMEM((ITERS + 1, tall, levels, LANES), f32),
            pltpu.VMEM((4, tall, levels, LANES), f32),
            pltpu.VMEM((2, 4, levels, LANES), f32),
            pltpu.VMEM((2, 4, levels, LANES), f32),
            pltpu.VMEM((2, 2, levels, LANES), f32),
            pltpu.VMEM((2, 2, levels, LANES), f32),
            pltpu.VMEM((samples, rows, levels, LANES), f32),
            pltpu.VMEM((rows, 2, levels, LANES), f32),
            pltpu.VMEM((2, size, levels, LANES), f32),
            dma((8, 2)),
            dma((2, ITERS + 2)),
            dma((2, ITERS + 2)),
            dma((2,)),
            dma((2,)),
            dma((2, 2)),
            dma((2, 2)),
            dma((2,)),
            dma((2,)),
        ],
        compiler_params=pltpu.CompilerParams(
            collective_id=0, has_side_effects=True, vmem_limit_bytes=60 << 20
        ),
    )(
        noise.reshape(samples, flat, cols),
        diff_lat.reshape(flat, cols),
        diff_lon.reshape(flat, cols),
        shear.reshape(flat, cols),
        sea_mask.reshape(flat, cols),
    )
    out, mean_var = pl.pallas_call(
        scale,
        out_shape=(jax.ShapeDtypeStruct((samples, flat, cols), f32), jax.ShapeDtypeStruct((1, LANES), f32)),
        in_specs=[vmem, vmem],
        out_specs=(hbm, hbm),
        scratch_shapes=[pltpu.VMEM((samples, 2, flat, LANES), f32), dma((samples + 1, 2))],
        compiler_params=pltpu.CompilerParams(vmem_limit_bytes=8 << 20),
    )(pltpu.with_memory_space_constraint(field, pltpu.VMEM), pltpu.with_memory_space_constraint(stat, pltpu.VMEM))
    return out.reshape(noise.shape), mean_var[0, 0]


def solution(mesh):
    return jax.shard_map(
        functools.partial(shards, mesh.shape["lat"], mesh.shape["lon"]),
        mesh=mesh,
        in_specs=(
            P(None, None, "lat", "lon"),
            P(None, "lat", "lon"),
            P(None, "lat", "lon"),
            P(None, "lat", "lon"),
            P(None, "lat", "lon"),
        ),
        out_specs=(P(None, None, "lat", "lon"), P()),
        check_vma=False,
    )
```

```python
import functools

import jax
import jax.numpy as jnp
from jax import lax
from jax.experimental import pallas as pl
from jax.experimental.pallas import tpu as pltpu
from jax.sharding import PartitionSpec as P

SAMPLES = 4
LEVELS = 8
ITERS = 4
LANES = 128
MESH = pl.DeviceIdType.MESH


def kernel(
    n_lat, n_lon, rows, groups,
    noise, k_lat, k_lon, shear, sea,
    out, stat,
    raw, raw_k, raw_m, x, a, edge_tx, edge_rx, k_tx, k_rx, k_mid, echo, corner_tx, corner_rx, hx, ha, lon_tx, lon_rx, diag_tx, diag_rx, xs, var, part,
    in_sem, lat_tx_sem, lat_rx_sem, lon_tx_sem, lon_rx_sem, diag_tx_sem, diag_rx_sem, sum_tx_sem, sum_rx_sem,
):
    w = ITERS
    tall = rows + 2 * w
    ia, ib = lax.axis_index("lat"), lax.axis_index("lon")
    east, west = lax.rem(ib + 1, n_lon), lax.rem(ib + n_lon - 1, n_lon)
    has_north, has_south = ia > 0, ia < n_lat - 1
    present = (has_north, has_south)
    pa_of = (ia - 1, ia + 1)
    lane = lax.broadcasted_iota(jnp.int32, (LEVELS, LANES), 1)
    zero = jnp.zeros((LEVELS, LANES), jnp.float32)

    def half(h):
        return pl.ds(h * LANES, LANES)

    loads = []
    for f, src in enumerate((k_lat, k_lon, shear)):
        for h in range(2):
            loads.append(pltpu.make_async_copy(src.at[:, half(h)], raw_k.at[f, h], in_sem.at[f, h]))
    for h in range(2):
        loads.append(pltpu.make_async_copy(sea.at[:, half(h)], raw_m.at[h], in_sem.at[3, h]))
    for s in range(SAMPLES):
        for h in range(2):
            loads.append(pltpu.make_async_copy(noise.at[s, :, half(h)], raw.at[s, h], in_sem.at[4 + s, h]))

    barrier = pltpu.get_barrier_semaphore()

    def greet(pa, pb):
        pl.semaphore_signal(barrier, inc=1, device_id=(pa, pb), device_id_type=MESH)

    for end in range(2):

        @pl.when(present[end])
        def _(end=end):
            for pb in (west, east, ib):
                greet(pa_of[end], pb)

    greet(ia, west)
    greet(ia, east)
    for c in loads:
        c.start()
    for group in groups:
        for _, (ma, mb) in far_first(group):
            greet(lax.bitwise_xor(ia, ma), lax.bitwise_xor(ib, mb))

    for c in loads[:8]:
        c.wait()
    for r in range(rows):
        for h in range(2):
            at = pl.ds(r, LEVELS, stride=rows)
            m = raw_m[h, at, :].astype(jnp.float32)
            k11 = raw_k[0, h, at, :]
            k22 = raw_k[1, h, at, :]
            a1 = m * k11
            a2 = m * k22
            a[1, r, h] = a1
            a[2, r, h] = a2
            a[3, r, h] = (0.5 * m) * (raw_k[2, h, at, :] * jnp.sqrt(k11 * k22))
            a[0, r, h] = m - 2.0 * (a1 + a2)

    place = lax.bitwise_and(lane, 31)
    sample_of = lax.shift_right_logical(lane, 5)
    low_own = jnp.logical_and(place >= 4, place < 16)
    high_own = jnp.logical_and(place >= 16, place < 28)

    def rolled(value, shift):
        shift %= LANES
        return pltpu.roll(value, shift, 1) if shift else value

    def replicate(value):
        value = value + pltpu.roll(value, 32, 1)
        return value + pltpu.roll(value, 64, 1)

    for f in range(1, 4):
        for r in range(rows):
            low = jnp.where(jnp.logical_and(low_own, lane < 32), rolled(a[f, r, 0], 4), 0.0)
            high = jnp.where(jnp.logical_and(high_own, lane < 32), rolled(a[f, r, 1], 28), low)
            ha[f, w + r] = replicate(high)

    for c in loads[8:]:
        c.wait()
    for s in range(SAMPLES):
        for r in range(rows):
            for h in range(2):
                x[0, s, r, h] = raw[s, h, pl.ds(r, LEVELS, stride=rows), :]
    for r in range(rows):
        side = zero
        for s in range(SAMPLES):
            mine = sample_of == s
            side = jnp.where(jnp.logical_and(low_own, mine), rolled(x[0, s, r, 0], 32 * s + 4), side)
            side = jnp.where(jnp.logical_and(high_own, mine), rolled(x[0, s, r, 1], 32 * s + 28), side)
        hx[0, w + r] = side

    offset = (24, 4)
    fours = lax.shift_right_logical(lane, 2)
    in_sample = lax.bitwise_and(fours, 7)
    for side in range(2):
        for v in range(2):
            packed, packed_k = zero, zero
            for j in range(8):
                e = w + 8 * v + j
                packed = jnp.where(in_sample == j, rolled(hx[0, e], 4 * j - offset[side]), packed)
                for f in range(3):
                    packed_k = jnp.where(fours == 8 * f + j, rolled(ha[1 + f, e], 4 * j - offset[side]), packed_k)
            lon_tx[side, v] = packed
            lon_tx[side, 2 + v] = packed_k
        for end, first in enumerate((w, rows)):
            packed = zero
            for i in range(w):
                e = first + i
                packed = jnp.where(in_sample == i, rolled(hx[0, e], 4 * i - offset[side]), packed)
                for f in range(3):
                    packed = jnp.where(fours == 8 * f + 4 + i, rolled(ha[1 + f, e], 16 + 4 * i - offset[side]), packed)
            diag_tx[end, side] = packed

    first_of_two = lax.bitwise_and(lane + 4, 8) != 0
    block_of = lax.bitwise_and(lax.shift_right_logical(lane + LANES - 4, 5), 3)
    for end, first in enumerate((w, rows)):
        for n in range(w // 2):
            e = first + 2 * n
            corner_tx[end, n] = jnp.where(first_of_two, hx[0, e], rolled(hx[0, e + 1], 8))
            packed = zero
            for f in range(3):
                two = jnp.where(first_of_two, ha[1 + f, e], rolled(ha[1 + f, e + 1], 8))
                packed = jnp.where(block_of == f, two, packed)
            corner_tx[end, 2 + n] = packed

    first_lane, last_lane = lane == 0, lane == LANES - 1

    def left(u):
        r0, r1 = pltpu.roll(u[0], 1, 1), pltpu.roll(u[1], 1, 1)
        return [r0, jnp.where(first_lane, r0, r1)]

    def right(u):
        r0, r1 = pltpu.roll(u[0], LANES - 1, 1), pltpu.roll(u[1], LANES - 1, 1)
        return [jnp.where(last_lane, r1, r0), r1]

    def add(*lists):
        lists = [u for u in lists if u is not None]
        total = lists[0]
        for u in lists[1:]:
            total = [p + q for p, q in zip(total, u)]
        return total

    def sub(u, v):
        return [p - q for p, q in zip(u, v)]

    def times(weights, z):
        return [[p * q for p, q in zip(k, z)] if k is not None else None for k in weights]

    def combine(local, above, below, known=None):
        base = add(*[u for u in (known, local and local[0], above and above[1], below and below[1]) if u is not None])
        q3 = sub(above[3], below[3]) if above and below else None
        if local and q3:
            u, v = add(local[2], q3), sub(local[2], q3)
        elif local and above:
            u, v = add(local[2], above[3]), sub(local[2], above[3])
        elif local:
            u, v = sub(local[2], below[3]), add(local[2], below[3])
        elif above:
            return add(base, sub(left(above[3]), right(above[3])))
        else:
            return add(base, sub(right(below[3]), left(below[3])))
        return add(base, add(left(u), right(v)))

    def weights_of(r):
        return [[a[f, r, 0], a[f, r, 1]] for f in range(4)]

    def state(t, s, r):
        return [x[t, s, r, 0], x[t, s, r, 1]]

    def store(t, s, r, value):
        x[t, s, r, 0] = value[0]
        x[t, s, r, 1] = value[1]

    def advance(t, s, first, last):
        def term(r):
            return times(weights_of(r), state(t - 1, s, r))

        above, here = term(first - 1), term(first)
        for r in range(first, last):
            below = term(r + 1)
            store(t, s, r, combine(here, above, below))
            above, here = here, below

    for end in range(2):
        rows_in = (0, 1) if end == 0 else (rows - 1, rows - 2)
        for n, (f, d) in enumerate(((1, 0), (2, 0), (3, 0), (1, 1), (3, 1))):
            for h in range(2):
                k_tx[end, n, h] = a[f, rows_in[d], h]

    pairs = [(end, s) for s in range(SAMPLES) for end in range(2)]

    def row_of(end, d):
        return d if end == 0 else rows - 1 - d

    def term(t, end, s, d):
        return times(weights_of(row_of(end, d)), state(t, s, row_of(end, d)))

    def cross(n, end, s, local):
        value = combine(None, None, local) if end == 0 else combine(None, local, None)
        for h in range(2):
            edge_tx[end, n, s, h] = value[h]

    def partial(end, local, inner, outer=None):
        return combine(local, outer, inner) if end == 0 else combine(local, inner, outer)

    for end, s in pairs:
        cross(0, end, s, term(0, end, s, 0))

    for end in range(2):

        @pl.when(jnp.logical_not(present[end]))
        def _(end=end):
            for h in range(2):
                for n in range(5):
                    k_rx[end, n, h] = zero
                for s in range(SAMPLES):
                    for n in range(w):
                        edge_rx[end, n, s, h] = zero
            for side in range(2):
                diag_rx[end, side] = zero
            for n in range(4):
                corner_rx[end, n] = zero

    n_sum = sum(len(group) - 1 for group in groups)
    pl.semaphore_wait(barrier, 2 + n_sum + 3 * has_north.astype(jnp.int32) + 3 * has_south.astype(jnp.int32))

    def remote(src, dst, tx, rx, pa, pb):
        return pltpu.make_async_remote_copy(
            src_ref=src, dst_ref=dst, send_sem=tx, recv_sem=rx, device_id=(pa, pb), device_id_type=MESH
        )

    lon_copies = [
        remote(lon_tx.at[side], lon_rx.at[side], lon_tx_sem.at[side], lon_rx_sem.at[side], ia, (east, west)[side])
        for side in range(2)
    ]
    diag_copies = [
        [
            remote(diag_tx.at[end, side], diag_rx.at[1 - end, side], diag_tx_sem.at[end, side], diag_rx_sem.at[1 - end, side], pa_of[end], (east, west)[side])
            for side in range(2)
        ]
        for end in range(2)
    ]

    def lat_copy(end, piece):
        tx, rx = lat_tx_sem.at[end, piece], lat_rx_sem.at[1 - end, piece]
        if piece == ITERS:
            return remote(k_tx.at[end], k_rx.at[1 - end], tx, rx, pa_of[end], ib)
        if piece == ITERS + 1:
            return remote(corner_tx.at[end], corner_rx.at[1 - end], tx, rx, pa_of[end], ib)
        return remote(edge_tx.at[end, piece], edge_rx.at[1 - end, piece], tx, rx, pa_of[end], ib)

    lat_copies = [[lat_copy(end, piece) for piece in range(ITERS + 2)] for end in range(2)]

    for end in range(2):

        @pl.when(present[end])
        def _(end=end):
            for c in diag_copies[end]:
                c.start()

    for c in lon_copies:
        c.start()
    def send(piece):
        odd = lax.rem(ia, 2) == 1
        for end, now in ((1, odd), (0, has_north), (1, jnp.logical_not(odd))):

            @pl.when(jnp.logical_and(present[end], now))
            def _(end=end):
                lat_copies[end][piece].start()

    send(ITERS + 1)
    send(0)
    send(ITERS)
    alone = {}
    for end, s in pairs:
        alone[end, s] = times(weights_of(row_of(end, 0)), partial(end, term(0, end, s, 0), term(0, end, s, 1)))
        cross(1, end, s, alone[end, s])
    send(1)
    for s in range(SAMPLES):
        advance(1, s, 1, 3)
        advance(1, s, rows - 3, rows - 1)
    for end, s in pairs:
        t10, t11 = alone[end, s], term(1, end, s, 1)
        t20 = times(weights_of(row_of(end, 0)), partial(end, t10, t11))
        t21 = times(weights_of(row_of(end, 1)), partial(end, t11, term(1, end, s, 2), t10))
        alone[end, s] = t20, t21
        cross(2, end, s, t20)
    send(2)
    for end, s in pairs:
        cross(3, end, s, times(weights_of(row_of(end, 0)), partial(end, *alone[end, s])))
    send(3)

    def interior(s, carry):
        advance(1, s, 3, rows - 3)
        for t in range(2, ITERS + 1):
            advance(t, s, t, rows - t)
        return carry

    lax.fori_loop(0, SAMPLES, interior, 0)

    for c in lon_copies:
        c.wait_recv()
    beyond_edge = jnp.logical_or(place < 4, place >= 28)
    even_four = lax.bitwise_and(fours, 1) == 0
    block_before = lax.bitwise_and(lax.shift_right_logical(lane + 4, 5), 3)

    def woven(fw, fe, shift):
        fe = rolled(fe, shift)
        return jnp.where(even_four, fw, fe), jnp.where(even_four, fe, fw)

    for v in range(2):
        both = woven(lon_rx[0, v], lon_rx[1, v], 28)
        for j in range(8):
            e = w + 8 * v + j
            hx[0, e] = jnp.where(beyond_edge, rolled(both[j % 2], -4 * j), hx[0, e])
        both = woven(lon_rx[0, 2 + v], lon_rx[1, 2 + v], -4)
        for f in range(3):
            even = replicate(jnp.where(block_before == f, both[0], 0.0))
            odd = replicate(jnp.where(sample_of == f, both[1], 0.0))
            for j in range(8):
                e = w + 8 * v + j
                ha[1 + f, e] = jnp.where(beyond_edge, rolled((even, odd)[j % 2], -4 * j), ha[1 + f, e])
    for end, first in enumerate((0, w + rows)):

        @pl.when(present[end])
        def _(end=end):
            for side in range(2):
                diag_copies[1 - end][side].wait_recv()
            lat_copies[1 - end][ITERS + 1].wait_recv()

        dw, de = diag_rx[end, 0], diag_rx[end, 1]
        both = woven(dw, de, 28)
        for i in range(w):
            own = rolled(corner_rx[end, i // 2], -8 * (i % 2))
            hx[0, first + i] = jnp.where(beyond_edge, rolled(both[i % 2], -4 * i), own)
        both = woven(dw, de, -4)
        for f in range(3):
            mine = jnp.logical_and(sample_of == f, place >= 12)
            halves = [replicate(jnp.where(mine, u, 0.0)) for u in both]
            for n in range(w // 2):
                own = replicate(jnp.where(block_of == f, corner_rx[end, 2 + n], 0.0))
                for i in (2 * n, 2 * n + 1):
                    moved = rolled(halves[i % 2], -16 - 4 * i)
                    ha[1 + f, first + i] = jnp.where(beyond_edge, moved, rolled(own, -8 * (i % 2)))

    def centre(a1, a2):
        return jnp.where(a1 > 0.0, 1.0, 0.0) - 2.0 * (a1 + a2)

    for e in range(tall):
        ha[0, e] = centre(ha[1, e], ha[2, e])
    for t in range(1, ITERS + 1):

        def term(e):
            z = hx[t - 1, e]
            return [ha[f, e] * z for f in range(4)]

        above, here = term(t - 1), term(t)
        for e in range(t, tall - t):
            below = term(e + 1)
            q3 = above[3] - below[3]
            total = here[0] + (above[1] + below[1])
            total = total + pltpu.roll(here[2] + q3, 1, 1)
            hx[t, e] = total + pltpu.roll(here[2] - q3, LANES - 1, 1)
            above, here = here, below

    low_edge, high_edge = lane < 4, lane >= LANES - 4
    for r in range(rows):
        side = hx[ITERS, w + r]
        side = jnp.where(place < 4, rolled(side, -24), side)
        for s in range(SAMPLES):
            xs[s, r] = rolled(side, -32 * s - 4)

    def finish(s, r, value):
        value = [jnp.where(low_edge, xs[s, r], value[0]), jnp.where(high_edge, xs[s, r], value[1])]
        store(ITERS, s, r, value)
        return [u * u for u in value]

    def wet_sum(total, r, squares):
        for h in range(2):
            v = squares[h] * (1.0 / SAMPLES)
            var[r, h] = v
            total = total + jnp.where(a[1, r, h] > 0.0, v, 0.0)
        return total

    total_v, total_m = zero, zero
    for r in range(rows):
        for h in range(2):
            total_m = total_m + jnp.where(a[1, r, h] > 0.0, 1.0, 0.0)
    for r in range(w, rows - w):
        total_v = wet_sum(total_v, r, add(*[finish(s, r, state(ITERS, s, r)) for s in range(SAMPLES)]))

    def arrived(piece):
        for end in range(2):

            @pl.when(present[end])
            def _(end=end):
                lat_copies[1 - end][piece].wait_recv()

    def toward(end, local, outer, inner, known=None):
        above, below = (outer, inner) if end == 0 else (inner, outer)
        return combine(local, above, below, known)

    def known(n, end, s):
        return [edge_rx[end, n, s, 0], edge_rx[end, n, s, 1]]

    def near(end):
        return [[k_mid[end, 0], k_mid[end, 1]]] + [[k_rx[end, n, 0], k_rx[end, n, 1]] for n in range(3)]

    def far(end):
        return [None, [k_rx[end, 3, 0], k_rx[end, 3, 1]], None, [k_rx[end, 4, 0], k_rx[end, 4, 1]]]

    def keep(end, s, n, value):
        echo[end, s, n, 0], echo[end, s, n, 1] = value

    def kept(end, s, n):
        return [echo[end, s, n, 0], echo[end, s, n, 1]]

    def terms(t, end, s, count):
        return [times(weights_of(row_of(end, d)), state(t, s, row_of(end, d))) for d in range(count)]

    arrived(0)
    for end, s in pairs:
        t0 = terms(0, end, s, 2)
        keep(end, s, 0, toward(end, None, None, t0[0]))
        store(1, s, row_of(end, 0), toward(end, t0[0], None, t0[1], known(0, end, s)))
    arrived(ITERS)
    for end in range(2):
        for h in range(2):
            k_mid[end, h] = centre(k_rx[end, 0, h], k_rx[end, 1, h])
    arrived(1)
    for end, s in pairs:
        t1 = terms(1, end, s, 3)
        beyond = times(near(end), kept(end, s, 0))
        keep(end, s, 1, toward(end, None, None, beyond))
        keep(end, s, 0, toward(end, beyond, None, t1[0]))
        store(2, s, row_of(end, 0), toward(end, t1[0], beyond, t1[1], known(1, end, s)))
        store(2, s, row_of(end, 1), toward(end, t1[1], t1[0], t1[2]))
    arrived(2)
    for end, s in pairs:
        t2 = terms(2, end, s, 4)
        beyond = times(near(end), kept(end, s, 0))
        keep(end, s, 0, toward(end, beyond, times(far(end), kept(end, s, 1)), t2[0]))
        store(3, s, row_of(end, 0), toward(end, t2[0], beyond, t2[1], known(2, end, s)))
        for d in (1, 2):
            store(3, s, row_of(end, d), toward(end, t2[d], t2[d - 1], t2[d + 1]))
    squares = {}
    for end, s in pairs:
        t3 = terms(3, end, s, 5)
        beyond = times(near(end), kept(end, s, 0))
        store(ITERS, s, row_of(end, 0), toward(end, t3[0], beyond, t3[1]))
        for d in range(1, ITERS):
            r = row_of(end, d)
            squares.setdefault(r, []).append(finish(s, r, toward(end, t3[d], t3[d - 1], t3[d + 1])))
    for r in sorted(squares):
        total_v = wet_sum(total_v, r, add(*squares[r]))
    arrived(3)
    for end in range(2):
        r = row_of(end, 0)
        ends = [finish(s, r, add(state(ITERS, s, r), known(3, end, s))) for s in range(SAMPLES)]
        total_v = wet_sum(total_v, r, add(*ends))

    row = lax.broadcasted_iota(jnp.int32, (LEVELS, LANES), 0)
    mine = jnp.where(row == 0, jnp.sum(total_v, axis=0, keepdims=True), jnp.sum(total_m, axis=0, keepdims=True))

    def rank(masks):
        out = 0
        for bit, (ma, mb) in enumerate(masks):
            hit = lax.bitwise_and(ia, ma) + lax.bitwise_and(ib, mb)
            out = out + jnp.where(hit > 0, 1 << bit, 0)
        return out

    def sums(phase, mine):
        group = groups[phase]
        size = len(group)
        me = rank([group[1 << i] for i in range(size.bit_length() - 1)])
        part[phase, me] = mine
        copies = []
        for _, (ma, mb) in far_first(group):
            pa, pb = lax.bitwise_xor(ia, ma), lax.bitwise_xor(ib, mb)
            slot = part.at[phase, me, pl.ds(0, 2)]
            copies.append(remote(slot, slot, sum_tx_sem.at[phase], sum_rx_sem.at[phase], pa, pb))
            copies[-1].start()

    def all_but_mine(phase):
        slots = part.at[phase, pl.ds(0, len(groups[phase]) - 1), pl.ds(0, 2)]
        return remote(slots, slots, sum_tx_sem.at[phase], sum_rx_sem.at[phase], ia, ib)

    def gather(phase):
        all_but_mine(phase).wait_recv()
        total = part[phase, 0, 0:2]
        for j in range(1, len(groups[phase])):
            total = total + part[phase, j, 0:2]
        return total

    sums(0, mine)
    for r in range(rows):
        for h in range(2):
            wet = jnp.where(a[1, r, h] > 0.0, 1.0, 0.0)
            var[r, h] = wet * lax.rsqrt(jnp.where(wet > 0.0, var[r, h], 1.0) + 1e-06)

    def scaled(s, carry):
        for r in range(rows):
            for h in range(2):
                out[s, h, pl.ds(r, LEVELS, stride=rows), :] = x[ITERS, s, r, h] * var[r, h]
        return carry

    lax.fori_loop(0, SAMPLES, scaled, 0)
    for c in lon_copies:
        c.wait_send()
    for end in range(2):

        @pl.when(present[end])
        def _(end=end):
            for c in diag_copies[end] + lat_copies[end]:
                c.wait_send()

    total = gather(0)
    sums(1, jnp.concatenate([total] * (LEVELS // 2), axis=0))
    for phase in range(2):
        all_but_mine(phase).wait_send()
    total = gather(1)
    both = jnp.sum(total, axis=1, keepdims=True)
    stat[...] = jnp.broadcast_to(both[0:1] / both[1:2], stat.shape)


def scale(field, stat, out, mean, buf, sem):
    copies = [pltpu.make_async_copy(stat, mean, sem.at[SAMPLES, 0])]
    copies[0].start()
    factor = jnp.sqrt(stat[...])
    for s in range(SAMPLES):
        for h in range(2):
            buf[s, h] = field[s, h] * factor
            copies.append(pltpu.make_async_copy(buf.at[s, h], out.at[s, :, pl.ds(h * LANES, LANES)], sem.at[s, h]))
            copies[-1].start()
    for c in copies:
        c.wait()


def hops(ma, mb):
    def apart(p, q, n):
        return min((p - q) % n, (q - p) % n)

    most = 0
    for i in range(16):
        for j in range(16):
            k, n = i ^ ma, j ^ mb
            x, other_x = j % 2 * 2 + i // 2 % 2, n % 2 * 2 + k // 2 % 2
            most = max(most, apart(i // 4, k // 4, 4) + apart(j // 2, n // 2, 8) + apart(x, other_x, 4))
    return most


def far_first(group):
    return sorted(((hops(*masks), masks) for masks in group[1:]), reverse=True)


def bits_of(n):
    return [1 << i for i in range(n.bit_length() - 1)]


def span(masks):
    out = [(0, 0)]
    for ma, mb in masks:
        out += [(x + ma, z + mb) for x, z in out]
    return out


def shards(n_lat, n_lon, noise, diff_lat, diff_lon, shear, sea_mask):
    samples, levels, rows, cols = noise.shape
    lat_bits, lon_bits = bits_of(n_lat), bits_of(n_lon)
    groups = (
        span([(b, 0) for b in lat_bits[:1]] + [(0, b) for b in lon_bits[1:]]),
        span([(b, 0) for b in lat_bits[1:]] + [(0, b) for b in lon_bits[:1]]),
    )
    size = max(len(g) for g in groups)
    tall = rows + 2 * ITERS
    flat = levels * rows
    f32 = jnp.float32
    dma = pltpu.SemaphoreType.DMA
    hbm = pl.BlockSpec(memory_space=pltpu.HBM)
    vmem = pl.BlockSpec(memory_space=pltpu.VMEM)
    field, stat = pl.pallas_call(
        functools.partial(kernel, n_lat, n_lon, rows, groups),
        out_shape=(
            pltpu.VMEM((samples, 2, flat, LANES), f32),
            pltpu.VMEM((1, LANES), f32),
        ),
        in_specs=[hbm] * 5,
        out_specs=(vmem, vmem),
        scratch_shapes=[
            pltpu.VMEM((samples, 2, flat, LANES), f32),
            pltpu.VMEM((3, 2, flat, LANES), f32),
            pltpu.VMEM((2, flat, LANES), jnp.int32),
            pltpu.VMEM((ITERS + 1, samples, rows, 2, levels, LANES), f32),
            pltpu.VMEM((4, rows, 2, levels, LANES), f32),
            pltpu.VMEM((2, ITERS, samples, 2, levels, LANES), f32),
            pltpu.VMEM((2, ITERS, samples, 2, levels, LANES), f32),
            pltpu.VMEM((2, 5, 2, levels, LANES), f32),
            pltpu.VMEM((2, 5, 2, levels, LANES), f32),
            pltpu.VMEM((2, 2, levels, LANES), f32),
            pltpu.VMEM((2, samples, 2, 2, levels, LANES), f32),
            pltpu.VMEM((2, 4, levels, LANES), f32),
            pltpu.VMEM((2, 4, levels, LANES), f32),
            pltpu.VMEM((ITERS + 1, tall, levels, LANES), f32),
            pltpu.VMEM((4, tall, levels, LANES), f32),
            pltpu.VMEM((2, 4, levels, LANES), f32),
            pltpu.VMEM((2, 4, levels, LANES), f32),
            pltpu.VMEM((2, 2, levels, LANES), f32),
            pltpu.VMEM((2, 2, levels, LANES), f32),
            pltpu.VMEM((samples, rows, levels, LANES), f32),
            pltpu.VMEM((rows, 2, levels, LANES), f32),
            pltpu.VMEM((2, size, levels, LANES), f32),
            dma((8, 2)),
            dma((2, ITERS + 2)),
            dma((2, ITERS + 2)),
            dma((2,)),
            dma((2,)),
            dma((2, 2)),
            dma((2, 2)),
            dma((2,)),
            dma((2,)),
        ],
        compiler_params=pltpu.CompilerParams(
            collective_id=0, has_side_effects=True, vmem_limit_bytes=60 << 20
        ),
    )(
        noise.reshape(samples, flat, cols),
        diff_lat.reshape(flat, cols),
        diff_lon.reshape(flat, cols),
        shear.reshape(flat, cols),
        sea_mask.reshape(flat, cols),
    )
    out, mean_var = pl.pallas_call(
        scale,
        out_shape=(jax.ShapeDtypeStruct((samples, flat, cols), f32), jax.ShapeDtypeStruct((1, LANES), f32)),
        in_specs=[vmem, vmem],
        out_specs=(hbm, hbm),
        scratch_shapes=[pltpu.VMEM((samples, 2, flat, LANES), f32), dma((samples + 1, 2))],
        compiler_params=pltpu.CompilerParams(vmem_limit_bytes=8 << 20),
    )(pltpu.with_memory_space_constraint(field, pltpu.VMEM), pltpu.with_memory_space_constraint(stat, pltpu.VMEM))
    return out.reshape(noise.shape), mean_var[0, 0]


def solution(mesh):
    return jax.shard_map(
        functools.partial(shards, mesh.shape["lat"], mesh.shape["lon"]),
        mesh=mesh,
        in_specs=(
            P(None, None, "lat", "lon"),
            P(None, "lat", "lon"),
            P(None, "lat", "lon"),
            P(None, "lat", "lon"),
            P(None, "lat", "lon"),
        ),
        out_specs=(P(None, None, "lat", "lon"), P()),
        check_vma=False,
    )
```
